128 devices in a mesh: section: 2 (over core), seq: 4 (over z), dp: 16 (over y, x).
Axes of the slice: x: 4, y: 4, z: 4, core: 2. Of those that a mesh axis runs over, the one named last changes fastest.
Arguments:
- inputs: bfloat16 [32, 1024, 768], P('dp', 'seq'), may hold values from -6 to 6
- cotangent: bfloat16 [32, 1024, 768], P('dp', 'seq'), may hold values from -6 to 6
- w_qkv: bfloat16 [2, 768, 2304], P('section', 'dp'), may hold values from -0.21875 to 0.21875
- w_out: bfloat16 [2, 768, 768], P('section', 'dp'), may hold values from -1.25 to 1.25
- w_fc: bfloat16 [2, 768, 3072], P('section', 'dp'), may hold values from -0.21875 to 0.21875
- w_proj: bfloat16 [2, 3072, 768], P('section', 'dp'), may hold values from -0.109375 to 0.109375
- gains: bfloat16 [2, 2, 768], P('section', None, 'dp'), may hold values from 0.099609375 to 1.8984375
- biases: bfloat16 [2, 6, 768], P('section', None, 'dp'), may hold values from -3 to 3
- fc_bias: bfloat16 [2, 3072], P('section', 'dp'), may hold values from -3 to 3
Outputs:
- section_out: bfloat16 [2, 32, 1024, 768], P('section', 'dp', 'seq')
- in_grad: bfloat16 [2, 32, 1024, 768], P('section', 'dp', 'seq')
- grad_qkv: float32 [2, 768, 2304], P('section', 'dp')
- grad_out: float32 [2, 768, 768], P('section', 'dp')
- grad_fc: float32 [2, 768, 3072], P('section', 'dp')
- grad_proj: float32 [2, 3072, 768], P('section', 'dp')
- grad_gains: float32 [2, 2, 768], P('section', None, 'dp')
- grad_biases: float32 [2, 6, 768], P('section', None, 'dp')
- grad_fc_bias: float32 [2, 3072], P('section', 'dp')
The draws below stay inside these ranges and needn't reach their ends.
All inputs are finite; a program needn't handle non-finite values.
Results may differ from the reference program's by a relative error of at most 0.019.
Values may be sent and summed in bfloat16 or wider, within the bound.
A program may use at most 256 MiB of HBM per device.

```python
import jax
import jax.numpy as jnp
from jax import lax

D = 768
HEADS = 12
HEAD = 64
FF = 3072
L = 1024
SEQS = 32


def block_scale(rng, shape, pieces, least, top_value):
    def one(axis_at, parts):
        heights = jax.random.uniform(jax.random.fold_in(jax.random.fold_in(rng, 6), axis_at), (parts,), jnp.float32, least / len(pieces), top_value / len(pieces))
        return jnp.repeat(jnp.exp(heights), shape[axis_at] // parts).reshape((-1,) + (1,) * (len(shape) - axis_at - 1))

    loudness = one(*pieces[0])
    for cut in pieces[1:]:
        loudness = loudness * one(*cut)
    return loudness


def normal_values(rng, extent, width, reach, shards=(), kind=jnp.bfloat16):
    entries = jax.random.normal(rng, extent, jnp.float32) * width
    if len(shards) > 0:
        entries = block_scale(rng, extent, shards, -0.22, 0.18) * entries
    return jnp.clip(entries, min=-reach, max=reach).astype(kind)


def setup_inputs(seed: int = 0) -> dict:
    keys = jax.random.split(jax.random.key(seed), 10)
    inputs = normal_values(keys[0], (SEQS, L, D), 1.0, 6.0, ((0, 16), (1, 4)))
    cotangent = normal_values(keys[1], (SEQS, L, D), 1.0, 6.0, ((0, 16), (1, 4)))
    w_qkv = normal_values(keys[2], (2, D, 3 * D), D ** -0.5, 0.21875, ((0, 2), (1, 16)))
    w_out = normal_values(keys[3], (2, D, D), (max(D // 32, 1)) ** -0.5, 1.25, ((0, 2), (1, 16)))
    w_fc = normal_values(keys[4], (2, D, FF), D ** -0.5, 0.21875, ((0, 2), (1, 16)))
    w_proj = normal_values(keys[5], (2, FF, D), FF ** -0.5, 0.109375, ((0, 2), (1, 16)))
    gains = jnp.clip(1.0 + 0.18 * jax.random.normal(keys[6], (2, 2, D), jnp.float32), 0.099609375, 1.8984375).astype(jnp.bfloat16)
    biases = normal_values(keys[7], (2, 6, D), 0.5, 3.0, ((0, 2), (2, 16)))
    fc_bias = normal_values(keys[8], (2, FF), 0.5, 3.0, ((0, 2), (1, 16)))
    return {"inputs": inputs, "cotangent": cotangent, "w_qkv": w_qkv, "w_out": w_out, "w_fc": w_fc, "w_proj": w_proj, "gains": gains, "biases": biases, "fc_bias": fc_bias}


epsilon = 1e-05

@jax.custom_vjp
def low(v):
    return lax.optimization_barrier(v.astype(jnp.bfloat16)).astype(jnp.float32)

@jax.custom_vjp
def low_back(v):
    return v

def low_keep(v):
    return (low(v), None)

def low_pass(kept, grad):
    return (grad,)

def back_keep(v):
    return (v, None)

def back_low(kept, grad):
    return (low(grad),)
low.defvjp(low_keep, low_pass)
low_back.defvjp(back_keep, back_low)

def matmul_high(left, right):
    return jnp.dot(left, right, precision=lax.Precision.HIGHEST, preferred_element_type=jnp.float32)

def layer_norm(stream, gain, shift):
    centre = stream - lax.optimization_barrier(jnp.mean(stream, axis=-1, keepdims=True))
    spread = lax.optimization_barrier(jnp.mean(centre * centre, axis=-1, keepdims=True))
    return centre * lax.rsqrt(spread + epsilon) * gain + shift

def attention(queries, keys_in, values_in):
    rows = min(512, L)
    scale = HEAD ** (-0.5)
    starts = jnp.arange(L // rows, dtype=jnp.int32) * rows

    def one_block(start):
        block_q = lax.dynamic_slice_in_dim(queries, start, rows, 0)
        scores = jnp.einsum('qhd,khd->hqk', block_q, keys_in, precision=lax.Precision.HIGHEST) * scale
        scores = low_back(scores)
        query_pos = start + jnp.arange(rows, dtype=jnp.int32)
        key_pos = jnp.arange(L, dtype=jnp.int32)
        scores = jnp.where(key_pos[None, None, :] <= query_pos[None, :, None], scores, -1e+30)
        weights = low(jax.nn.softmax(scores, axis=-1))
        mixed = jnp.einsum('hqk,khd->qhd', weights, values_in, precision=lax.Precision.HIGHEST)
        return mixed.reshape(rows, D)
    return lax.map(jax.checkpoint(one_block), starts).reshape(L, D)

def block(stream, w_in, w_mix, w_up, w_down, gain, shift, up_shift):
    normed = low(layer_norm(stream, gain[0], shift[0]))
    qkv_shift = jnp.concatenate([shift[1], jnp.zeros_like(shift[1]), shift[2]])
    packed = low(low_back(matmul_high(normed, w_in) + qkv_shift))
    queries = packed[:, :D].reshape(L, HEADS, HEAD)
    keys_in = packed[:, D:2 * D].reshape(L, HEADS, HEAD)
    values_in = packed[:, 2 * D:].reshape(L, HEADS, HEAD)
    mixed = low(low_back(attention(queries, keys_in, values_in)))
    middle = stream + (low_back(matmul_high(mixed, w_mix)) + shift[3])
    normed2 = low(layer_norm(middle, gain[1], shift[4]))
    pre_act = low_back(matmul_high(normed2, w_up) + up_shift)
    active = low(jax.nn.gelu(pre_act, approximate=True))
    return middle + (low_back(matmul_high(active, w_down)) + shift[5])

def reference(inputs, cotangent, w_qkv, w_out, w_fc, w_proj, gains, biases, fc_bias):
    params = tuple((item.astype(jnp.float32) for item in (w_qkv, w_out, w_fc, w_proj, gains, biases, fc_bias)))

    def two_blocks(row, extra, weights):
        first = block(row, *(item[0] for item in weights))
        middle = low(low_back(first)) + extra
        return (first, block(middle, *(item[1] for item in weights)))

    def forward(stream, extra, weights):

        def one_sequence(pair):
            return two_blocks(pair[0], pair[1], weights)
        return lax.map(jax.checkpoint(one_sequence), (stream, extra))
    start = inputs.astype(jnp.float32)
    extra = jnp.zeros_like(start)
    (first, final), pull = jax.vjp(forward, start, extra, params)
    grad_in, grad_mid, grad_params = pull((jnp.zeros_like(first), cotangent.astype(jnp.float32)))
    section_out = jnp.stack([first, final]).astype(jnp.bfloat16)
    in_grad = jnp.stack([grad_in, grad_mid]).astype(jnp.bfloat16)
    return (section_out, in_grad, grad_params[0], grad_params[1], grad_params[2], grad_params[3], grad_params[4], grad_params[5], grad_params[6])
```

```python
import functools
import math

import jax
import jax.numpy as jnp
from jax import lax
from jax.experimental import pallas as pl
from jax.experimental.pallas import tpu as pltpu
from jax.sharding import PartitionSpec as P

MESH = pl.DeviceIdType.MESH
BF = jnp.bfloat16
F32 = jnp.float32
D = 768
T = 512
L = 1024
HALF = 384
ROWS = 608
HROWS = ROWS // 2
EPS = 1e-05
SCALE = 0.125
C2 = SCALE * math.log2(math.e)
VLIM = 60 * 1024 * 1024
ANY = pl.BlockSpec(memory_space=pl.ANY)
VM = pl.BlockSpec(memory_space=pltpu.VMEM)


def where_am_i():
    core = lax.axis_index("section")
    z = lax.axis_index("seq")
    dp = lax.axis_index("dp")
    return core, z, dp // 4, dp % 4


def greet(peers):
    barrier = pltpu.get_barrier_semaphore()
    for peer in peers:
        pl.semaphore_signal(barrier, inc=1, device_id=peer, device_id_type=MESH)
    pl.semaphore_wait(barrier, len(peers))


def remote(src, dst, send, recv, peer):
    return pltpu.make_async_remote_copy(
        src_ref=src, dst_ref=dst, send_sem=send, recv_sem=recv, device_id=peer, device_id_type=MESH
    )


def comm_params(ident):
    return pltpu.CompilerParams(
        collective_id=ident, has_side_effects=True, vmem_limit_bytes=VLIM
    )


def gather_kernel(shard, ins, cots, full, stream, lsem, ssem, rsem, xs, xr):
    core, z, y, x = where_am_i()
    block = z % 2
    sib = 1 - core
    dp = y * 4 + x
    sibling = (sib, z, dp)
    first = core == 0

    def along(axis, step):
        if axis == 0:
            return (core, z, y * 4 + (x + step) % 4)
        return (core, z, ((y + step) % 4) * 4 + x)

    peers = [sibling]
    for step in (1, 2, 3):
        peers += [along(0, step), along(1, step), (core, (z + step) % 4, dp)]
    greet(peers)

    mine = pl.ds(pl.multiple_of(core * HROWS, 16), HROWS)
    other = pl.ds(pl.multiple_of(sib * HROWS, 16), HROWS)

    own_local = pltpu.make_async_copy(shard.at[mine], full.at[y, x, mine], lsem.at[0])
    give = remote(
        shard.at[other], full.at[y, x, other], ssem.at[0], rsem.at[0], sibling
    )
    take = remote(
        shard.at[mine], full.at[y, x, mine], ssem.at[0], rsem.at[0], sibling
    )

    @pl.when(core == block)
    def _():
        own_local.start()
        give.start()
        own_local.wait()

    @pl.when(core != block)
    def _():
        take.wait_recv()

    def shard_at(axis, step):
        if axis == 0:
            return full.at[y, (x + step) % 4, mine]
        return full.at[(y + step) % 4, x, mine]

    def line_at(axis, step, part):
        if axis == 0:
            return full.at[pl.ds(2 * part, 2), (x + step) % 4, mine]
        return full.at[(y + step) % 4, pl.ds(2 * part, 2), mine]

    def relay(view, slot):
        return remote(view, view, ssem.at[slot], rsem.at[slot], sibling)

    def rest(axis):
        cross = 1 - axis
        hops = [
            remote(shard_at(axis, 0), shard_at(axis, 0), ssem.at[k], rsem.at[k], along(axis, k))
            for k in (1, 2, 3)
        ]
        for hop in hops:
            hop.start()
        own_relay = relay(shard_at(axis, 0), 14)
        own_relay.start()
        relays = [own_relay]

        for k in (1, 3, 2):
            land = shard_at(axis, 4 - k)
            remote(land, land, ssem.at[k], rsem.at[k], sibling).wait_recv()
        sends = []
        for part in (0, 1):
            for slot, step in ((4, 1), (6, 3)):
                view = line_at(cross, 0, part)
                hop = remote(
                    view, view, ssem.at[slot + part], rsem.at[slot + part], along(cross, step)
                )
                hop.start()
                sends.append(hop)
        for k in (1, 3, 2):
            copy = relay(shard_at(axis, 4 - k), 15 + k - 1)
            copy.start()
            relays.append(copy)
        for part, slot, came, to in ((0, 4, 3, 1), (1, 6, 1, 3), (1, 4, 3, None), (0, 6, 1, None)):
            land = line_at(cross, came, part)
            remote(land, land, ssem.at[slot + part], rsem.at[slot + part], sibling).wait_recv()
            if to is not None:
                hop = remote(land, land, ssem.at[8 + part], rsem.at[8 + part], along(cross, to))
                hop.start()
                sends.append(hop)
            copy = relay(land, 18 + slot - 4 + part)
            copy.start()
            relays.append(copy)
        for part in (0, 1):
            land = line_at(cross, 2, part)
            remote(land, land, ssem.at[8 + part], rsem.at[8 + part], sibling).wait_recv()
            copy = relay(land, 22 + part)
            copy.start()
            relays.append(copy)
        for hop in hops + sends + relays:
            hop.wait_send()

    def arrivals(axis):
        cross = 1 - axis

        def there(view_axis, step):
            if view_axis == 0:
                return full.at[y, (x + step) % 4, other]
            return full.at[(y + step) % 4, x, other]

        def lines(view_axis, step, part):
            if view_axis == 0:
                return full.at[pl.ds(2 * part, 2), (x + step) % 4, other]
            return full.at[(y + step) % 4, pl.ds(2 * part, 2), other]

        def done(view, slot):
            remote(view, view, ssem.at[slot], rsem.at[slot], sibling).wait_recv()

        done(there(axis, 0), 14)
        for k in (1, 3, 2):
            done(there(axis, 4 - k), 15 + k - 1)
        for part, slot, came in ((0, 4, 3), (1, 6, 1), (1, 4, 3), (0, 6, 1)):
            done(lines(cross, came, part), 18 + slot - 4 + part)
        for part in (0, 1):
            done(lines(cross, 2, part), 22 + part)

    quarter = pl.ds(pl.multiple_of((z % 2) * 256, 256), 256)
    sends_tokens = (z // 2) == core
    for step in (1, 2, 3):
        to = (z + step) % 4
        for source, parity in ((ins, 0), (cots, 1)):

            @pl.when(sends_tokens & (to % 2 == parity))
            def _():
                remote(
                    source.at[to // 2],
                    stream.at[quarter],
                    xs.at[step],
                    xr.at[z % 2],
                    (core, to, dp),
                ).start()

    for source, parity in ((ins, 0), (cots, 1)):

        @pl.when(sends_tokens & (z % 2 == parity))
        def _():
            copy = pltpu.make_async_copy(source.at[z // 2], stream.at[quarter], lsem.at[1])
            copy.start()
            copy.wait()

    @pl.when(first)
    def _():
        rest(0)
        arrivals(1)

    @pl.when(jnp.logical_not(first))
    def _():
        rest(1)
        arrivals(0)

    @pl.when(core == block)
    def _():
        give.wait_send()

    for step in (1, 2, 3):

        @pl.when(sends_tokens)
        def _():
            remote(ins.at[0], stream.at[quarter], xs.at[step], xr.at[0], sibling).wait_send()

    for j in (0, 1):

        @pl.when(z != 2 * core + j)
        def _():
            land = stream.at[pl.ds(256 * j, 256)]
            remote(land, land, xs.at[0], xr.at[j], sibling).wait_recv()


def gather(shard, ins, cots):
    return pl.pallas_call(
        gather_kernel,
        name="gather_weights",
        out_shape=(
            jax.ShapeDtypeStruct((4, 4, ROWS, D), BF),
            jax.ShapeDtypeStruct((T, D), BF),
        ),
        in_specs=[ANY] * 3,
        out_specs=(ANY, ANY),
        scratch_shapes=[
            pltpu.SemaphoreType.DMA((2,)),
            pltpu.SemaphoreType.DMA((24,)),
            pltpu.SemaphoreType.DMA((24,)),
            pltpu.SemaphoreType.DMA((4,)),
            pltpu.SemaphoreType.DMA((2,)),
        ],
        compiler_params=comm_params(0),
    )(shard, ins, cots)


def cross_kernel(src, dst, lsem, ssem, rsem):
    core, z, y, x = where_am_i()
    sibling = (1 - core, z, y * 4 + x)
    greet([sibling])
    local = pltpu.make_async_copy(src.at[core], dst.at[core], lsem)
    local.start()
    out = remote(src.at[1 - core], dst.at[core], ssem, rsem, sibling)
    out.start()
    local.wait()
    out.wait_send()
    remote(src.at[1 - core], dst.at[1 - core], ssem, rsem, sibling).wait_recv()


def cross(pieces, ident):
    return pl.pallas_call(
        cross_kernel,
        name="cross_cores",
        out_shape=jax.ShapeDtypeStruct(pieces.shape, pieces.dtype),
        in_specs=[ANY],
        out_specs=ANY,
        scratch_shapes=[pltpu.SemaphoreType.DMA] * 3,
        compiler_params=comm_params(ident),
    )(pieces)


def hand_kernel(giver, made, held, dst, lsem, ssem, rsem):
    core, z, y, x = where_am_i()
    partner = (core, z + 1 - 2 * (z % 2), y * 4 + x)
    greet([partner])
    out = remote(made, dst, ssem, rsem, partner)

    @pl.when(z % 2 == giver)
    def _():
        out.start()
        local = pltpu.make_async_copy(held, dst, lsem)
        local.start()
        local.wait()
        out.wait_send()

    @pl.when(z % 2 != giver)
    def _():
        out.wait_recv()


def hand_over(made, held, giver):
    return pl.pallas_call(
        functools.partial(hand_kernel, giver),
        name="hand_over",
        out_shape=jax.ShapeDtypeStruct(made.shape, made.dtype),
        in_specs=[ANY, ANY],
        out_specs=ANY,
        scratch_shapes=[pltpu.SemaphoreType.DMA] * 3,
        compiler_params=comm_params(3 + giver),
    )(made, held)


def dot(a, b):
    return jnp.dot(a, b, preferred_element_type=F32)


def dot_nt(a, b):
    return lax.dot_general(a, b, (((1,), (1,)), ((), ())), preferred_element_type=F32)


def dot_tn(a, b):
    return lax.dot_general(a, b, (((0,), (0,)), ((), ())), preferred_element_type=F32)


def normalized(v):
    centre = v - jnp.mean(v, axis=-1, keepdims=True)
    inv = lax.rsqrt(jnp.mean(centre * centre, axis=-1, keepdims=True) + EPS)
    return centre * inv, inv


def norm_back(grad, gain, unit, inv):
    g = grad * gain
    return inv * (
        g
        - jnp.mean(g, axis=-1, keepdims=True)
        - unit * jnp.mean(g * unit, axis=-1, keepdims=True)
    )


def matrix(ref, m):
    return ref[:, m * 48 : (m + 1) * 48, :].reshape(D, D)


def down_matrix(ref, m):
    return ref[4 * m : 4 * m + 4].reshape(D, D)


def weight_spec(rows, index):
    return pl.BlockSpec(
        (16, rows, D), lambda i: (0, index, 0), pipeline_mode=pl.Buffered(1)
    )


def whole(shape):
    return pl.BlockSpec(shape, lambda i: (0,) * len(shape))


TILE = 256
STEPS = T // TILE


def tile(width):
    return pl.BlockSpec((TILE, width), lambda i: (i, 0))


def pair_tile(width):
    return pl.BlockSpec((2, TILE, width), lambda i: (0, i, 0))


def local_params():
    return pltpu.CompilerParams(vmem_limit_bytes=VLIM)


def front_kernel(x, w, par, packed, normed_out):
    unit, _ = normalized(x[...].astype(F32))
    normed = (unit * par[0:1] + par[2:3]).astype(BF)
    normed_out[...] = normed
    a = (dot(normed, matrix(w, 0)) + par[12:13]).astype(BF)
    packed[0, :, :D] = a
    b = (dot(normed, matrix(w, 1)) + par[13:14]).astype(BF)
    packed[0, :, D:] = b[:, :HALF]
    packed[1, :, :HALF] = b[:, HALF:]
    c = (dot(normed, matrix(w, 2)) + par[14:15]).astype(BF)
    packed[1, :, HALF:] = c


def front(x, w, par):
    return pl.pallas_call(
        front_kernel,
        name="front",
        grid=(STEPS,),
        out_shape=(
            jax.ShapeDtypeStruct((2, T, 3 * HALF), BF),
            jax.ShapeDtypeStruct((T, D), BF),
        ),
        in_specs=[tile(D), weight_spec(144, 0), whole((16, D))],
        out_specs=(pair_tile(3 * HALF), tile(D)),
        compiler_params=local_params(),
    )(x, w, par)


QB = 256


def head_masks(ref_value):
    lane = lax.broadcasted_iota(jnp.int32, ref_value.shape, 1)
    zero = jnp.zeros_like(ref_value)
    return (
        jnp.where(lane < 64, ref_value, zero),
        jnp.where(lane >= 64, ref_value, zero),
    )


def causal(rows, cols, offset):
    row = lax.broadcasted_iota(jnp.int32, (rows, cols), 0) + offset
    return lax.broadcasted_iota(jnp.int32, (rows, cols), 1) <= row


def attend_kernel(q_ref, k_ref, v_ref, mixed, logs):
    for i in range(L // QB):
        at = slice(i * QB, (i + 1) * QB)
        stop = (i + 1) * QB
        keys = k_ref[:stop]
        queries = head_masks(q_ref[at])
        values = head_masks(v_ref[:stop])
        keep = causal(QB, stop, i * QB)
        total = None
        saved = []
        for h in range(2):
            s = jnp.where(keep, dot_nt(queries[h], keys), -1e30)
            peak = jnp.max(s, axis=-1, keepdims=True)
            p = jnp.exp2((s - peak) * C2)
            norm = jnp.sum(p, axis=-1, keepdims=True)
            o = dot(p.astype(BF), values[h]) * (1.0 / norm)
            total = o if total is None else total + o
            saved.append(peak * C2 + jnp.log2(norm))
        mixed[at] = total.astype(BF)
        lane = lax.broadcasted_iota(jnp.int32, (QB, 128), 1)
        logs[0, at] = jnp.where(lane < 64, saved[0], saved[1])


def attend(heads):
    def col(k):
        return pl.BlockSpec((L, 128), lambda p: (0, p + 3 * k))

    return pl.pallas_call(
        attend_kernel,
        name="attend",
        grid=(3,),
        out_shape=(
            jax.ShapeDtypeStruct((L, HALF), BF),
            jax.ShapeDtypeStruct((3, L, 128), F32),
        ),
        in_specs=[col(0), col(1), col(2)],
        out_specs=(col(0), pl.BlockSpec((1, L, 128), lambda p: (p, 0, 0))),
        compiler_params=local_params(),
    )(heads, heads, heads)


def attend_back_kernel(q_ref, k_ref, v_ref, o_ref, do_ref, logs, out, dk, dv):
    p_at = pl.program_id(0)
    dk[...] = jnp.zeros_like(dk)
    dv[...] = jnp.zeros_like(dv)

    def columns(part):
        return pl.ds(pl.multiple_of(part * HALF + p_at * 128, 128), 128)

    for i in range(L // QB):
        at = slice(i * QB, (i + 1) * QB)
        stop = (i + 1) * QB
        keys = k_ref[:stop]
        values = v_ref[:stop]
        keys_of = head_masks(keys)
        queries = head_masks(q_ref[at])
        tops = head_masks(do_ref[at])
        keep = causal(QB, stop, i * QB)
        inner = head_masks(do_ref[at].astype(F32) * o_ref[at].astype(F32))
        dq = None
        for h in range(2):
            s = dot_nt(queries[h], keys)
            total = logs[0, at, 64 * h : 64 * h + 1]
            p = jnp.where(keep, jnp.exp2(s * C2 - total), 0.0)
            gw = dot_nt(tops[h], values)
            delta = jnp.sum(inner[h], axis=-1, keepdims=True)
            ds = (p * (gw - delta)).astype(BF)
            part = dot(ds, keys_of[h])
            dq = part if dq is None else dq + part
            dk[:stop] += dot_tn(ds, queries[h])
            dv[:stop] += dot_tn(p.astype(BF), tops[h])
        out[at, columns(0)] = (dq * SCALE).astype(BF)
    out[:, columns(1)] = (dk[...] * SCALE).astype(BF)
    out[:, columns(2)] = dv[...].astype(BF)


def attend_back(heads, mixed, grad_mixed, logs):
    def col(k):
        return pl.BlockSpec((L, 128), lambda p: (0, p + 3 * k))

    return pl.pallas_call(
        attend_back_kernel,
        name="attend_back",
        grid=(3,),
        out_shape=jax.ShapeDtypeStruct((L, 3 * HALF), BF),
        in_specs=[
            col(0),
            col(1),
            col(2),
            col(0),
            col(0),
            pl.BlockSpec((1, L, 128), lambda p: (p, 0, 0)),
        ],
        out_specs=pl.BlockSpec((L, 3 * HALF), lambda p: (0, 0)),
        scratch_shapes=[pltpu.VMEM((L, 128), F32)] * 2,
        compiler_params=local_params(),
    )(heads, heads, heads, mixed, grad_mixed, logs)


def gelu(v):
    return 0.5 * v * (1.0 + jnp.tanh(0.79788456 * (v + 0.044715 * v * v * v)))


def gelu_slope(v):
    square = v * v
    t = jnp.tanh(0.79788456 * v * (1.0 + 0.044715 * square))
    return 0.5 * (1.0 + t) + 0.5 * v * (1.0 - t * t) * 0.79788456 * (
        1.0 + 3 * 0.044715 * square
    )


def rear_kernel(x, mixed, wo, wf, wp, par, result, *kept):
    mix = jnp.concatenate([mixed[0], mixed[1]], axis=1)
    middle = x[...].astype(F32) + (dot(mix, matrix(wo, 0)) + par[5:6])
    unit, _ = normalized(middle)
    normed = (unit * par[1:2] + par[6:7]).astype(BF)
    total = middle + par[7:8]
    for m in range(4):
        pre = dot(normed, matrix(wf, m)) + par[8 + m : 9 + m]
        active = gelu(pre).astype(BF)
        if kept:
            kept[2][:, m * D : (m + 1) * D] = pre.astype(BF)
            kept[3][:, m * D : (m + 1) * D] = active
        total = total + dot(active, down_matrix(wp, m))
    result[...] = total.astype(BF)
    if kept:
        kept[0][...] = middle
        kept[1][...] = normed


def rear(x, mixed, w, par, keep):
    outs = [((T, D), BF)]
    specs = [tile(D)]
    if keep:
        outs += [((T, D), F32), ((T, D), BF), ((T, 4 * D), BF), ((T, 4 * D), BF)]
        specs += [tile(D), tile(D), tile(4 * D), tile(4 * D)]
    return pl.pallas_call(
        rear_kernel,
        name="rear",
        grid=(STEPS,),
        out_shape=tuple(jax.ShapeDtypeStruct(s, t) for s, t in outs),
        in_specs=[
            tile(D),
            pair_tile(HALF),
            weight_spec(48, 3),
            weight_spec(192, 1),
            weight_spec(192, 2),
            whole((16, D)),
        ],
        out_specs=tuple(specs),
        compiler_params=local_params(),
    )(x, mixed, w, w, w, par)


def column_sum(v):
    return jnp.sum(v, axis=0, keepdims=True)


def rear_back_kernel(e, middle, pre, wo, wf, wp, par, gmixed, gmiddle, mlow, gpre, sums):
    @pl.when(pl.program_id(0) == 0)
    def _():
        sums[...] = jnp.zeros_like(sums)

    top = e[...]
    top_wide = top.astype(F32)
    gnorm = None
    for m in range(4):
        cols = slice(m * D, (m + 1) * D)
        gact = dot_nt(top, down_matrix(wp, m))
        low = (gact * gelu_slope(pre[:, cols].astype(F32))).astype(BF)
        gpre[:, cols] = low
        sums[4 + m : 5 + m] += column_sum(low.astype(F32))
        part = dot_nt(low, matrix(wf, m))
        gnorm = part if gnorm is None else gnorm + part
    unit, inv = normalized(middle[...])
    sums[0:1] += column_sum(top_wide)
    sums[1:2] += column_sum(gnorm * unit)
    sums[2:3] += column_sum(gnorm)
    gmid = top_wide + norm_back(gnorm, par[1:2], unit, inv)
    sums[3:4] += column_sum(gmid)
    gmiddle[...] = gmid
    low = gmid.astype(BF)
    mlow[...] = low
    gm = dot_nt(low, matrix(wo, 0)).astype(BF)
    gmixed[0] = gm[:, :HALF]
    gmixed[1] = gm[:, HALF:]


def rear_back(e, middle, pre, w, par):
    return pl.pallas_call(
        rear_back_kernel,
        name="rear_back",
        grid=(STEPS,),
        out_shape=(
            jax.ShapeDtypeStruct((2, T, HALF), BF),
            jax.ShapeDtypeStruct((T, D), F32),
            jax.ShapeDtypeStruct((T, D), BF),
            jax.ShapeDtypeStruct((T, 4 * D), BF),
            jax.ShapeDtypeStruct((8, D), F32),
        ),
        in_specs=[
            tile(D),
            tile(D),
            tile(4 * D),
            weight_spec(48, 3),
            weight_spec(192, 1),
            weight_spec(192, 2),
            whole((16, D)),
        ],
        out_specs=(pair_tile(HALF), tile(D), tile(D), tile(4 * D), whole((8, D))),
        compiler_params=local_params(),
    )(e, middle, pre, w, w, w, par)


def front_back_kernel(gp, gmiddle, x, w, par, grad, sums):
    @pl.when(pl.program_id(0) == 0)
    def _():
        sums[...] = jnp.zeros_like(sums)

    gnorm = None
    for m, piece in enumerate(packed_pieces(gp)):
        sums[2 + m : 3 + m] += column_sum(piece.astype(F32))
        part = dot_nt(piece, matrix(w, m))
        gnorm = part if gnorm is None else gnorm + part
    unit, inv = normalized(x[...].astype(F32))
    sums[0:1] += column_sum(gnorm * unit)
    sums[1:2] += column_sum(gnorm)
    grad[...] = (gmiddle[...] + norm_back(gnorm, par[0:1], unit, inv)).astype(BF)


def packed_pieces(gp):
    return (
        gp[0, :, :D],
        jnp.concatenate([gp[0, :, D:], gp[1, :, :HALF]], axis=1),
        gp[1, :, HALF:],
    )


def front_back(gp, gmiddle, x, w, par):
    return pl.pallas_call(
        front_back_kernel,
        name="front_back",
        grid=(STEPS,),
        out_shape=(
            jax.ShapeDtypeStruct((T, D), BF),
            jax.ShapeDtypeStruct((8, D), F32),
        ),
        in_specs=[
            pair_tile(3 * HALF),
            tile(D),
            tile(D),
            weight_spec(144, 0),
            whole((16, D)),
        ],
        out_specs=(tile(D), whole((8, D))),
        compiler_params=local_params(),
    )(gp, gmiddle, x, w, par)


def weight_grads_kernel(normed, gp, mixed, mlow, normed2, gpre, active, top, small, out):
    def put(m, value):
        out[:, m * 48 : (m + 1) * 48, :] = value.astype(BF).reshape(16, 48, D)

    for m, piece in enumerate(packed_pieces(gp)):
        put(m, dot_tn(normed[...], piece))
    put(3, dot_tn(jnp.concatenate([mixed[0], mixed[1]], axis=1), mlow[...]))
    for m in range(4):
        put(4 + m, dot_tn(normed2[...], gpre[:, m * D : (m + 1) * D]))
    for m in range(4):
        value = dot_tn(active[:, m * D : (m + 1) * D], top[...])
        out[4 * m : 4 * m + 4, 384:576, :] = value.astype(BF).reshape(4, 192, D)
    out[:, 576:608, :] = small[...]


def weight_grads(*operands):
    return pl.pallas_call(
        weight_grads_kernel,
        name="weight_grads",
        out_shape=jax.ShapeDtypeStruct((16, ROWS, D), BF),
        in_specs=[VM] * len(operands),
        out_specs=VM,
        compiler_params=local_params(),
    )(*operands)


def reduce_kernel(
    grads, result, ingrad, total, out_a, out_b,
    own, r0, r1, r2, s1, s2, r3, lsem, s0s, s0r, s1s, s1r, s2s, s2r, s3s, s3r, os, orr, ol,
):
    core, z, y, x = where_am_i()
    block = z % 2
    sib = 1 - core
    dp = y * 4 + x
    sibling = (sib, z, dp)
    first = core == 0
    line = jnp.where(first, y, x)
    place = jnp.where(first, x, y)

    def on_line(step):
        to = (line + step) % 4
        return (core, z, jnp.where(first, to * 4 + x, y * 4 + to))

    def on_place(step):
        to = (place + step) % 4
        return (core, z, jnp.where(first, y * 4 + to, to * 4 + x))

    peers = [sibling]
    for step in (1, 2, 3):
        peers += [on_line(step), on_place(step)]
        for k in (0, 1):
            peers.append((k, (z + step) % 4, dp))
    greet(peers)

    mine = pl.ds(pl.multiple_of(core * HROWS, 16), HROWS)
    other = pl.ds(pl.multiple_of(sib * HROWS, 16), HROWS)

    def zero_copies(step):
        at = (line + step) % 4
        return at

    @pl.when(first)
    def _():
        for k in range(4):
            remote(grads.at[:, k, other], r0.at[k], s0s.at[k], s0r.at[k], sibling).start()
        for k in range(4):
            pltpu.make_async_copy(grads.at[k, :, mine], own.at[k], lsem.at[k]).start()

    @pl.when(jnp.logical_not(first))
    def _():
        for k in range(4):
            remote(grads.at[k, :, other], r0.at[k], s0s.at[k], s0r.at[k], sibling).start()
        for k in range(4):
            pltpu.make_async_copy(grads.at[:, k, mine], own.at[k], lsem.at[k]).start()

    for j in (0, 1):
        for n, (src, dst) in enumerate(((result, out_a), (ingrad, out_b))):
            here = (core == block) & (z == 2 * core + j)
            view = src.at[pl.ds(256 * j, 256)]

            @pl.when(here)
            def _():
                pltpu.make_async_copy(view, dst.at[z // 2], ol.at[n]).start()

            @pl.when(jnp.logical_not(here))
            def _():
                remote(
                    view, dst.at[z // 2], os.at[2 * j + n], orr.at[z // 2, n],
                    (block, 2 * core + j, dp),
                ).start()

    for k in range(4):
        pltpu.make_async_copy(own.at[k], own.at[k], lsem.at[k]).wait()
        remote(r0.at[k], r0.at[k], s0s.at[k], s0r.at[k], sibling).wait()

        @pl.loop(0, 4)
        def _(i):
            own[k, i] = (own[k, i].astype(F32) + r0[k, i].astype(F32)).astype(BF)

    for step in (2, 1, 3):
        at = (line + step) % 4
        remote(
            own.at[at], r1.at[step - 1], s1s.at[step], s1r.at[step], on_line(step)
        ).start()
    for step in (1, 3, 2):
        remote(own.at[0], r1.at[step - 1], s1s.at[step], s1r.at[step], sibling).wait()

    @pl.loop(0, 4)
    def _(i):
        s1[i] = (
            (own[line, i].astype(F32) + r1[0, i].astype(F32))
            + (r1[1, i].astype(F32) + r1[2, i].astype(F32))
        ).astype(BF)

    for step in (2, 1, 3):
        at = (place + step) % 4
        remote(
            s1.at[at], r2.at[step - 1], s2s.at[step], s2r.at[step], on_place(step)
        ).start()
    for step in (1, 3, 2):
        remote(s1.at[0], r2.at[step - 1], s2s.at[step], s2r.at[step], sibling).wait()
    s2[...] = (
        (s1[place].astype(F32) + r2[0].astype(F32))
        + (r2[1].astype(F32) + r2[2].astype(F32))
    ).astype(BF)

    for step in (2, 1, 3, 0):
        to = (z + step) % 4
        if step == 0:

            @pl.when(core == block)
            def _():
                pltpu.make_async_copy(s2, r3.at[core, z // 2], ol.at[2]).start()

            @pl.when(core != block)
            def _():
                remote(
                    s2, r3.at[core, z // 2], s3s.at[step], s3r.at[core, z // 2], sibling
                ).start()

        else:
            remote(
                s2, r3.at[core, z // 2], s3s.at[step], s3r.at[core, z // 2], (block, to, dp)
            ).start()
    for step in (1, 2, 3):
        remote(s2, s2, s3s.at[step], s3r.at[0, 0], sibling).wait_send()

    @pl.when(core == block)
    def _():
        pltpu.make_async_copy(s2, r3.at[core, z // 2], ol.at[2]).wait()

    @pl.when(core != block)
    def _():
        remote(s2, s2, s3s.at[0], s3r.at[0, 0], sibling).wait_send()

    for c in (0, 1):
        for s in (0, 1):
            here = (core == block) & (core == c) & (z // 2 == s)

            @pl.when(jnp.logical_not(here))
            def _():
                remote(s2, r3.at[c, s], s3s.at[0], s3r.at[c, s], sibling).wait_recv()

    for c in (0, 1):
        total[c * HROWS : (c + 1) * HROWS] = r3[c, 0].astype(F32) + r3[c, 1].astype(F32)

    for j in (0, 1):
        for n, (src, dst) in enumerate(((result, out_a), (ingrad, out_b))):
            here = (core == block) & (z == 2 * core + j)
            view = src.at[pl.ds(256 * j, 256)]

            @pl.when(here)
            def _():
                pltpu.make_async_copy(view, dst.at[z // 2], ol.at[n]).wait()

            @pl.when(jnp.logical_not(here))
            def _():
                remote(
                    view, dst.at[z // 2], os.at[2 * j + n], orr.at[0, n], sibling
                ).wait_send()

    for s in (0, 1):
        for n, dst in enumerate((out_a, out_b)):
            here = (core == z // 2) & (z == 2 * s + core)

            @pl.when(jnp.logical_not(here))
            def _():
                remote(
                    dst.at[s], dst.at[s], os.at[0], orr.at[s, n], sibling
                ).wait_recv()


def reduce(grads, result, ingrad):
    dma = pltpu.SemaphoreType.DMA
    return pl.pallas_call(
        reduce_kernel,
        name="reduce_grads",
        out_shape=(
            jax.ShapeDtypeStruct((ROWS, D), F32),
            jax.ShapeDtypeStruct((2, 256, D), BF),
            jax.ShapeDtypeStruct((2, 256, D), BF),
        ),
        in_specs=[ANY] * 3,
        out_specs=(VM, ANY, ANY),
        scratch_shapes=[
            pltpu.VMEM((4, 4, HROWS, D), BF),
            pltpu.VMEM((4, 4, HROWS, D), BF),
            pltpu.VMEM((3, 4, HROWS, D), BF),
            pltpu.VMEM((3, HROWS, D), BF),
            pltpu.VMEM((4, HROWS, D), BF),
            pltpu.VMEM((HROWS, D), BF),
            pltpu.VMEM((2, 2, HROWS, D), BF),
            dma((4,)),
            dma((4,)),
            dma((4,)),
            dma((4,)),
            dma((4,)),
            dma((4,)),
            dma((4,)),
            dma((4,)),
            dma((2, 2)),
            dma((4,)),
            dma((2, 2)),
            dma((3,)),
        ],
        compiler_params=comm_params(5),
    )(grads, result, ingrad)


def halves_first(v, rows):
    return v.reshape(rows, 3, 2, HALF).transpose(0, 2, 1, 3).reshape(rows, 3 * D)


def thirds_first(v, rows):
    return v.reshape(rows, 2, 3, HALF).transpose(0, 2, 1, 3).reshape(rows, 3 * D)


def body(inputs, cotangent, w_qkv, w_out, w_fc, w_proj, gains, biases, fc_bias):
    def stacked(v, blocks):
        return v.reshape(48, blocks, D).transpose(1, 0, 2).reshape(48 * blocks, D)

    small = jnp.concatenate([gains.reshape(96), biases.reshape(288), fc_bias.reshape(192)])
    small = jnp.pad(small[None], ((0, 31), (0, D - 576)))
    shard = jnp.concatenate(
        [
            stacked(halves_first(w_qkv[0], 48), 3),
            w_out[0],
            stacked(w_fc[0], 4),
            w_proj[0],
            small,
        ],
        0,
    )
    full, stream = gather(shard, inputs, cotangent)
    full = full.reshape(16, ROWS, D)

    def lanes(v, rows):
        return v.reshape(16, rows, 48).transpose(1, 0, 2).reshape(rows, D)

    values = full[:, 576, :576].astype(F32)
    shifts = lanes(values[:, 96:384], 6)
    packed_shift = jnp.concatenate([shifts[1], jnp.zeros((D,), F32), shifts[2]])
    par = jnp.concatenate(
        [
            lanes(values[:, :96], 2),
            shifts,
            values[:, 384:].reshape(4, D),
            halves_first(packed_shift[None], 1).reshape(3, D),
            jnp.zeros((1, D), F32),
        ],
        0,
    )

    def forward(x, keep):
        packed, normed = front(x, full, par)
        heads = cross(packed, 1).reshape(L, 3 * HALF)
        mixed_heads, logs = attend(heads)
        mixed = cross(mixed_heads.reshape(2, T, HALF), 2)
        return rear(x, mixed, full, par, keep), (normed, heads, mixed_heads, logs, mixed)

    (made,), _ = forward(stream, False)
    x = hand_over(made, stream, 0)
    (result, middle, normed2, pre, active), (normed, heads, mixed_heads, logs, mixed) = forward(
        x, True
    )

    def backward(e):
        gmixed, gmiddle, mlow, gpre, rear_sums = rear_back(e, middle, pre, full, par)
        gheads = cross(gmixed, 2).reshape(L, HALF)
        gpacked = attend_back(heads, mixed_heads, gheads, logs)
        gp = cross(gpacked.reshape(2, T, 3 * HALF), 1)
        grad, front_sums = front_back(gp, gmiddle, x, full, par)
        return grad, gp, mlow, gpre, rear_sums, front_sums

    grad = backward(stream)[0]
    e = hand_over(grad, stream, 1)
    grad, gp, mlow, gpre, rear_sums, front_sums = backward(e)

    def shards(v, rows):
        return v.reshape(rows, 16, 48).transpose(1, 0, 2).reshape(16, rows * 48)

    packed_sums = thirds_first(front_sums[2:5].reshape(1, 3 * D), 1).reshape(3, D)
    small = jnp.concatenate(
        [
            shards(jnp.stack([front_sums[0], rear_sums[1]]), 2),
            shards(
                jnp.stack(
                    [
                        front_sums[1],
                        packed_sums[0],
                        packed_sums[2],
                        rear_sums[3],
                        rear_sums[2],
                        rear_sums[0],
                    ]
                ),
                6,
            ),
            rear_sums[4:8].reshape(16, 192),
        ],
        1,
    ).astype(BF)
    small = jnp.pad(small[:, None, :], ((0, 0), (0, 31), (0, D - 576)))
    grads = weight_grads(normed, gp, mixed, mlow, normed2, gpre, active, e, small)
    total, section_out, in_grad = reduce(grads.reshape(4, 4, ROWS, D), result, grad)

    def unstacked(v, blocks):
        return v.reshape(blocks, 48, D).transpose(1, 0, 2).reshape(48, blocks * D)

    tail = total[576, :576]
    return (
        section_out[None],
        in_grad[None],
        thirds_first(unstacked(total[:144], 3), 48)[None],
        total[144:192][None],
        unstacked(total[192:384], 4)[None],
        total[384:576][None],
        tail[:96].reshape(1, 2, 48),
        tail[96:384].reshape(1, 6, 48),
        tail[384:].reshape(1, 192),
    )


def solution(mesh):
    in_specs = (
        P("dp", "seq", None),
        P("dp", "seq", None),
        P("section", "dp", None),
        P("section", "dp", None),
        P("section", "dp", None),
        P("section", "dp", None),
        P("section", None, "dp"),
        P("section", None, "dp"),
        P("section", "dp"),
    )
    out_specs = (
        P("section", "dp", "seq", None),
        P("section", "dp", "seq", None),
        P("section", "dp", None),
        P("section", "dp", None),
        P("section", "dp", None),
        P("section", "dp", None),
        P("section", None, "dp"),
        P("section", None, "dp"),
        P("section", "dp"),
    )
    return jax.shard_map(body, mesh=mesh, in_specs=in_specs, out_specs=out_specs, check_vma=False)
```

```python
import functools
import math

import jax
import jax.numpy as jnp
from jax import lax
from jax.experimental import pallas as pl
from jax.experimental.pallas import tpu as pltpu
from jax.sharding import PartitionSpec as P

MESH = pl.DeviceIdType.MESH
BF = jnp.bfloat16
F32 = jnp.float32
D = 768
T = 512
L = 1024
HALF = 384
ROWS = 608
HROWS = ROWS // 2
EPS = 1e-05
FC_ROWS = (192, 240, 304, 352)
SCALE = 0.125
C2 = SCALE * math.log2(math.e)
VLIM = 60 * 1024 * 1024
ANY = pl.BlockSpec(memory_space=pl.ANY)
VM = pl.BlockSpec(memory_space=pltpu.VMEM)


def where_am_i():
    core = lax.axis_index("section")
    z = lax.axis_index("seq")
    dp = lax.axis_index("dp")
    return core, z, dp // 4, dp % 4


def greet(peers):
    barrier = pltpu.get_barrier_semaphore()
    for peer in peers:
        pl.semaphore_signal(barrier, inc=1, device_id=peer, device_id_type=MESH)
    pl.semaphore_wait(barrier, len(peers))


def remote(src, dst, send, recv, peer):
    return pltpu.make_async_remote_copy(
        src_ref=src, dst_ref=dst, send_sem=send, recv_sem=recv, device_id=peer, device_id_type=MESH
    )


def comm_params(ident):
    return pltpu.CompilerParams(
        collective_id=ident, has_side_effects=True, vmem_limit_bytes=VLIM
    )


PIECES = ((0, 96), (96, 96), (192, 112))


def gather_kernel(
    wq, wo, wf, wp, small, ins, cots, full, stream, shard, part, lsem, gs, gr, ssem, rsem, xs, xr
):
    core, z, y, x = where_am_i()
    block = z % 2
    sib = 1 - core
    dp = y * 4 + x
    sibling = (sib, z, dp)
    first = core == 0
    count = len(PIECES)

    def along(axis, step):
        if axis == 0:
            return (core, z, y * 4 + (x + step) % 4)
        return (core, z, ((y + step) % 4) * 4 + x)

    @pl.when(core == block)
    def _():
        for h in range(2):
            for k in range(3):
                at = h * 3 + k
                shard[(at // 2) * 48 : (at // 2 + 1) * 48, (at % 2) * HALF : (at % 2 + 1) * HALF] = (
                    wq[0, :, k * D + h * HALF : k * D + (h + 1) * HALF]
                )
        shard[144:192] = wo[0]
        for m in range(4):
            shard[FC_ROWS[m] : FC_ROWS[m] + 48] = wf[0, :, m * D : (m + 1) * D]
        shard[288:304] = small[...]
        shard[400:592] = wp[0]
        shard[592:608] = jnp.zeros((16, D), BF)

    peers = [sibling]
    for step in (1, 2, 3):
        peers += [along(0, step), along(1, step), (core, (z + step) % 4, dp)]
    greet(peers)

    def span(p, whose):
        at, rows = PIECES[p]
        return pl.ds(pl.multiple_of(whose * HROWS + at, 16), rows)

    def give(p):
        view = shard.at[span(p, sib)]
        return remote(view, view, gs.at[p], gr.at[p], sibling)

    @pl.when(core == block)
    def _():
        for p in range(count):
            give(p).start()

    quarter = pl.ds(pl.multiple_of((z % 2) * 256, 256), 256)
    sends_tokens = (z // 2) == core
    for step in (1, 2, 3):
        to = (z + step) % 4
        for source, parity in ((ins, 0), (cots, 1)):

            @pl.when(sends_tokens & (to % 2 == parity))
            def _():
                remote(
                    source.at[to // 2],
                    stream.at[quarter],
                    xs.at[step],
                    xr.at[z % 2],
                    (core, to, dp),
                ).start()

    for source, parity in ((ins, 0), (cots, 1)):

        @pl.when(sends_tokens & (z % 2 == parity))
        def _():
            pltpu.make_async_copy(source.at[z // 2], part, lsem.at[count]).start()

    def shard_at(p, axis, step, whose):
        rows = span(p, whose)
        if axis == 0:
            return full.at[y, (x + step) % 4, rows]
        return full.at[(y + step) % 4, x, rows]

    def line_at(p, axis, step, half, whose):
        rows = span(p, whose)
        if axis == 0:
            return full.at[pl.ds(2 * half, 2), (x + step) % 4, rows]
        return full.at[(y + step) % 4, pl.ds(2 * half, 2), rows]

    def rest(axis):
        cross = 1 - axis
        out = []

        def send(p, slot, src, dst, to):
            copy = remote(src, dst, ssem.at[p, slot], rsem.at[p, slot], to)
            copy.start()
            out.append(copy)

        def came(p, slot, land):
            remote(land, land, ssem.at[p, slot], rsem.at[p, slot], sibling).wait_recv()

        for p in range(count):

            @pl.when(core != block)
            def _():
                view = shard.at[span(p, core)]
                remote(view, view, gs.at[p], gr.at[p], sibling).wait_recv()

            view = shard.at[span(p, core)]
            land = shard_at(p, axis, 0, core)
            for k in (2, 1, 3):
                send(p, k, view, land, along(axis, k))
            send(p, 14, view, land, sibling)
            pltpu.make_async_copy(view, land, lsem.at[p]).start()
        for p in range(count):
            land = shard_at(p, axis, 0, core)
            pltpu.make_async_copy(shard.at[span(p, core)], land, lsem.at[p]).wait()
            for k in (1, 3, 2):
                came(p, k, shard_at(p, axis, 4 - k, core))
            for half in (0, 1):
                for slot, step in ((4, 1), (6, 3)):
                    view = line_at(p, cross, 0, half, core)
                    send(p, slot + half, view, view, along(cross, step))
            for k in (1, 3, 2):
                view = shard_at(p, axis, 4 - k, core)
                send(p, 14 + k, view, view, sibling)
        for p in range(count):
            for half, slot, step, to in ((0, 4, 3, 1), (1, 6, 1, 3), (1, 4, 3, 0), (0, 6, 1, 0)):
                land = line_at(p, cross, step, half, core)
                came(p, slot + half, land)
                if to:
                    send(p, 8 + half, land, land, along(cross, to))
                send(p, 14 + slot + half, land, land, sibling)
        for p in range(count):
            for half in (0, 1):
                land = line_at(p, cross, 2, half, core)
                came(p, 8 + half, land)
                send(p, 22 + half, land, land, sibling)
        for p in range(count):
            came(p, 14, shard_at(p, cross, 0, sib))
            for k in (1, 3, 2):
                came(p, 14 + k, shard_at(p, cross, 4 - k, sib))
            for half, slot, step in ((0, 4, 3), (1, 6, 1), (1, 4, 3), (0, 6, 1)):
                came(p, 14 + slot + half, line_at(p, axis, step, half, sib))
            for half in (0, 1):
                came(p, 22 + half, line_at(p, axis, 2, half, sib))
        for copy in out:
            copy.wait_send()

    @pl.when(first)
    def _():
        rest(0)

    @pl.when(jnp.logical_not(first))
    def _():
        rest(1)

    @pl.when(core == block)
    def _():
        for p in range(count):
            give(p).wait_send()

    @pl.when(sends_tokens)
    def _():
        pltpu.make_async_copy(ins.at[0], part, lsem.at[count]).wait()
        copy = pltpu.make_async_copy(part, stream.at[quarter], lsem.at[count])
        copy.start()
        for step in (1, 2, 3):
            remote(ins.at[0], stream.at[quarter], xs.at[step], xr.at[0], sibling).wait_send()
        copy.wait()

    for j in (0, 1):

        @pl.when(z != 2 * core + j)
        def _():
            land = stream.at[pl.ds(256 * j, 256)]
            remote(land, land, xs.at[0], xr.at[j], sibling).wait_recv()


def gather(wq, wo, wf, wp, small, ins, cots):
    dma = pltpu.SemaphoreType.DMA
    n = len(PIECES)
    return pl.pallas_call(
        gather_kernel,
        name="gather_weights",
        out_shape=(
            jax.ShapeDtypeStruct((4, 4, ROWS, D), BF),
            jax.ShapeDtypeStruct((T, D), BF),
        ),
        in_specs=[VM] * 5 + [ANY] * 2,
        out_specs=(ANY, ANY),
        scratch_shapes=[
            pltpu.VMEM((ROWS, D), BF),
            pltpu.VMEM((256, D), BF),
            dma((n + 1,)),
            dma((n,)),
            dma((n,)),
            dma((n, 24)),
            dma((n, 24)),
            dma((4,)),
            dma((2,)),
        ],
        compiler_params=comm_params(0),
    )(wq, wo, wf, wp, small, ins, cots)


def cross_kernel(src, dst, stage, lsem, ssem, rsem):
    core, z, y, x = where_am_i()
    sibling = (1 - core, z, y * 4 + x)
    local_in = pltpu.make_async_copy(src.at[core], stage, lsem)
    local_in.start()
    greet([sibling])
    out = remote(src.at[1 - core], dst.at[core], ssem, rsem, sibling)
    out.start()
    local_in.wait()
    local_out = pltpu.make_async_copy(stage, dst.at[core], lsem)
    local_out.start()
    local_out.wait()
    out.wait_send()
    remote(src.at[1 - core], dst.at[1 - core], ssem, rsem, sibling).wait_recv()


def cross(pieces, ident):
    return pl.pallas_call(
        cross_kernel,
        name="cross_cores",
        out_shape=jax.ShapeDtypeStruct(pieces.shape, pieces.dtype),
        in_specs=[ANY],
        out_specs=ANY,
        scratch_shapes=[pltpu.VMEM(pieces.shape[1:], pieces.dtype)]
        + [pltpu.SemaphoreType.DMA] * 3,
        compiler_params=comm_params(ident),
    )(pieces)


def dot(a, b):
    return jnp.dot(a, b, preferred_element_type=F32)


def dot_nt(a, b):
    return lax.dot_general(a, b, (((1,), (1,)), ((), ())), preferred_element_type=F32)


def dot_tn(a, b):
    return lax.dot_general(a, b, (((0,), (0,)), ((), ())), preferred_element_type=F32)


def normalized(v):
    centre = v - jnp.mean(v, axis=-1, keepdims=True)
    inv = lax.rsqrt(jnp.mean(centre * centre, axis=-1, keepdims=True) + EPS)
    return centre * inv, inv


def norm_back(grad, gain, unit, inv):
    g = grad * gain
    return inv * (
        g
        - jnp.mean(g, axis=-1, keepdims=True)
        - unit * jnp.mean(g * unit, axis=-1, keepdims=True)
    )


def matrix(ref, m):
    return ref[m].reshape(D, D)


class Fetch:
    def __init__(self, w, sems, parts):
        self.copies = []
        for at, (buffer, m, kind) in enumerate(parts):
            if kind is None:
                src = w.at[pl.ds(4 * m, 4), pl.ds(400, 192)]
            else:
                src = w.at[:, pl.ds(kind, 48)]
            self.copies.append(pltpu.make_async_copy(src, buffer.at[m], sems.at[at]))
        for copy in self.copies:
            copy.start()

    def need(self, at):
        self.copies[at].wait()


class Store:
    def __init__(self, sems):
        self.sems = sems
        self.copies = []

    def put(self, src, dst):
        copy = pltpu.make_async_copy(src, dst, self.sems.at[len(self.copies)])
        copy.start()
        self.copies.append(copy)

    def finish(self):
        for copy in self.copies:
            copy.wait()


def wide(*lead):
    return pltpu.VMEM((*lead, D), BF)


def local_params():
    return pltpu.CompilerParams(vmem_limit_bytes=VLIM)


TILES = (slice(0, 256), slice(256, 512))


def front_tile(at, need, x, wq, par, packed, normed_out):
    unit, _ = normalized(x[at].astype(F32))
    normed = (unit * par[0:1] + par[2:3]).astype(BF)
    normed_out[at] = normed
    need(0)
    a = (dot(normed, matrix(wq, 0)) + par[12:13]).astype(BF)
    packed[0, at, :D] = a
    need(1)
    b = (dot(normed, matrix(wq, 1)) + par[13:14]).astype(BF)
    packed[0, at, D:] = b[:, :HALF]
    packed[1, at, :HALF] = b[:, HALF:]
    need(2)
    c = (dot(normed, matrix(wq, 2)) + par[14:15]).astype(BF)
    packed[1, at, HALF:] = c


def nothing(at):
    pass


def front_kernel(x, w, par, packed, normed_out, wq, sems):
    fetch = Fetch(w, sems, QKV_PARTS(wq))
    for i, at in enumerate(TILES):
        front_tile(at, nothing if i else fetch.need, x, wq, par, packed, normed_out)


def QKV_PARTS(wq):
    return [(wq, m, 48 * m) for m in range(3)]


def front(x, w, par):
    return pl.pallas_call(
        front_kernel,
        name="front",
        out_shape=(
            jax.ShapeDtypeStruct((2, T, 3 * HALF), BF),
            jax.ShapeDtypeStruct((T, D), BF),
        ),
        in_specs=[VM, ANY, VM],
        out_specs=(VM, VM),
        scratch_shapes=[wide(3, 16, 48), pltpu.SemaphoreType.DMA((3,))],
        compiler_params=local_params(),
    )(x, w, par)


QB = 256


def head_masks(ref_value):
    lane = lax.broadcasted_iota(jnp.int32, ref_value.shape, 1)
    zero = jnp.zeros_like(ref_value)
    return (
        jnp.where(lane < 64, ref_value, zero),
        jnp.where(lane >= 64, ref_value, zero),
    )


def causal(rows, cols, offset):
    row = lax.broadcasted_iota(jnp.int32, (rows, cols), 0) + offset
    return lax.broadcasted_iota(jnp.int32, (rows, cols), 1) <= row


def attend_kernel(q_ref, k_ref, v_ref, mixed, logs):
    for i in range(L // QB):
        at = slice(i * QB, (i + 1) * QB)
        stop = (i + 1) * QB
        keys = k_ref[:stop]
        queries = head_masks(q_ref[at])
        values = head_masks(v_ref[:stop])
        keep = causal(QB, stop, i * QB)
        total = None
        saved = []
        for h in range(2):
            s = jnp.where(keep, dot_nt(queries[h], keys), -1e30)
            peak = jnp.max(s, axis=-1, keepdims=True)
            p = jnp.exp2((s - peak) * C2)
            norm = jnp.sum(p, axis=-1, keepdims=True)
            o = dot(p.astype(BF), values[h]) * (1.0 / norm)
            total = o if total is None else total + o
            saved.append(peak * C2 + jnp.log2(norm))
        mixed[at] = total.astype(BF)
        lane = lax.broadcasted_iota(jnp.int32, (QB, 128), 1)
        logs[0, at] = jnp.where(lane < 64, saved[0], saved[1])


def attend(heads):
    def col(k):
        return pl.BlockSpec((L, 128), lambda p: (0, p + 3 * k))

    return pl.pallas_call(
        attend_kernel,
        name="attend",
        grid=(3,),
        out_shape=(
            jax.ShapeDtypeStruct((L, HALF), BF),
            jax.ShapeDtypeStruct((3, L, 128), F32),
        ),
        in_specs=[col(0), col(1), col(2)],
        out_specs=(col(0), pl.BlockSpec((1, L, 128), lambda p: (p, 0, 0))),
        compiler_params=local_params(),
    )(heads, heads, heads)


def attend_back_kernel(q_ref, k_ref, v_ref, o_ref, do_ref, logs, out, dk, dv):
    p_at = pl.program_id(0)
    dk[...] = jnp.zeros_like(dk)
    dv[...] = jnp.zeros_like(dv)

    def columns(part):
        return pl.ds(pl.multiple_of(part * HALF + p_at * 128, 128), 128)

    for i in range(L // QB):
        at = slice(i * QB, (i + 1) * QB)
        stop = (i + 1) * QB
        keys = k_ref[:stop]
        values = v_ref[:stop]
        keys_of = head_masks(keys)
        queries = head_masks(q_ref[at])
        tops = head_masks(do_ref[at])
        keep = causal(QB, stop, i * QB)
        inner = head_masks(do_ref[at].astype(F32) * o_ref[at].astype(F32))
        dq = None
        for h in range(2):
            s = dot_nt(queries[h], keys)
            total = logs[0, at, 64 * h : 64 * h + 1]
            p = jnp.where(keep, jnp.exp2(s * C2 - total), 0.0)
            gw = dot_nt(tops[h], values)
            delta = jnp.sum(inner[h], axis=-1, keepdims=True)
            ds = (p * (gw - delta)).astype(BF)
            part = dot(ds, keys_of[h])
            dq = part if dq is None else dq + part
            dk[:stop] += dot_tn(ds, queries[h])
            dv[:stop] += dot_tn(p.astype(BF), tops[h])
        out[at, columns(0)] = (dq * SCALE).astype(BF)
    out[:, columns(1)] = (dk[...] * SCALE).astype(BF)
    out[:, columns(2)] = dv[...].astype(BF)


def attend_back(heads, mixed, grad_mixed, logs):
    def col(k):
        return pl.BlockSpec((L, 128), lambda p: (0, p + 3 * k))

    return pl.pallas_call(
        attend_back_kernel,
        name="attend_back",
        grid=(3,),
        out_shape=jax.ShapeDtypeStruct((L, 3 * HALF), BF),
        in_specs=[
            col(0),
            col(1),
            col(2),
            col(0),
            col(0),
            pl.BlockSpec((1, L, 128), lambda p: (p, 0, 0)),
        ],
        out_specs=pl.BlockSpec((L, 3 * HALF), lambda p: (0, 0)),
        scratch_shapes=[pltpu.VMEM((L, 128), F32)] * 2,
        compiler_params=local_params(),
    )(heads, heads, heads, mixed, grad_mixed, logs)


REAR_SCRATCH = [
    wide(1, 16, 48),
    wide(4, 16, 48),
    wide(4, 4, 192),
    pltpu.SemaphoreType.DMA((9,)),
]


def gelu(v):
    return 0.5 * v * (1.0 + jnp.tanh(0.79788456 * (v + 0.044715 * v * v * v)))


def gelu_slope(v):
    square = v * v
    t = jnp.tanh(0.79788456 * v * (1.0 + 0.044715 * square))
    return 0.5 * (1.0 + t) + 0.5 * v * (1.0 - t * t) * 0.79788456 * (
        1.0 + 3 * 0.044715 * square
    )


def forward_parts(wo, wf, wp):
    parts = [(wo, 0, 144)]
    for m in range(4):
        parts += [(wf, m, FC_ROWS[m]), (wp, m, None)]
    return parts


def backward_parts(wo, wf, wp):
    parts = []
    for m in range(4):
        parts += [(wp, m, None), (wf, m, FC_ROWS[m])]
    return parts + [(wo, 0, 144)]


def rear_tile(at, need, x, mixed, wo, wf, wp, par, result, kept, store):
    mix = jnp.concatenate([mixed[0, at], mixed[1, at]], axis=1)
    need(0)
    middle = x[at].astype(F32) + (dot(mix, matrix(wo, 0)) + par[5:6])
    unit, _ = normalized(middle)
    normed = (unit * par[1:2] + par[6:7]).astype(BF)
    if kept:
        kept[0][at] = middle
        kept[1][at] = normed
        store(0, at, None)
        store(1, at, None)
    total = middle + par[7:8]
    for m in range(4):
        need(1 + 2 * m)
        pre = dot(normed, matrix(wf, m)) + par[8 + m : 9 + m]
        active = gelu(pre).astype(BF)
        if kept:
            cols = slice(m * D, (m + 1) * D)
            kept[2][at, cols] = pre.astype(BF)
            kept[3][at, cols] = active
            store(2, at, cols)
            store(3, at, cols)
        need(2 + 2 * m)
        total = total + dot(active, matrix(wp, m))
    result[at] = total.astype(BF)


def column_sum(v):
    return jnp.sum(v, axis=0, keepdims=True)


def adder(sums, i):
    def add(row, v):
        if i:
            sums[row : row + 1] += column_sum(v)
        else:
            sums[row : row + 1] = column_sum(v)

    return add


def rear_back_tile(at, need, e, middle, pre, wo, wf, wp, par, gmixed, gmiddle, full):
    if full:
        add, mlow, gpre, store = full
    top = e[at]
    gnorm = None
    for m in range(4):
        cols = slice(m * D, (m + 1) * D)
        need(2 * m)
        gact = dot_nt(top, matrix(wp, m))
        low = (gact * gelu_slope(pre[at, cols].astype(F32))).astype(BF)
        if full:
            gpre[at, cols] = low
            store(0, at, cols)
            add(4 + m, low.astype(F32))
        need(2 * m + 1)
        part = dot_nt(low, matrix(wf, m))
        gnorm = part if gnorm is None else gnorm + part
    unit, inv = normalized(middle[at])
    top_wide = top.astype(F32)
    gmid = top_wide + norm_back(gnorm, par[1:2], unit, inv)
    gmiddle[at] = gmid
    low = gmid.astype(BF)
    if full:
        add(0, top_wide)
        add(1, gnorm * unit)
        add(2, gnorm)
        add(3, gmid)
        mlow[at] = low
        store(1, at, None)
    need(8)
    gm = dot_nt(low, matrix(wo, 0)).astype(BF)
    gmixed[0, at] = gm[:, :HALF]
    gmixed[1, at] = gm[:, HALF:]


def front_back_tile(at, need, gp, gmiddle, x, wq, par, grad, add):
    gnorm = None
    for m, piece in enumerate(packed_pieces(gp, at)):
        if add:
            add(2 + m, piece.astype(F32))
        need(m)
        part = dot_nt(piece, matrix(wq, m))
        gnorm = part if gnorm is None else gnorm + part
    unit, inv = normalized(x[at].astype(F32))
    if add:
        add(0, gnorm * unit)
        add(1, gnorm)
    grad[at] = (gmiddle[at] + norm_back(gnorm, par[0:1], unit, inv)).astype(BF)


def partner_of():
    core, z, y, x = where_am_i()
    return z % 2, (core, z + 1 - 2 * (z % 2), y * 4 + x)


def rear_front_kernel(
    x, mixed, w, par, x2, packed, normed, wo, wf, wp, sems, wq, qsems, res, ssem, rsem
):
    block, partner = partner_of()
    fetch = Fetch(w, sems, forward_parts(wo, wf, wp))
    fetch_q = Fetch(w, qsems, QKV_PARTS(wq))
    greet([partner])

    def hand(i):
        rows = pl.ds(256 * i, 256)
        return remote(res.at[rows], x2.at[rows], ssem.at[i], rsem.at[i], partner)

    @pl.when(block == 0)
    def _():
        for i, at in enumerate(TILES):
            rear_tile(
                at, nothing if i else fetch.need, x, mixed, wo, wf, wp, par, res, None, None
            )
            hand(i).start()
        x2[...] = x[...]

    @pl.when(block == 1)
    def _():
        for k in range(9):
            fetch.need(k)

    for k in range(3):
        fetch_q.need(k)
    for i, at in enumerate(TILES):
        pl.when(block == 1)(hand(i).wait_recv)
        front_tile(at, nothing, x2, wq, par, packed, normed)

    @pl.when(block == 0)
    def _():
        for i in range(2):
            hand(i).wait_send()


def rear_front(x, mixed, w, par):
    dma = pltpu.SemaphoreType.DMA
    return pl.pallas_call(
        rear_front_kernel,
        name="rear_hand_front",
        out_shape=(
            jax.ShapeDtypeStruct((T, D), BF),
            jax.ShapeDtypeStruct((2, T, 3 * HALF), BF),
            jax.ShapeDtypeStruct((T, D), BF),
        ),
        in_specs=[VM, VM, ANY, VM],
        out_specs=(VM, VM, VM),
        scratch_shapes=REAR_SCRATCH
        + [wide(3, 16, 48), dma((3,)), wide(T), dma((2,)), dma((2,))],
        compiler_params=comm_params(3),
    )(x, mixed, w, par)


def turn_kernel(
    x, mixed, e, w, par, result, gmixed, gmiddle, middle_out, normed_out, pre_out, active_out,
    wo, wf, wp, sems, middle, normed, pre, active, osems,
):
    fetch = Fetch(w, sems, forward_parts(wo, wf, wp))
    store = Store(osems)
    kept = (middle, normed, pre, active)
    outs = (middle_out, normed_out, pre_out, active_out)

    def put(n, at, cols):
        rows = pl.ds(at.start, at.stop - at.start)
        if cols is None:
            store.put(kept[n].at[rows], outs[n].at[rows])
        else:
            lanes = pl.ds(cols.start, D)
            store.put(kept[n].at[rows, lanes], outs[n].at[rows, lanes])

    for i, at in enumerate(TILES):
        rear_tile(
            at, nothing if i else fetch.need, x, mixed, wo, wf, wp, par, result, kept, put
        )
    for at in TILES:
        rear_back_tile(at, nothing, e, middle, pre, wo, wf, wp, par, gmixed, gmiddle, None)
    store.finish()


def turn(x, mixed, e, w, par):
    kept = [((T, D), F32), ((T, D), BF), ((T, 4 * D), BF), ((T, 4 * D), BF)]
    outs = [((T, D), BF), ((2, T, HALF), BF), ((T, D), F32)] + kept
    return pl.pallas_call(
        turn_kernel,
        name="turn",
        out_shape=tuple(jax.ShapeDtypeStruct(s, t) for s, t in outs),
        in_specs=[VM, VM, VM, ANY, VM],
        out_specs=(VM, VM, VM, ANY, ANY, ANY, ANY),
        scratch_shapes=REAR_SCRATCH
        + [pltpu.VMEM(s, t) for s, t in kept]
        + [pltpu.SemaphoreType.DMA((20,))],
        compiler_params=local_params(),
    )(x, mixed, e, w, par)


def back_back_kernel(
    gp, gmid_in, x, stream, middle, pre_in, w, par,
    e, gmixed, gmiddle, sums, mlow_out, gpre_out,
    wo, wf, wp, sems, wq, qsems, res, ssem, rsem, pre, mlow, gpre, psem, osems,
):
    block, partner = partner_of()
    fetch_q = Fetch(w, qsems, QKV_PARTS(wq))
    fetch = Fetch(w, sems, backward_parts(wo, wf, wp))
    load = pltpu.make_async_copy(pre_in, pre, psem)
    load.start()
    greet([partner])

    def hand(i):
        rows = pl.ds(256 * i, 256)
        return remote(res.at[rows], e.at[rows], ssem.at[i], rsem.at[i], partner)

    for k in range(3):
        fetch_q.need(k)

    @pl.when(block == 1)
    def _():
        for i, at in enumerate(TILES):
            front_back_tile(at, nothing, gp, gmid_in, x, wq, par, res, None)
            hand(i).start()
        e[...] = stream[...]

    for k in range(9):
        fetch.need(k)
    load.wait()
    store = Store(osems)

    def put(n, at, cols):
        rows = pl.ds(at.start, at.stop - at.start)
        if cols is None:
            store.put(mlow.at[rows], mlow_out.at[rows])
        else:
            lanes = pl.ds(cols.start, D)
            store.put(gpre.at[rows, lanes], gpre_out.at[rows, lanes])

    for i, at in enumerate(TILES):
        pl.when(block == 0)(hand(i).wait_recv)
        rear_back_tile(
            at, nothing, e, middle, pre, wo, wf, wp, par, gmixed, gmiddle,
            (adder(sums, i), mlow, gpre, put),
        )

    @pl.when(block == 1)
    def _():
        for i in range(2):
            hand(i).wait_send()

    store.finish()


def back_back(gp, gmid, x, stream, middle, pre, w, par):
    dma = pltpu.SemaphoreType.DMA
    return pl.pallas_call(
        back_back_kernel,
        name="front_back_hand_rear_back",
        out_shape=(
            jax.ShapeDtypeStruct((T, D), BF),
            jax.ShapeDtypeStruct((2, T, HALF), BF),
            jax.ShapeDtypeStruct((T, D), F32),
            jax.ShapeDtypeStruct((8, D), F32),
            jax.ShapeDtypeStruct((T, D), BF),
            jax.ShapeDtypeStruct((T, 4 * D), BF),
        ),
        in_specs=[VM, VM, VM, VM, VM, ANY, ANY, VM],
        out_specs=(VM, VM, VM, VM, ANY, ANY),
        scratch_shapes=REAR_SCRATCH
        + [wide(3, 16, 48), dma((3,)), wide(T), dma((2,)), dma((2,))]
        + [pltpu.VMEM((T, 4 * D), BF), wide(T), pltpu.VMEM((T, 4 * D), BF)]
        + [dma, dma((10,))],
        compiler_params=comm_params(4),
    )(gp, gmid, x, stream, middle, pre, w, par)


def front_back_kernel(gp, gmiddle, x, w, par, grad, sums, wq, sems):
    fetch = Fetch(w, sems, QKV_PARTS(wq))
    sums[5:8] = jnp.zeros((3, D), F32)
    for i, at in enumerate(TILES):
        front_back_tile(
            at, nothing if i else fetch.need, gp, gmiddle, x, wq, par, grad, adder(sums, i)
        )


def packed_pieces(gp, at=slice(None)):
    return (
        gp[0, at, :D],
        jnp.concatenate([gp[0, at, D:], gp[1, at, :HALF]], axis=1),
        gp[1, at, HALF:],
    )


def front_back(gp, gmiddle, x, w, par):
    return pl.pallas_call(
        front_back_kernel,
        name="front_back",
        out_shape=(
            jax.ShapeDtypeStruct((T, D), BF),
            jax.ShapeDtypeStruct((8, D), F32),
        ),
        in_specs=[VM, VM, VM, ANY, VM],
        out_specs=(VM, VM),
        scratch_shapes=[wide(3, 16, 48), pltpu.SemaphoreType.DMA((3,))],
        compiler_params=local_params(),
    )(gp, gmiddle, x, w, par)


def weight_grads_kernel(normed, gp, mixed, mlow, normed2, gpre, active, top, small, out):
    def put(m, value):
        at = FC_ROWS[m - 4] if m > 3 else m * 48
        out[:, at : at + 48, :] = value.astype(BF).reshape(16, 48, D)

    for m, piece in enumerate(packed_pieces(gp)):
        put(m, dot_tn(normed[...], piece))
    put(3, dot_tn(jnp.concatenate([mixed[0], mixed[1]], axis=1), mlow[...]))
    for m in range(4):
        put(4 + m, dot_tn(normed2[...], gpre[:, m * D : (m + 1) * D]))
    for m in range(4):
        value = dot_tn(active[:, m * D : (m + 1) * D], top[...])
        out[4 * m : 4 * m + 4, 400:592, :] = value.astype(BF).reshape(4, 192, D)
    out[:, 288:304, :] = small[...]
    out[:, 592:608, :] = jnp.zeros((16, 16, D), BF)


def weight_grads(*operands):
    return pl.pallas_call(
        weight_grads_kernel,
        name="weight_grads",
        out_shape=jax.ShapeDtypeStruct((16, ROWS, D), BF),
        in_specs=[VM] * len(operands),
        out_specs=VM,
        compiler_params=local_params(),
    )(*operands)


STAGES = ((0, 48), (48, 48), (96, 48), (144, 48), (192, 48), (240, 64))


def reduce_kernel(
    grads, result, ingrad, gq, go, gf, gp, gsmall, out_a, out_b,
    own, r0, r1, r2, s1, s2, r3, lsem, s0s, s0r, s1s, s1r, s2s, s2r, s3s, s3r, os, orr, ol,
):
    core, z, y, x = where_am_i()
    block = z % 2
    sib = 1 - core
    dp = y * 4 + x
    sibling = (sib, z, dp)
    first = core == 0
    line = jnp.where(first, y, x)
    place = jnp.where(first, x, y)
    seq = z // 2

    def on_line(step):
        to = (line + step) % 4
        return (core, z, jnp.where(first, to * 4 + x, y * 4 + to))

    def on_place(step):
        to = (place + step) % 4
        return (core, z, jnp.where(first, y * 4 + to, to * 4 + x))

    peers = [sibling]
    for step in (1, 2, 3):
        peers += [on_line(step), on_place(step)]
        for k in (0, 1):
            peers.append((k, (z + step) % 4, dp))
    greet(peers)

    def rows(p):
        return pl.ds(*STAGES[p])

    def span(p, whose):
        at, n = STAGES[p]
        return pl.ds(pl.multiple_of(whose * HROWS + at, 16), n)

    def exchange(p, k):
        return remote(
            own.at[k, :, rows(p)], r0.at[k, :, rows(p)], s0s.at[p, k], s0r.at[p, k], sibling
        )

    def load(p, k):
        return pltpu.make_async_copy(
            r0.at[k, :, rows(p)], own.at[k, :, rows(p)], lsem.at[p, k]
        )

    @pl.when(first)
    def _():
        for p in range(len(STAGES)):
            for k in range(4):
                remote(
                    grads.at[:, k, span(p, sib)],
                    r0.at[k, :, rows(p)],
                    s0s.at[p, k],
                    s0r.at[p, k],
                    sibling,
                ).start()
                pltpu.make_async_copy(
                    grads.at[k, :, span(p, core)], own.at[k, :, rows(p)], lsem.at[p, k]
                ).start()

    @pl.when(jnp.logical_not(first))
    def _():
        for p in range(len(STAGES)):
            for k in range(4):
                remote(
                    grads.at[k, :, span(p, sib)],
                    r0.at[k, :, rows(p)],
                    s0s.at[p, k],
                    s0r.at[p, k],
                    sibling,
                ).start()
                pltpu.make_async_copy(
                    grads.at[:, k, span(p, core)], own.at[k, :, rows(p)], lsem.at[p, k]
                ).start()

    def outputs(j, n):
        src, dst = ((result, out_a), (ingrad, out_b))[n]
        here = (core == block) & (z == 2 * core + j)
        view = src.at[pl.ds(256 * j, 256)]
        keep = pltpu.make_async_copy(view, dst.at[seq], ol.at[n])
        give = remote(
            view, dst.at[seq], os.at[2 * j + n], orr.at[seq, n], (block, 2 * core + j, dp)
        )
        return here, keep, give

    for j in (0, 1):
        for n in (0, 1):
            here, keep, give = outputs(j, n)
            pl.when(here)(keep.start)
            pl.when(jnp.logical_not(here))(give.start)

    def swap_cores(p):
        for k in range(4):
            load(p, k).wait()
            exchange(p, k).wait()

        @pl.loop(0, 16)
        def _(i):
            a = own[i // 4, i % 4, rows(p)].astype(F32)
            b = r0[i // 4, i % 4, rows(p)].astype(F32)
            own[i // 4, i % 4, rows(p)] = (a + b).astype(BF)

        for step in (2, 1, 3):
            remote(
                own.at[(line + step) % 4, :, rows(p)],
                r1.at[step - 1, :, rows(p)],
                s1s.at[p, step],
                s1r.at[p, step],
                on_line(step),
            ).start()

    def over_lines(p):
        for step in (1, 3, 2):
            remote(
                own.at[0, :, rows(p)],
                r1.at[step - 1, :, rows(p)],
                s1s.at[p, step],
                s1r.at[p, step],
                sibling,
            ).wait()

        @pl.loop(0, 4)
        def _(i):
            s1[i, rows(p)] = (
                (own[line, i, rows(p)].astype(F32) + r1[0, i, rows(p)].astype(F32))
                + (r1[1, i, rows(p)].astype(F32) + r1[2, i, rows(p)].astype(F32))
            ).astype(BF)

        for step in (2, 1, 3):
            remote(
                s1.at[(place + step) % 4, rows(p)],
                r2.at[step - 1, rows(p)],
                s2s.at[p, step],
                s2r.at[p, step],
                on_place(step),
            ).start()

    def along_z(p, step):
        return remote(
            s2.at[rows(p)],
            r3.at[core, seq, rows(p)],
            s3s.at[p, step],
            s3r.at[p, core, seq],
            (block, (z + step) % 4, dp),
        )

    def keep_sum(p):
        return pltpu.make_async_copy(s2.at[rows(p)], r3.at[core, seq, rows(p)], ol.at[2 + p])

    def over_places(p):
        for step in (1, 3, 2):
            remote(
                s1.at[0, rows(p)],
                r2.at[step - 1, rows(p)],
                s2s.at[p, step],
                s2r.at[p, step],
                sibling,
            ).wait()
        s2[rows(p)] = (
            (s1[place, rows(p)].astype(F32) + r2[0, rows(p)].astype(F32))
            + (r2[1, rows(p)].astype(F32) + r2[2, rows(p)].astype(F32))
        ).astype(BF)
        for step in (2, 1, 3):
            along_z(p, step).start()
        pl.when(core == block)(keep_sum(p).start)

        @pl.when(core != block)
        def _():
            remote(
                s2.at[rows(p)],
                r3.at[core, seq, rows(p)],
                s3s.at[p, 0],
                s3r.at[p, core, seq],
                sibling,
            ).start()

    def finish(p):
        for step in (1, 2, 3):
            along_z(p, step).wait_send()
        pl.when(core == block)(keep_sum(p).wait)

        @pl.when(core != block)
        def _():
            remote(
                s2.at[rows(p)], s2.at[rows(p)], s3s.at[p, 0], s3r.at[p, 0, 0], sibling
            ).wait_send()

        for c in (0, 1):
            for s in (0, 1):
                here = (core == block) & (core == c) & (seq == s)

                @pl.when(jnp.logical_not(here))
                def _():
                    land = r3.at[c, s, rows(p)]
                    remote(land, land, s3s.at[p, 0], s3r.at[p, c, s], sibling).wait_recv()

        for c in (0, 1):
            at = STAGES[p][0]
            value = r3[c, 0, at : at + 48].astype(F32) + r3[c, 1, at : at + 48].astype(F32)
            if c == 0 and p < 3:
                for side in (0, 1):
                    h, k = (2 * p + side) // 3, (2 * p + side) % 3
                    cols = slice(k * D + h * HALF, k * D + (h + 1) * HALF)
                    gq[0, :, cols] = value[:, side * HALF : (side + 1) * HALF]
            elif c == 0 and p == 3:
                go[0] = value
            elif c == 0:
                gf[0, :, (p - 4) * D : (p - 3) * D] = value
            elif p < 2:
                gf[0, :, (p + 2) * D : (p + 3) * D] = value
            else:
                gp[0, (p - 2) * 48 : (p - 1) * 48] = value
        if p == 5:
            gsmall[...] = r3[0, 0, 288:304].astype(F32) + r3[0, 1, 288:304].astype(F32)

    count = len(STAGES)
    for t in range(count + 3):
        if t < count:
            swap_cores(t)
        if 0 <= t - 1 < count:
            over_lines(t - 1)
        if 0 <= t - 2 < count:
            over_places(t - 2)
        if 0 <= t - 3 < count:
            finish(t - 3)

    for j in (0, 1):
        for n in (0, 1):
            here, keep, give = outputs(j, n)
            pl.when(here)(keep.wait)
            pl.when(jnp.logical_not(here))(give.wait_send)

    for s in (0, 1):
        for n, dst in enumerate((out_a, out_b)):
            here = (core == seq) & (z == 2 * s + core)

            @pl.when(jnp.logical_not(here))
            def _():
                remote(
                    dst.at[s], dst.at[s], os.at[0], orr.at[s, n], sibling
                ).wait_recv()


def reduce(grads, result, ingrad):
    dma = pltpu.SemaphoreType.DMA
    n = len(STAGES)
    return pl.pallas_call(
        reduce_kernel,
        name="reduce_grads",
        out_shape=(
            jax.ShapeDtypeStruct((1, 48, 3 * D), F32),
            jax.ShapeDtypeStruct((1, 48, D), F32),
            jax.ShapeDtypeStruct((1, 48, 4 * D), F32),
            jax.ShapeDtypeStruct((1, 192, D), F32),
            jax.ShapeDtypeStruct((16, D), F32),
            jax.ShapeDtypeStruct((2, 256, D), BF),
            jax.ShapeDtypeStruct((2, 256, D), BF),
        ),
        in_specs=[ANY] + [VM] * 2,
        out_specs=(VM, VM, VM, VM, VM, VM, VM),
        scratch_shapes=[
            pltpu.VMEM((4, 4, HROWS, D), BF),
            pltpu.VMEM((4, 4, HROWS, D), BF),
            pltpu.VMEM((3, 4, HROWS, D), BF),
            pltpu.VMEM((3, HROWS, D), BF),
            pltpu.VMEM((4, HROWS, D), BF),
            pltpu.VMEM((HROWS, D), BF),
            pltpu.VMEM((2, 2, HROWS, D), BF),
            dma((n, 4)),
            dma((n, 4)),
            dma((n, 4)),
            dma((n, 4)),
            dma((n, 4)),
            dma((n, 4)),
            dma((n, 4)),
            dma((n, 4)),
            dma((n, 2, 2)),
            dma((4,)),
            dma((2, 2)),
            dma((2 + n,)),
        ],
        compiler_params=comm_params(5),
    )(grads, result, ingrad)


def halves_first(v, rows):
    return v.reshape(rows, 3, 2, HALF).transpose(0, 2, 1, 3).reshape(rows, 3 * D)


def thirds_first(v, rows):
    return v.reshape(rows, 2, 3, HALF).transpose(0, 2, 1, 3).reshape(rows, 3 * D)


def body(inputs, cotangent, w_qkv, w_out, w_fc, w_proj, gains, biases, fc_bias):
    small = jnp.concatenate([gains.reshape(96), biases.reshape(288), fc_bias.reshape(192)])
    small = jnp.pad(small[None], ((0, 15), (0, D - 576)))
    full, stream = gather(w_qkv, w_out, w_fc, w_proj, small, inputs, cotangent)
    full = full.reshape(16, ROWS, D)

    def lanes(v, rows):
        return v.reshape(16, rows, 48).transpose(1, 0, 2).reshape(rows, D)

    values = full[:, 288, :576].astype(F32)
    shifts = lanes(values[:, 96:384], 6)
    packed_shift = jnp.concatenate([shifts[1], jnp.zeros((D,), F32), shifts[2]])
    par = jnp.concatenate(
        [
            lanes(values[:, :96], 2),
            shifts,
            values[:, 384:].reshape(4, D),
            halves_first(packed_shift[None], 1).reshape(3, D),
            jnp.zeros((1, D), F32),
        ],
        0,
    )

    def attention(packed):
        heads = cross(packed, 1).reshape(L, 3 * HALF)
        mixed_heads, logs = attend(heads)
        return cross(mixed_heads.reshape(2, T, HALF), 2), (heads, mixed_heads, logs)

    def attention_back(kept, gmixed):
        heads, mixed_heads, logs = kept
        gheads = cross(gmixed, 2).reshape(L, HALF)
        gpacked = attend_back(heads, mixed_heads, gheads, logs)
        return cross(gpacked.reshape(2, T, 3 * HALF), 1)

    packed, _ = front(stream, full, par)
    mixed, _ = attention(packed)
    x, packed, normed = rear_front(stream, mixed, full, par)
    mixed, kept = attention(packed)
    result, gmixed, gmiddle, middle, normed2, pre, active = turn(x, mixed, stream, full, par)
    gp = attention_back(kept, gmixed)
    e, gmixed, gmiddle, rear_sums, mlow, gpre = back_back(
        gp, gmiddle, x, stream, middle, pre, full, par
    )
    gp = attention_back(kept, gmixed)
    grad, front_sums = front_back(gp, gmiddle, x, full, par)

    def shards(v, rows):
        return v.reshape(rows, 16, 48).transpose(1, 0, 2).reshape(16, rows * 48)

    packed_sums = thirds_first(front_sums[2:5].reshape(1, 3 * D), 1).reshape(3, D)
    small = jnp.concatenate(
        [
            shards(jnp.stack([front_sums[0], rear_sums[1]]), 2),
            shards(
                jnp.stack(
                    [
                        front_sums[1],
                        packed_sums[0],
                        packed_sums[2],
                        rear_sums[3],
                        rear_sums[2],
                        rear_sums[0],
                    ]
                ),
                6,
            ),
            rear_sums[4:8].reshape(16, 192),
        ],
        1,
    ).astype(BF)
    small = jnp.pad(small[:, None, :], ((0, 0), (0, 15), (0, D - 576)))
    grads = weight_grads(normed, gp, mixed, mlow, normed2, gpre, active, e, small)
    gq, go, gf, gd, total, section_out, in_grad = reduce(
        grads.reshape(4, 4, ROWS, D), result, grad
    )
    tail = total[0, :576]
    return (
        section_out[None],
        in_grad[None],
        gq,
        go,
        gf,
        gd,
        tail[:96].reshape(1, 2, 48),
        tail[96:384].reshape(1, 6, 48),
        tail[384:].reshape(1, 192),
    )


def solution(mesh):
    in_specs = (
        P("dp", "seq", None),
        P("dp", "seq", None),
        P("section", "dp", None),
        P("section", "dp", None),
        P("section", "dp", None),
        P("section", "dp", None),
        P("section", None, "dp"),
        P("section", None, "dp"),
        P("section", "dp"),
    )
    out_specs = (
        P("section", "dp", "seq", None),
        P("section", "dp", "seq", None),
        P("section", "dp", None),
        P("section", "dp", None),
        P("section", "dp", None),
        P("section", "dp", None),
        P("section", None, "dp"),
        P("section", None, "dp"),
        P("section", "dp"),
    )
    return jax.shard_map(body, mesh=mesh, in_specs=in_specs, out_specs=out_specs, check_vma=False)
```

```python
import functools
import math

import jax
import jax.numpy as jnp
from jax import lax
from jax.experimental import pallas as pl
from jax.experimental.pallas import tpu as pltpu
from jax.sharding import PartitionSpec as P

MESH = pl.DeviceIdType.MESH
BF = jnp.bfloat16
F32 = jnp.float32
D = 768
T = 512
L = 1024
HALF = 384
ROWS = 608
HROWS = ROWS // 2
EPS = 1e-05
FC_ROWS = (192, 240, 304, 352)
SCALE = 0.125
C2 = SCALE * math.log2(math.e)
VLIM = 60 * 1024 * 1024
ANY = pl.BlockSpec(memory_space=pl.ANY)
VM = pl.BlockSpec(memory_space=pltpu.VMEM)


def where_am_i():
    core = lax.axis_index("section")
    z = lax.axis_index("seq")
    dp = lax.axis_index("dp")
    return core, z, dp // 4, dp % 4


def greet(peers):
    barrier = pltpu.get_barrier_semaphore()
    for peer in peers:
        pl.semaphore_signal(barrier, inc=1, device_id=peer, device_id_type=MESH)
    pl.semaphore_wait(barrier, len(peers))


def remote(src, dst, send, recv, peer):
    return pltpu.make_async_remote_copy(
        src_ref=src, dst_ref=dst, send_sem=send, recv_sem=recv, device_id=peer, device_id_type=MESH
    )


def comm_params(ident):
    return pltpu.CompilerParams(
        collective_id=ident, has_side_effects=True, vmem_limit_bytes=VLIM
    )


PIECES = ((0, 96), (96, 96), (192, 112))


def gather_kernel(
    wq, wo, wf, wp, small, ins, cots, full, stream, shard, part, lsem, gs, gr, ssem, rsem, xs, xr
):
    core, z, y, x = where_am_i()
    block = z % 2
    sib = 1 - core
    dp = y * 4 + x
    sibling = (sib, z, dp)
    first = core == 0
    count = len(PIECES)

    def along(axis, step):
        if axis == 0:
            return (core, z, y * 4 + (x + step) % 4)
        return (core, z, ((y + step) % 4) * 4 + x)

    @pl.when(core == block)
    def _():
        for h in range(2):
            for k in range(3):
                at = h * 3 + k
                shard[(at // 2) * 48 : (at // 2 + 1) * 48, (at % 2) * HALF : (at % 2 + 1) * HALF] = (
                    wq[0, :, k * D + h * HALF : k * D + (h + 1) * HALF]
                )
        shard[144:192] = wo[0]
        for m in range(4):
            shard[FC_ROWS[m] : FC_ROWS[m] + 48] = wf[0, :, m * D : (m + 1) * D]
        shard[288:304] = small[...]
        shard[400:592] = wp[0]
        shard[592:608] = jnp.zeros((16, D), BF)

    peers = [sibling]
    for step in (1, 2, 3):
        peers += [along(0, step), along(1, step), (core, (z + step) % 4, dp)]
    greet(peers)

    def span(p, whose):
        at, rows = PIECES[p]
        return pl.ds(pl.multiple_of(whose * HROWS + at, 16), rows)

    def give(p):
        view = shard.at[span(p, sib)]
        return remote(view, view, gs.at[p], gr.at[p], sibling)

    @pl.when(core == block)
    def _():
        for p in range(count):
            give(p).start()

    quarter = pl.ds(pl.multiple_of((z % 2) * 256, 256), 256)
    sends_tokens = (z // 2) == core
    for step in (1, 2, 3):
        to = (z + step) % 4
        for source, parity in ((ins, 0), (cots, 1)):

            @pl.when(sends_tokens & (to % 2 == parity))
            def _():
                remote(
                    source.at[to // 2],
                    stream.at[quarter],
                    xs.at[step],
                    xr.at[z % 2],
                    (core, to, dp),
                ).start()

    for source, parity in ((ins, 0), (cots, 1)):

        @pl.when(sends_tokens & (z % 2 == parity))
        def _():
            pltpu.make_async_copy(source.at[z // 2], part, lsem.at[count]).start()

    def shard_at(p, axis, step, whose):
        rows = span(p, whose)
        if axis == 0:
            return full.at[y, (x + step) % 4, rows]
        return full.at[(y + step) % 4, x, rows]

    def line_at(p, axis, step, half, whose):
        rows = span(p, whose)
        if axis == 0:
            return full.at[pl.ds(2 * half, 2), (x + step) % 4, rows]
        return full.at[(y + step) % 4, pl.ds(2 * half, 2), rows]

    def rest(axis):
        cross = 1 - axis
        out = []

        def send(p, slot, src, dst, to):
            copy = remote(src, dst, ssem.at[p, slot], rsem.at[p, slot], to)
            copy.start()
            out.append(copy)

        def came(p, slot, land):
            remote(land, land, ssem.at[p, slot], rsem.at[p, slot], sibling).wait_recv()

        for p in range(count):

            @pl.when(core != block)
            def _():
                view = shard.at[span(p, core)]
                remote(view, view, gs.at[p], gr.at[p], sibling).wait_recv()

            view = shard.at[span(p, core)]
            land = shard_at(p, axis, 0, core)
            for k in (2, 1, 3):
                send(p, k, view, land, along(axis, k))
            send(p, 14, view, land, sibling)
            pltpu.make_async_copy(view, land, lsem.at[p]).start()
        for p in range(count):
            land = shard_at(p, axis, 0, core)
            pltpu.make_async_copy(shard.at[span(p, core)], land, lsem.at[p]).wait()
            for k in (1, 3, 2):
                came(p, k, shard_at(p, axis, 4 - k, core))
            for half in (0, 1):
                for slot, step in ((4, 1), (6, 3)):
                    view = line_at(p, cross, 0, half, core)
                    send(p, slot + half, view, view, along(cross, step))
            for k in (1, 3, 2):
                view = shard_at(p, axis, 4 - k, core)
                send(p, 14 + k, view, view, sibling)
        for p in range(count):
            for half, slot, step, to in ((0, 4, 3, 1), (1, 6, 1, 3), (1, 4, 3, 0), (0, 6, 1, 0)):
                land = line_at(p, cross, step, half, core)
                came(p, slot + half, land)
                if to:
                    send(p, 8 + half, land, land, along(cross, to))
                send(p, 14 + slot + half, land, land, sibling)
        for p in range(count):
            for half in (0, 1):
                land = line_at(p, cross, 2, half, core)
                came(p, 8 + half, land)
                send(p, 22 + half, land, land, sibling)
        for p in range(count):
            came(p, 14, shard_at(p, cross, 0, sib))
            for k in (1, 3, 2):
                came(p, 14 + k, shard_at(p, cross, 4 - k, sib))
            for half, slot, step in ((0, 4, 3), (1, 6, 1), (1, 4, 3), (0, 6, 1)):
                came(p, 14 + slot + half, line_at(p, axis, step, half, sib))
            for half in (0, 1):
                came(p, 22 + half, line_at(p, axis, 2, half, sib))
        for copy in out:
            copy.wait_send()

    @pl.when(first)
    def _():
        rest(0)

    @pl.when(jnp.logical_not(first))
    def _():
        rest(1)

    @pl.when(core == block)
    def _():
        for p in range(count):
            give(p).wait_send()

    @pl.when(sends_tokens)
    def _():
        pltpu.make_async_copy(ins.at[0], part, lsem.at[count]).wait()
        copy = pltpu.make_async_copy(part, stream.at[quarter], lsem.at[count])
        copy.start()
        for step in (1, 2, 3):
            remote(ins.at[0], stream.at[quarter], xs.at[step], xr.at[0], sibling).wait_send()
        copy.wait()

    for j in (0, 1):

        @pl.when(z != 2 * core + j)
        def _():
            land = stream.at[pl.ds(256 * j, 256)]
            remote(land, land, xs.at[0], xr.at[j], sibling).wait_recv()


def gather(wq, wo, wf, wp, small, ins, cots):
    dma = pltpu.SemaphoreType.DMA
    n = len(PIECES)
    return pl.pallas_call(
        gather_kernel,
        name="gather_weights",
        out_shape=(
            jax.ShapeDtypeStruct((4, 4, ROWS, D), BF),
            jax.ShapeDtypeStruct((T, D), BF),
        ),
        in_specs=[VM] * 5 + [ANY] * 2,
        out_specs=(ANY, ANY),
        scratch_shapes=[
            pltpu.VMEM((ROWS, D), BF),
            pltpu.VMEM((256, D), BF),
            dma((n + 1,)),
            dma((n,)),
            dma((n,)),
            dma((n, 24)),
            dma((n, 24)),
            dma((4,)),
            dma((2,)),
        ],
        compiler_params=comm_params(0),
    )(wq, wo, wf, wp, small, ins, cots)


def cross_kernel(src, dst, stage, lsem, ssem, rsem):
    core, z, y, x = where_am_i()
    sibling = (1 - core, z, y * 4 + x)
    local_in = pltpu.make_async_copy(src.at[core], stage, lsem)
    local_in.start()
    greet([sibling])
    out = remote(src.at[1 - core], dst.at[core], ssem, rsem, sibling)
    out.start()
    local_in.wait()
    local_out = pltpu.make_async_copy(stage, dst.at[core], lsem)
    local_out.start()
    local_out.wait()
    out.wait_send()
    remote(src.at[1 - core], dst.at[1 - core], ssem, rsem, sibling).wait_recv()


def cross(pieces, ident):
    return pl.pallas_call(
        cross_kernel,
        name="cross_cores",
        out_shape=jax.ShapeDtypeStruct(pieces.shape, pieces.dtype),
        in_specs=[ANY],
        out_specs=ANY,
        scratch_shapes=[pltpu.VMEM(pieces.shape[1:], pieces.dtype)]
        + [pltpu.SemaphoreType.DMA] * 3,
        compiler_params=comm_params(ident),
    )(pieces)


def dot(a, b):
    return jnp.dot(a, b, preferred_element_type=F32)


def dot_nt(a, b):
    return lax.dot_general(a, b, (((1,), (1,)), ((), ())), preferred_element_type=F32)


def dot_tn(a, b):
    return lax.dot_general(a, b, (((0,), (0,)), ((), ())), preferred_element_type=F32)


def normalized(v):
    centre = v - jnp.mean(v, axis=-1, keepdims=True)
    inv = lax.rsqrt(jnp.mean(centre * centre, axis=-1, keepdims=True) + EPS)
    return centre * inv, inv


def norm_back(grad, gain, unit, inv):
    g = grad * gain
    return inv * (
        g
        - jnp.mean(g, axis=-1, keepdims=True)
        - unit * jnp.mean(g * unit, axis=-1, keepdims=True)
    )


def matrix(ref, m):
    return ref[m].reshape(D, D)


class Fetch:
    def __init__(self, w, sems, parts):
        self.copies = []
        for at, (buffer, m, kind) in enumerate(parts):
            if kind is None:
                src = w.at[pl.ds(4 * m, 4), pl.ds(400, 192)]
            else:
                src = w.at[:, pl.ds(kind, 48)]
            self.copies.append(pltpu.make_async_copy(src, buffer.at[m], sems.at[at]))
        for copy in self.copies:
            copy.start()

    def need(self, at):
        self.copies[at].wait()


class Store:
    def __init__(self, sems):
        self.sems = sems
        self.copies = []

    def put(self, src, dst):
        copy = pltpu.make_async_copy(src, dst, self.sems.at[len(self.copies)])
        copy.start()
        self.copies.append(copy)

    def finish(self):
        for copy in self.copies:
            copy.wait()


def wide(*lead):
    return pltpu.VMEM((*lead, D), BF)


def local_params():
    return pltpu.CompilerParams(vmem_limit_bytes=VLIM)


TILES = (slice(0, 256), slice(256, 512))


def front_tile(at, need, x, wq, par, packed, normed_out):
    unit, _ = normalized(x[at].astype(F32))
    normed = (unit * par[0:1] + par[2:3]).astype(BF)
    normed_out[at] = normed
    need(0)
    a = (dot(normed, matrix(wq, 0)) + par[12:13]).astype(BF)
    packed[0, at, :D] = a
    need(1)
    b = (dot(normed, matrix(wq, 1)) + par[13:14]).astype(BF)
    packed[0, at, D:] = b[:, :HALF]
    packed[1, at, :HALF] = b[:, HALF:]
    need(2)
    c = (dot(normed, matrix(wq, 2)) + par[14:15]).astype(BF)
    packed[1, at, HALF:] = c


def nothing(at):
    pass


def front_kernel(x, w, par, packed, normed_out, wq, sems):
    fetch = Fetch(w, sems, QKV_PARTS(wq))
    for i, at in enumerate(TILES):
        front_tile(at, nothing if i else fetch.need, x, wq, par, packed, normed_out)


def QKV_PARTS(wq):
    return [(wq, m, 48 * m) for m in range(3)]


def front(x, w, par):
    return pl.pallas_call(
        front_kernel,
        name="front",
        out_shape=(
            jax.ShapeDtypeStruct((2, T, 3 * HALF), BF),
            jax.ShapeDtypeStruct((T, D), BF),
        ),
        in_specs=[VM, ANY, VM],
        out_specs=(VM, VM),
        scratch_shapes=[wide(3, 16, 48), pltpu.SemaphoreType.DMA((3,))],
        compiler_params=local_params(),
    )(x, w, par)


QB = 256


def head_masks(ref_value):
    lane = lax.broadcasted_iota(jnp.int32, ref_value.shape, 1)
    zero = jnp.zeros_like(ref_value)
    return (
        jnp.where(lane < 64, ref_value, zero),
        jnp.where(lane >= 64, ref_value, zero),
    )


def causal(rows, cols, offset):
    row = lax.broadcasted_iota(jnp.int32, (rows, cols), 0) + offset
    return lax.broadcasted_iota(jnp.int32, (rows, cols), 1) <= row


def attend_kernel(q_ref, k_ref, v_ref, mixed, logs):
    for i in range(L // QB):
        at = slice(i * QB, (i + 1) * QB)
        stop = (i + 1) * QB
        keys = k_ref[:stop]
        queries = head_masks(q_ref[at])
        values = head_masks(v_ref[:stop])
        keep = causal(QB, stop, i * QB)
        total = None
        saved = []
        for h in range(2):
            s = jnp.where(keep, dot_nt(queries[h], keys), -1e30)
            peak = jnp.max(s, axis=-1, keepdims=True)
            p = jnp.exp2((s - peak) * C2)
            norm = jnp.sum(p, axis=-1, keepdims=True)
            o = dot(p.astype(BF), values[h]) * (1.0 / norm)
            total = o if total is None else total + o
            saved.append(peak * C2 + jnp.log2(norm))
        mixed[at] = total.astype(BF)
        lane = lax.broadcasted_iota(jnp.int32, (QB, 128), 1)
        logs[0, at] = jnp.where(lane < 64, saved[0], saved[1])


def attend(heads):
    def col(k):
        return pl.BlockSpec((L, 128), lambda p: (0, p + 3 * k))

    return pl.pallas_call(
        attend_kernel,
        name="attend",
        grid=(3,),
        out_shape=(
            jax.ShapeDtypeStruct((L, HALF), BF),
            jax.ShapeDtypeStruct((3, L, 128), F32),
        ),
        in_specs=[col(0), col(1), col(2)],
        out_specs=(col(0), pl.BlockSpec((1, L, 128), lambda p: (p, 0, 0))),
        compiler_params=local_params(),
    )(heads, heads, heads)


def attend_back_pair(get, put, logs_at, dk, dv):
    dk[...] = jnp.zeros_like(dk)
    dv[...] = jnp.zeros_like(dv)
    for i in range(L // QB):
        at = slice(i * QB, (i + 1) * QB)
        stop = (i + 1) * QB
        keys = get("k", slice(0, stop))
        values = get("v", slice(0, stop))
        keys_of = head_masks(keys)
        queries = head_masks(get("q", at))
        top = get("do", at)
        tops = head_masks(top)
        keep = causal(QB, stop, i * QB)
        inner = head_masks(top.astype(F32) * get("o", at).astype(F32))
        dq = None
        for h in range(2):
            s = dot_nt(queries[h], keys)
            p = jnp.where(keep, jnp.exp2(s * C2 - logs_at(at, h)), 0.0)
            gw = dot_nt(tops[h], values)
            delta = jnp.sum(inner[h], axis=-1, keepdims=True)
            ds = (p * (gw - delta)).astype(BF)
            part = dot(ds, keys_of[h])
            dq = part if dq is None else dq + part
            dk[:stop] += dot_tn(ds, queries[h])
            dv[:stop] += dot_tn(p.astype(BF), tops[h])
        put("q", at, (dq * SCALE).astype(BF))
    put("k", slice(0, L), (dk[...] * SCALE).astype(BF))
    put("v", slice(0, L), dv[...].astype(BF))


def part_columns(pair):
    def columns(name):
        return pl.ds(pl.multiple_of("qkv".index(name) * HALF + pair * 128, 128), 128)

    return columns


def attend_back_kernel(q_ref, k_ref, v_ref, o_ref, do_ref, logs, out, dk, dv):
    refs = {"q": q_ref, "k": k_ref, "v": v_ref, "o": o_ref, "do": do_ref}
    columns = part_columns(pl.program_id(0))

    def get(name, rows):
        return refs[name][rows]

    def put(name, rows, value):
        out[rows, columns(name)] = value

    attend_back_pair(
        get, put, lambda at, h: logs[0, at, 64 * h : 64 * h + 1], dk, dv
    )


def attend_back(heads, mixed, grad_mixed, logs):
    def col(k):
        return pl.BlockSpec((L, 128), lambda p: (0, p + 3 * k))

    return pl.pallas_call(
        attend_back_kernel,
        name="attend_back",
        grid=(3,),
        out_shape=jax.ShapeDtypeStruct((L, 3 * HALF), BF),
        in_specs=[
            col(0),
            col(1),
            col(2),
            col(0),
            col(0),
            pl.BlockSpec((1, L, 128), lambda p: (p, 0, 0)),
        ],
        out_specs=pl.BlockSpec((L, 3 * HALF), lambda p: (0, 0)),
        scratch_shapes=[pltpu.VMEM((L, 128), F32)] * 2,
        compiler_params=local_params(),
    )(heads, heads, heads, mixed, grad_mixed, logs)


REAR_SCRATCH = [
    wide(1, 16, 48),
    wide(4, 16, 48),
    wide(4, 4, 192),
    pltpu.SemaphoreType.DMA((9,)),
]


def gelu(v):
    return 0.5 * v * (1.0 + jnp.tanh(0.79788456 * (v + 0.044715 * v * v * v)))


def gelu_slope(v):
    square = v * v
    t = jnp.tanh(0.79788456 * v * (1.0 + 0.044715 * square))
    return 0.5 * (1.0 + t) + 0.5 * v * (1.0 - t * t) * 0.79788456 * (
        1.0 + 3 * 0.044715 * square
    )


def forward_parts(wo, wf, wp):
    parts = [(wo, 0, 144)]
    for m in range(4):
        parts += [(wf, m, FC_ROWS[m]), (wp, m, None)]
    return parts


def backward_parts(wo, wf, wp):
    parts = []
    for m in range(4):
        parts += [(wp, m, None), (wf, m, FC_ROWS[m])]
    return parts + [(wo, 0, 144)]


def rear_tile(at, need, x, mixed, wo, wf, wp, par, result, kept, store):
    mix = jnp.concatenate([mixed[0, at], mixed[1, at]], axis=1)
    need(0)
    middle = x[at].astype(F32) + (dot(mix, matrix(wo, 0)) + par[5:6])
    unit, _ = normalized(middle)
    normed = (unit * par[1:2] + par[6:7]).astype(BF)
    if kept:
        kept[0][at] = middle
        kept[1][at] = normed
        store(0, at, None)
        store(1, at, None)
    total = middle + par[7:8]
    for m in range(4):
        need(1 + 2 * m)
        pre = dot(normed, matrix(wf, m)) + par[8 + m : 9 + m]
        active = gelu(pre).astype(BF)
        if kept:
            cols = slice(m * D, (m + 1) * D)
            kept[2][at, cols] = pre.astype(BF)
            kept[3][at, cols] = active
            store(2, at, cols)
            store(3, at, cols)
        need(2 + 2 * m)
        total = total + dot(active, matrix(wp, m))
    result[at] = total.astype(BF)


def column_sum(v):
    return jnp.sum(v, axis=0, keepdims=True)


def adder(sums, i):
    def add(row, v):
        if i:
            sums[row : row + 1] += column_sum(v)
        else:
            sums[row : row + 1] = column_sum(v)

    return add


def rear_back_tile(at, need, e, middle, pre, wo, wf, wp, par, gmixed, gmiddle, full):
    if full:
        add, mlow, gpre, store = full
    top = e[at]
    gnorm = None
    for m in range(4):
        cols = slice(m * D, (m + 1) * D)
        need(2 * m)
        gact = dot_nt(top, matrix(wp, m))
        low = (gact * gelu_slope(pre[at, cols].astype(F32))).astype(BF)
        if full:
            gpre[at, cols] = low
            store(0, at, cols)
            add(4 + m, low.astype(F32))
        need(2 * m + 1)
        part = dot_nt(low, matrix(wf, m))
        gnorm = part if gnorm is None else gnorm + part
    unit, inv = normalized(middle[at])
    top_wide = top.astype(F32)
    gmid = top_wide + norm_back(gnorm, par[1:2], unit, inv)
    gmiddle[at] = gmid
    low = gmid.astype(BF)
    if full:
        add(0, top_wide)
        add(1, gnorm * unit)
        add(2, gnorm)
        add(3, gmid)
        mlow[at] = low
        store(1, at, None)
    need(8)
    gm = dot_nt(low, matrix(wo, 0)).astype(BF)
    gmixed[0, at] = gm[:, :HALF]
    gmixed[1, at] = gm[:, HALF:]


def front_back_tile(at, need, gp, gmiddle, x, wq, par, grad, add):
    gnorm = None
    for m, piece in enumerate(packed_pieces(gp, at)):
        if add:
            add(2 + m, piece.astype(F32))
        need(m)
        part = dot_nt(piece, matrix(wq, m))
        gnorm = part if gnorm is None else gnorm + part
    unit, inv = normalized(x[at].astype(F32))
    if add:
        add(0, gnorm * unit)
        add(1, gnorm)
    grad[at] = (gmiddle[at] + norm_back(gnorm, par[0:1], unit, inv)).astype(BF)


def partner_of():
    core, z, y, x = where_am_i()
    return z % 2, (core, z + 1 - 2 * (z % 2), y * 4 + x)


def rear_front_kernel(
    x, mixed, w, par, x2, packed, normed, wo, wf, wp, sems, wq, qsems, res, ssem, rsem
):
    block, partner = partner_of()
    fetch = Fetch(w, sems, forward_parts(wo, wf, wp))
    fetch_q = Fetch(w, qsems, QKV_PARTS(wq))
    greet([partner])

    def hand(i):
        rows = pl.ds(256 * i, 256)
        return remote(res.at[rows], x2.at[rows], ssem.at[i], rsem.at[i], partner)

    @pl.when(block == 0)
    def _():
        for i, at in enumerate(TILES):
            rear_tile(
                at, nothing if i else fetch.need, x, mixed, wo, wf, wp, par, res, None, None
            )
            hand(i).start()
        x2[...] = x[...]

    @pl.when(block == 1)
    def _():
        for k in range(9):
            fetch.need(k)

    for k in range(3):
        fetch_q.need(k)
    for i, at in enumerate(TILES):
        pl.when(block == 1)(hand(i).wait_recv)
        front_tile(at, nothing, x2, wq, par, packed, normed)

    @pl.when(block == 0)
    def _():
        for i in range(2):
            hand(i).wait_send()


def rear_front(x, mixed, w, par):
    dma = pltpu.SemaphoreType.DMA
    return pl.pallas_call(
        rear_front_kernel,
        name="rear_hand_front",
        out_shape=(
            jax.ShapeDtypeStruct((T, D), BF),
            jax.ShapeDtypeStruct((2, T, 3 * HALF), BF),
            jax.ShapeDtypeStruct((T, D), BF),
        ),
        in_specs=[VM, VM, ANY, VM],
        out_specs=(VM, VM, VM),
        scratch_shapes=REAR_SCRATCH
        + [wide(3, 16, 48), dma((3,)), wide(T), dma((2,)), dma((2,))],
        compiler_params=comm_params(3),
    )(x, mixed, w, par)


def turn_kernel(
    x, mixed, e, w, par, result, gmixed, gmiddle, middle_out, normed_out, pre_out, active_out,
    wo, wf, wp, sems, middle, normed, pre, active, osems,
):
    fetch = Fetch(w, sems, forward_parts(wo, wf, wp))
    store = Store(osems)
    kept = (middle, normed, pre, active)
    outs = (middle_out, normed_out, pre_out, active_out)

    def put(n, at, cols):
        rows = pl.ds(at.start, at.stop - at.start)
        if cols is None:
            store.put(kept[n].at[rows], outs[n].at[rows])
        else:
            lanes = pl.ds(cols.start, D)
            store.put(kept[n].at[rows, lanes], outs[n].at[rows, lanes])

    for i, at in enumerate(TILES):
        rear_tile(
            at, nothing if i else fetch.need, x, mixed, wo, wf, wp, par, result, kept, put
        )
    for at in TILES:
        rear_back_tile(at, nothing, e, middle, pre, wo, wf, wp, par, gmixed, gmiddle, None)
    store.finish()


def turn(x, mixed, e, w, par):
    kept = [((T, D), F32), ((T, D), BF), ((T, 4 * D), BF), ((T, 4 * D), BF)]
    outs = [((T, D), BF), ((2, T, HALF), BF), ((T, D), F32)] + kept
    return pl.pallas_call(
        turn_kernel,
        name="turn",
        out_shape=tuple(jax.ShapeDtypeStruct(s, t) for s, t in outs),
        in_specs=[VM, VM, VM, ANY, VM],
        out_specs=(VM, VM, VM, ANY, ANY, ANY, ANY),
        scratch_shapes=REAR_SCRATCH
        + [pltpu.VMEM(s, t) for s, t in kept]
        + [pltpu.SemaphoreType.DMA((20,))],
        compiler_params=local_params(),
    )(x, mixed, e, w, par)


def back_back_kernel(
    gp, gmid_in, x, stream, middle, pre_in, w, par,
    e, gmixed, gmiddle, sums, mlow_out, gpre_out,
    wo, wf, wp, sems, wq, qsems, res, ssem, rsem, pre, mlow, gpre, psem, osems,
):
    block, partner = partner_of()
    fetch_q = Fetch(w, qsems, QKV_PARTS(wq))
    fetch = Fetch(w, sems, backward_parts(wo, wf, wp))
    load = pltpu.make_async_copy(pre_in, pre, psem)
    load.start()
    greet([partner])

    def hand(i):
        rows = pl.ds(256 * i, 256)
        return remote(res.at[rows], e.at[rows], ssem.at[i], rsem.at[i], partner)

    for k in range(3):
        fetch_q.need(k)

    @pl.when(block == 1)
    def _():
        for i, at in enumerate(TILES):
            front_back_tile(at, nothing, gp, gmid_in, x, wq, par, res, None)
            hand(i).start()
        e[...] = stream[...]

    for k in range(9):
        fetch.need(k)
    load.wait()
    store = Store(osems)

    def put(n, at, cols):
        rows = pl.ds(at.start, at.stop - at.start)
        if cols is None:
            store.put(mlow.at[rows], mlow_out.at[rows])
        else:
            lanes = pl.ds(cols.start, D)
            store.put(gpre.at[rows, lanes], gpre_out.at[rows, lanes])

    for i, at in enumerate(TILES):
        pl.when(block == 0)(hand(i).wait_recv)
        rear_back_tile(
            at, nothing, e, middle, pre, wo, wf, wp, par, gmixed, gmiddle,
            (adder(sums, i), mlow, gpre, put),
        )

    @pl.when(block == 1)
    def _():
        for i in range(2):
            hand(i).wait_send()

    store.finish()


def back_back(gp, gmid, x, stream, middle, pre, w, par):
    dma = pltpu.SemaphoreType.DMA
    return pl.pallas_call(
        back_back_kernel,
        name="front_back_hand_rear_back",
        out_shape=(
            jax.ShapeDtypeStruct((T, D), BF),
            jax.ShapeDtypeStruct((2, T, HALF), BF),
            jax.ShapeDtypeStruct((T, D), F32),
            jax.ShapeDtypeStruct((8, D), F32),
            jax.ShapeDtypeStruct((T, D), BF),
            jax.ShapeDtypeStruct((T, 4 * D), BF),
        ),
        in_specs=[VM, VM, VM, VM, VM, ANY, ANY, VM],
        out_specs=(VM, VM, VM, VM, ANY, ANY),
        scratch_shapes=REAR_SCRATCH
        + [wide(3, 16, 48), dma((3,)), wide(T), dma((2,)), dma((2,))]
        + [pltpu.VMEM((T, 4 * D), BF), wide(T), pltpu.VMEM((T, 4 * D), BF)]
        + [dma, dma((10,))],
        compiler_params=comm_params(4),
    )(gp, gmid, x, stream, middle, pre, w, par)


def packed_pieces(gp, at=slice(None)):
    return (
        gp[0, at, :D],
        jnp.concatenate([gp[0, at, D:], gp[1, at, :HALF]], axis=1),
        gp[1, at, HALF:],
    )


def rows_of(stage):
    return pl.ds(*stage)


class Reducer:
    def __init__(self, stages, buffers, sems):
        self.stages = stages
        self.own, self.r0, self.r1, self.r2, self.s1, self.s2, self.r3 = buffers
        self.s1s, self.s1r, self.s2s, self.s2r, self.s3s, self.s3r, self.ks = sems
        self.core, self.z, y, x = where_am_i()
        self.x, self.y = x, y
        self.dp = y * 4 + x
        self.block = self.z % 2
        self.seq = self.z // 2
        self.first = self.core == 0
        self.sibling = (1 - self.core, self.z, self.dp)
        self.line = jnp.where(self.first, y, x)
        self.place = jnp.where(self.first, x, y)

    def on_line(self, step):
        to = (self.line + step) % 4
        return (self.core, self.z, jnp.where(self.first, to * 4 + self.x, self.y * 4 + to))

    def on_place(self, step):
        to = (self.place + step) % 4
        return (self.core, self.z, jnp.where(self.first, self.y * 4 + to, to * 4 + self.x))

    def peers(self):
        found = [self.sibling]
        for step in (1, 2, 3):
            found += [self.on_line(step), self.on_place(step)]
            for k in (0, 1):
                found.append((k, (self.z + step) % 4, self.dp))
        return found

    def over_cores(self, p):
        own, r0, rows = self.own, self.r0, rows_of(self.stages[p])

        @pl.loop(0, 16)
        def _(i):
            a = own[i // 4, i % 4, rows].astype(F32)
            b = r0[i // 4, i % 4, rows].astype(F32)
            own[i // 4, i % 4, rows] = (a + b).astype(BF)

        for step in (2, 1, 3):
            remote(
                own.at[(self.line + step) % 4, :, rows],
                self.r1.at[step - 1, :, rows],
                self.s1s.at[p, step],
                self.s1r.at[p, step],
                self.on_line(step),
            ).start()

    def over_lines(self, p):
        own, r1, s1, rows = self.own, self.r1, self.s1, rows_of(self.stages[p])
        line = self.line
        for step in (1, 3, 2):
            remote(
                own.at[0, :, rows],
                r1.at[step - 1, :, rows],
                self.s1s.at[p, step],
                self.s1r.at[p, step],
                self.sibling,
            ).wait()

        @pl.loop(0, 4)
        def _(i):
            s1[i, rows] = (
                (own[line, i, rows].astype(F32) + r1[0, i, rows].astype(F32))
                + (r1[1, i, rows].astype(F32) + r1[2, i, rows].astype(F32))
            ).astype(BF)

        for step in (2, 1, 3):
            remote(
                s1.at[(self.place + step) % 4, rows],
                self.r2.at[step - 1, rows],
                self.s2s.at[p, step],
                self.s2r.at[p, step],
                self.on_place(step),
            ).start()

    def along_z(self, p, step):
        rows = rows_of(self.stages[p])
        return remote(
            self.s2.at[rows],
            self.r3.at[self.core, self.seq, rows],
            self.s3s.at[p, step],
            self.s3r.at[p, self.core, self.seq],
            (self.block, (self.z + step) % 4, self.dp),
        )

    def to_sibling(self, p):
        rows = rows_of(self.stages[p])
        return remote(
            self.s2.at[rows],
            self.r3.at[self.core, self.seq, rows],
            self.s3s.at[p, 0],
            self.s3r.at[p, self.core, self.seq],
            self.sibling,
        )

    def keep_sum(self, p):
        rows = rows_of(self.stages[p])
        return pltpu.make_async_copy(
            self.s2.at[rows], self.r3.at[self.core, self.seq, rows], self.ks.at[p]
        )

    def over_places(self, p):
        s1, r2, rows = self.s1, self.r2, rows_of(self.stages[p])
        for step in (1, 3, 2):
            remote(
                s1.at[0, rows],
                r2.at[step - 1, rows],
                self.s2s.at[p, step],
                self.s2r.at[p, step],
                self.sibling,
            ).wait()
        self.s2[rows] = (
            (s1[self.place, rows].astype(F32) + r2[0, rows].astype(F32))
            + (r2[1, rows].astype(F32) + r2[2, rows].astype(F32))
        ).astype(BF)
        for step in (2, 1, 3):
            self.along_z(p, step).start()
        pl.when(self.core == self.block)(self.keep_sum(p).start)
        pl.when(self.core != self.block)(self.to_sibling(p).start)

    def finish(self, p):
        for step in (1, 2, 3):
            self.along_z(p, step).wait_send()
        pl.when(self.core == self.block)(self.keep_sum(p).wait)
        pl.when(self.core != self.block)(self.to_sibling(p).wait_send)
        rows = rows_of(self.stages[p])
        for c in (0, 1):
            for s in (0, 1):
                here = (self.core == self.block) & (self.core == c) & (self.seq == s)
                land = self.r3.at[c, s, rows]

                @pl.when(jnp.logical_not(here))
                def _():
                    remote(
                        land, land, self.s3s.at[p, 0], self.s3r.at[p, c, s], self.sibling
                    ).wait_recv()

    def total(self, c, p):
        rows = rows_of(self.stages[p])
        return self.r3[c, 0, rows].astype(F32) + self.r3[c, 1, rows].astype(F32)


def reducer_buffers(rows):
    return [
        pltpu.VMEM((4, 4, rows, D), BF),
        pltpu.VMEM((4, 4, rows, D), BF),
        pltpu.VMEM((3, 4, rows, D), BF),
        pltpu.VMEM((3, rows, D), BF),
        pltpu.VMEM((4, rows, D), BF),
        pltpu.VMEM((rows, D), BF),
        pltpu.VMEM((2, 2, rows, D), BF),
    ]


def reducer_sems(count):
    dma = pltpu.SemaphoreType.DMA
    return [dma((count, 4))] * 5 + [dma((count, 2, 2)), dma((count,))]


REAR_STAGES = ((0, 48), (48, 48), (96, 48), (144, 48))
REAR_ROWS = 192


def tail_kernel(*refs):
    sources, refs = refs[:12], refs[12:]
    gmixed, result, w, par, rear_sums = refs[:5]
    gf, gd, gq, go, gsmall, out_a, out_b = refs[5:12]
    loaded, refs = refs[12:24], refs[24:]
    gheads, gp, wq, snd, grad, fsums, dk, dv = refs[:8]
    buffers, refs = refs[8:15], refs[15:]
    late_buffers, refs = buffers[:2] + refs[:5], refs[5:]
    sems, refs = refs[:7], refs[7:]
    late_sems, refs = refs[:7], refs[7:]
    lsem, qsems, xsem, s0s, s0r, l0s, l0r, os, orr, ol = refs
    e, active, normed2, gpre, heads, omix, logs, mixed, mlow, normed, gmid, x = loaded
    own, r0 = buffers[0], buffers[1]

    copies = [
        pltpu.make_async_copy(src, dst, lsem.at[k])
        for k, (src, dst) in enumerate(zip(sources, loaded))
    ]
    for copy in copies:
        copy.start()
    fetch = Fetch(w, qsems, QKV_PARTS(wq))
    reducer = Reducer(REAR_STAGES, buffers, sems)
    late = Reducer(FRONT_STAGES, late_buffers, late_sems)
    core, sibling, first = reducer.core, reducer.sibling, reducer.first
    z, dp, block, seq = reducer.z, reducer.dp, reducer.block, reducer.seq
    greet(reducer.peers())

    def outputs(j, n):
        src, dst = ((result, out_a), (grad, out_b))[n]
        here = (core == block) & (z == 2 * core + j)
        view = src.at[pl.ds(256 * j, 256)]
        keep = pltpu.make_async_copy(view, dst.at[seq], ol.at[n])
        give = remote(
            view, dst.at[seq], os.at[2 * j + n], orr.at[seq, n], (block, 2 * core + j, dp)
        )
        return here, keep, give

    def send_output(j, n):
        here, keep, send = outputs(j, n)
        pl.when(here)(keep.start)
        pl.when(jnp.logical_not(here))(send.start)

    for j in (0, 1):
        send_output(j, 0)

    top_out = remote(gmixed.at[1 - core], gheads.at[core], xsem.at[0], xsem.at[1], sibling)
    top_in = remote(gmixed.at[0], gheads.at[1 - core], xsem.at[0], xsem.at[1], sibling)
    top_own = pltpu.make_async_copy(gmixed.at[core], gheads.at[core], xsem.at[2])
    top_out.start()
    top_own.start()

    def hidden_out(m):
        value = dot_tn(active[:, m * D : (m + 1) * D], e[...])
        return value.astype(BF).reshape(4, 192, D)

    def hidden_in(m):
        value = dot_tn(normed2[...], gpre[:, m * D : (m + 1) * D])
        return value.astype(BF).reshape(4, 4, 48, D)

    def give_out(m):
        return remote(snd.at[m], r0.at[:, m], s0s.at[m], s0r.at[m], sibling)

    def give_in(m):
        rows = pl.ds(m * 48, 48)
        return remote(
            snd.at[:, :, rows], r0.at[:, :, rows], s0s.at[m], s0r.at[m], sibling
        )

    for k in range(4):
        copies[k].wait()

    @pl.when(first)
    def _():
        for m in range(4):
            snd[m] = hidden_out(m)
            give_out(m).start()
        for m in range(4):
            own[:, :, m * 48 : (m + 1) * 48] = hidden_in(m)
            give_in(m).wait_recv()
            reducer.over_cores(m)

    @pl.when(jnp.logical_not(first))
    def _():
        for m in range(4):
            snd[:, :, m * 48 : (m + 1) * 48] = hidden_in(m)
            give_in(m).start()
        for m in range(4):
            own[:, m] = hidden_out(m)
        for m in range(4):
            give_out(m).wait_recv()
        for m in range(4):
            reducer.over_cores(m)

    top_own.wait()
    top_in.wait_recv()
    for k in range(4, 12):
        copies[k].wait()

    @pl.loop(0, 3)
    def _(pair):
        columns = part_columns(pair)
        narrow = pl.ds(pl.multiple_of(pair * 128, 128), 128)

        def get(name, rows):
            if name == "o":
                return omix[rows, narrow]
            if name == "do":
                half, start = rows.start // T, rows.start % T
                return gheads[half, start : start + QB, narrow]
            return heads[rows, columns(name)]

        def put(name, rows, value):
            heads[rows, columns(name)] = value

        attend_back_pair(
            get, put, lambda at, h: logs[pair, at, 64 * h : 64 * h + 1], dk, dv
        )

        @pl.when(pair == 1)
        def _():
            reducer.over_lines(0)

    def half_rows(c):
        return heads.at[pl.ds(pl.multiple_of(c * T, T), T)]

    gp_out = remote(half_rows(1 - core), gp.at[core], xsem.at[3], xsem.at[4], sibling)
    gp_in = remote(half_rows(core), gp.at[1 - core], xsem.at[3], xsem.at[4], sibling)
    gp_own = pltpu.make_async_copy(half_rows(core), gp.at[core], xsem.at[5])
    gp_out.start()
    gp_own.start()
    reducer.over_lines(1)
    reducer.over_places(0)
    for k in range(3):
        fetch.need(k)
    gp_own.wait()
    gp_in.wait_recv()

    for i, at in enumerate(TILES):
        front_back_tile(at, nothing, gp, gmid, x, wq, par, grad, adder(fsums, i))
        send_output(i, 1)
        reducer.over_lines(2 + i)
        reducer.over_places(1 + i)

    @pl.when(first)
    def _():
        for m in range(4):
            give_out(m).wait_send()

    @pl.when(jnp.logical_not(first))
    def _():
        for m in range(4):
            give_in(m).wait_send()

    zero = jnp.zeros((1, D), F32)
    small = jnp.concatenate(
        [
            fsums[0:1],
            rear_sums[1:2],
            fsums[1:2],
            zero,
            zero,
            rear_sums[3:4],
            rear_sums[2:3],
            rear_sums[0:1],
            rear_sums[4:8],
            fsums[2:5],
            zero,
        ],
        0,
    ).astype(BF)

    def packed_grad(m):
        piece = packed_pieces(gp)[m]
        return dot_tn(normed[...], piece).astype(BF).reshape(4, 4, 48, D)

    def out_grad():
        mix = jnp.concatenate([mixed[0], mixed[1]], axis=1)
        return dot_tn(mix, mlow[...]).astype(BF).reshape(4, 4, 48, D)

    def give_late(p, k):
        rows = rows_of(FRONT_STAGES[p])
        return rows, snd.at[k, :, rows], l0s.at[p, k], l0r.at[p, k]

    def give_late_0(p, k):
        rows, src, ss, rs = give_late(p, k)
        return remote(src, r0.at[:, k, rows], ss, rs, sibling)

    def give_late_1(p, k):
        rows, src, ss, rs = give_late(p, k)
        return remote(src, r0.at[k, :, rows], ss, rs, sibling)

    def fill(dst, swapped, at, value):
        for k in range(4):
            if swapped:
                dst[:, k, at : at + value.shape[2]] = value[k]
            else:
                dst[k, :, at : at + value.shape[2]] = value[k]

    smalls = jnp.broadcast_to(small[None, None], (4, 4, 16, D))

    @pl.when(first)
    def _():
        fill(snd, False, 0, packed_grad(2))
        for k in range(4):
            give_late_0(0, k).start()
        fill(snd, False, 48, out_grad())
        fill(snd, False, 96, jnp.zeros((4, 4, 16, D), BF))
        for k in range(4):
            give_late_0(1, k).start()
        fill(own, False, 0, packed_grad(0))
        fill(own, False, 48, packed_grad(1))
        fill(own, False, 96, smalls)

    @pl.when(jnp.logical_not(first))
    def _():
        fill(snd, False, 0, packed_grad(0))
        for k in range(4):
            give_late_1(0, k).start()
        fill(snd, False, 48, packed_grad(1))
        fill(snd, False, 96, smalls)
        for k in range(4):
            give_late_1(1, k).start()
        fill(own, True, 0, packed_grad(2))
        fill(own, True, 48, out_grad())
        fill(own, True, 96, jnp.zeros((4, 4, 16, D), BF))

    for p in range(2):
        for k in range(4):
            give_late_1(p, k).wait()
        late.over_cores(p)
    reducer.over_places(3)
    for m in range(4):
        reducer.finish(m)
        gf[0, :, m * D : (m + 1) * D] = reducer.total(0, m)
        gd[0, m * 48 : (m + 1) * 48] = reducer.total(1, m)
        if m == 1:
            late.over_lines(0)
    late.over_lines(1)
    for p in range(2):
        late.over_places(p)
    for p in range(2):
        late.finish(p)

    def put(m, value):
        for side in (0, 1):
            h, k = (2 * m + side) // 3, (2 * m + side) % 3
            gq[0, :, k * D + h * HALF : k * D + (h + 1) * HALF] = value[
                :, side * HALF : (side + 1) * HALF
            ]

    put(0, late.total(0, 0))
    put(2, late.total(1, 0))
    both = late.total(0, 1)
    put(1, both[:48])
    go[0] = late.total(1, 1)[:48]
    small = both[48:]
    gsmall[...] = small
    gsmall[3:4, :HALF] = small[12:13, :HALF]
    gsmall[3:4, HALF:] = small[13:14, HALF:]
    gsmall[4:5, :HALF] = small[13:14, :HALF]
    gsmall[4:5, HALF:] = small[14:15, HALF:]

    top_out.wait_send()
    gp_out.wait_send()
    for j in (0, 1):
        for n in (0, 1):
            here, keep, send = outputs(j, n)
            pl.when(here)(keep.wait)
            pl.when(jnp.logical_not(here))(send.wait_send)

    for s in (0, 1):
        for n, dst in enumerate((out_a, out_b)):
            here = (core == seq) & (z == 2 * s + core)

            @pl.when(jnp.logical_not(here))
            def _():
                remote(dst.at[s], dst.at[s], os.at[0], orr.at[s, n], sibling).wait_recv()


def tail(loads, gmixed, result, w, par, rear_sums):
    dma = pltpu.SemaphoreType.DMA
    return pl.pallas_call(
        tail_kernel,
        name="tail",
        out_shape=(
            jax.ShapeDtypeStruct((1, 48, 4 * D), F32),
            jax.ShapeDtypeStruct((1, 192, D), F32),
            jax.ShapeDtypeStruct((1, 48, 3 * D), F32),
            jax.ShapeDtypeStruct((1, 48, D), F32),
            jax.ShapeDtypeStruct((16, D), F32),
            jax.ShapeDtypeStruct((2, 256, D), BF),
            jax.ShapeDtypeStruct((2, 256, D), BF),
        ),
        in_specs=[ANY] * 15 + [VM] * 2,
        out_specs=(VM, VM, VM, VM, VM, ANY, ANY),
        scratch_shapes=[pltpu.VMEM(v.shape, v.dtype) for v in loads]
        + [
            pltpu.VMEM((2, T, HALF), BF),
            pltpu.VMEM((2, T, 3 * HALF), BF),
            wide(3, 16, 48),
            wide(4, 4, REAR_ROWS),
            wide(T),
            pltpu.VMEM((8, D), F32),
            pltpu.VMEM((L, 128), F32),
            pltpu.VMEM((L, 128), F32),
        ]
        + reducer_buffers(REAR_ROWS)
        + reducer_buffers(FRONT_ROWS)[2:]
        + reducer_sems(4)
        + reducer_sems(2)
        + [dma((12,)), dma((3,)), dma((6,)), dma((4,)), dma((4,))]
        + [dma((2, 4)), dma((2, 4)), dma((4,)), dma((2, 2)), dma((2,))],
        compiler_params=comm_params(5),
    )(*loads, gmixed, result, w, par, rear_sums)


FRONT_STAGES = ((0, 48), (48, 64))
FRONT_ROWS = 112


def halves_first(v, rows):
    return v.reshape(rows, 3, 2, HALF).transpose(0, 2, 1, 3).reshape(rows, 3 * D)


def body(inputs, cotangent, w_qkv, w_out, w_fc, w_proj, gains, biases, fc_bias):
    small = jnp.concatenate([gains.reshape(96), biases.reshape(288), fc_bias.reshape(192)])
    small = jnp.pad(small[None], ((0, 15), (0, D - 576)))
    full, stream = gather(w_qkv, w_out, w_fc, w_proj, small, inputs, cotangent)
    full = full.reshape(16, ROWS, D)

    def lanes(v, rows):
        return v.reshape(16, rows, 48).transpose(1, 0, 2).reshape(rows, D)

    values = full[:, 288, :576].astype(F32)
    shifts = lanes(values[:, 96:384], 6)
    packed_shift = jnp.concatenate([shifts[1], jnp.zeros((D,), F32), shifts[2]])
    par = jnp.concatenate(
        [
            lanes(values[:, :96], 2),
            shifts,
            values[:, 384:].reshape(4, D),
            halves_first(packed_shift[None], 1).reshape(3, D),
            jnp.zeros((1, D), F32),
        ],
        0,
    )

    def attention(packed):
        heads = cross(packed, 1).reshape(L, 3 * HALF)
        mixed_heads, logs = attend(heads)
        return cross(mixed_heads.reshape(2, T, HALF), 2), (heads, mixed_heads, logs)

    def attention_back(kept, gmixed):
        heads, mixed_heads, logs = kept
        gheads = cross(gmixed, 2).reshape(L, HALF)
        gpacked = attend_back(heads, mixed_heads, gheads, logs)
        return cross(gpacked.reshape(2, T, 3 * HALF), 1)

    packed, _ = front(stream, full, par)
    mixed, _ = attention(packed)
    x, packed, normed = rear_front(stream, mixed, full, par)
    mixed, kept = attention(packed)
    result, gmixed, gmiddle, middle, normed2, pre, active = turn(x, mixed, stream, full, par)
    gp = attention_back(kept, gmixed)
    e, gmixed, gmiddle, rear_sums, mlow, gpre = back_back(
        gp, gmiddle, x, stream, middle, pre, full, par
    )
    heads, mixed_heads, logs = kept
    gf, gd, gq, go, total, section_out, in_grad = tail(
        [
            e, active, normed2, gpre, heads, mixed_heads, logs, mixed, mlow, normed, gmiddle, x,
        ],
        gmixed, result, full, par, rear_sums,
    )
    dp = lax.axis_index("dp")
    strip = lax.dynamic_slice(total, (0, dp * 48), (8, 48))
    up = lax.dynamic_slice(total, (8 + dp // 4, (dp % 4) * 192), (1, 192))
    return (
        section_out[None],
        in_grad[None],
        gq,
        go,
        gf,
        gd,
        strip[None, :2],
        strip[None, 2:],
        up,
    )


def solution(mesh):
    in_specs = (
        P("dp", "seq", None),
        P("dp", "seq", None),
        P("section", "dp", None),
        P("section", "dp", None),
        P("section", "dp", None),
        P("section", "dp", None),
        P("section", None, "dp"),
        P("section", None, "dp"),
        P("section", "dp"),
    )
    out_specs = (
        P("section", "dp", "seq", None),
        P("section", "dp", "seq", None),
        P("section", "dp", None),
        P("section", "dp", None),
        P("section", "dp", None),
        P("section", "dp", None),
        P("section", None, "dp"),
        P("section", None, "dp"),
        P("section", "dp"),
    )
    return jax.shard_map(body, mesh=mesh, in_specs=in_specs, out_specs=out_specs, check_vma=False)
```

```python
import functools
import math

import jax
import jax.numpy as jnp
from jax import lax
from jax.experimental import pallas as pl
from jax.experimental.pallas import tpu as pltpu
from jax.sharding import PartitionSpec as P

MESH = pl.DeviceIdType.MESH
BF = jnp.bfloat16
F32 = jnp.float32
D = 768
T = 512
L = 1024
HALF = 384
ROWS = 608
HROWS = ROWS // 2
EPS = 1e-05
FC_ROWS = (112, 160, 208, 256)
QKV_ROWS = (16, 64, 304)
OUT_ROW = 352
SCALE = 0.125
C2 = SCALE * math.log2(math.e)
VLIM = 60 * 1024 * 1024
ANY = pl.BlockSpec(memory_space=pl.ANY)
VM = pl.BlockSpec(memory_space=pltpu.VMEM)


def where_am_i():
    core = lax.axis_index("section")
    z = lax.axis_index("seq")
    dp = lax.axis_index("dp")
    return core, z, dp // 4, dp % 4


def greet(peers):
    barrier = pltpu.get_barrier_semaphore()
    for peer in peers:
        pl.semaphore_signal(barrier, inc=1, device_id=peer, device_id_type=MESH)
    pl.semaphore_wait(barrier, len(peers))


def remote(src, dst, send, recv, peer):
    return pltpu.make_async_remote_copy(
        src_ref=src, dst_ref=dst, send_sem=send, recv_sem=recv, device_id=peer, device_id_type=MESH
    )


def comm_params(ident):
    return pltpu.CompilerParams(
        collective_id=ident, has_side_effects=True, vmem_limit_bytes=VLIM
    )


PIECES = ((0, 112), (112, 96), (208, 96))


def head_kernel(
    wq, wo, wf, wp, small, ins, cots,
    full, stream, par, mixed,
    shard, smalls, wqs, packed, normed, heads, omix,
    lsem, gs, gr, ssem, rsem, xs, xr, qsems, asem, psem,
):
    core, z, y, x = where_am_i()
    block = z % 2
    sib = 1 - core
    dp = y * 4 + x
    sibling = (sib, z, dp)
    first = core == 0
    count = len(PIECES)

    def along(axis, step):
        if axis == 0:
            return (core, z, y * 4 + (x + step) % 4)
        return (core, z, ((y + step) % 4) * 4 + x)

    @pl.when(core == block)
    def _():
        for h in range(2):
            for k in range(3):
                at = h * 3 + k
                row = QKV_ROWS[at // 2]
                shard[row : row + 48, (at % 2) * HALF : (at % 2 + 1) * HALF] = (
                    wq[0, :, k * D + h * HALF : k * D + (h + 1) * HALF]
                )
        shard[OUT_ROW : OUT_ROW + 48] = wo[0]
        for m in range(4):
            shard[FC_ROWS[m] : FC_ROWS[m] + 48] = wf[0, :, m * D : (m + 1) * D]
        shard[0:16] = small[...]
        shard[400:592] = wp[0]
        shard[592:608] = jnp.zeros((16, D), BF)

    peers = [sibling]
    for step in (1, 2, 3):
        peers += [along(0, step), along(1, step), (core, (z + step) % 4, dp)]
    greet(peers)

    def span(p, whose):
        at, rows = PIECES[p]
        return pl.ds(pl.multiple_of(whose * HROWS + at, 16), rows)

    def give(p):
        view = shard.at[span(p, sib)]
        return remote(view, view, gs.at[p], gr.at[p], sibling)

    @pl.when(core == block)
    def _():
        for p in range(count):
            give(p).start()

    quarter = pl.ds(pl.multiple_of((z % 2) * 256, 256), 256)
    sends_tokens = (z // 2) == core

    def send_tokens():
        for step in (1, 2, 3):
            to = (z + step) % 4
            for source, parity in ((ins, 0), (cots, 1)):

                @pl.when(sends_tokens & (to % 2 == parity))
                def _():
                    remote(
                        source.at[to // 2],
                        stream.at[quarter],
                        xs.at[step],
                        xr.at[z % 2],
                        (core, to, dp),
                    ).start()

        for source, parity in ((ins, 0), (cots, 1)):

            @pl.when(sends_tokens & (z % 2 == parity))
            def _():
                pltpu.make_async_copy(
                    source.at[z // 2], stream.at[quarter], lsem.at[count]
                ).start()

    def shard_at(p, axis, step, whose):
        rows = span(p, whose)
        if axis == 0:
            return full.at[y, (x + step) % 4, rows]
        return full.at[(y + step) % 4, x, rows]

    def line_at(p, axis, step, half, whose):
        rows = span(p, whose)
        if axis == 0:
            return full.at[pl.ds(2 * half, 2), (x + step) % 4, rows]
        return full.at[(y + step) % 4, pl.ds(2 * half, 2), rows]

    def send(p, slot, src, dst, to):
        remote(src, dst, ssem.at[p, slot], rsem.at[p, slot], to).start()

    def came(p, slot, land):
        remote(land, land, ssem.at[p, slot], rsem.at[p, slot], sibling).wait_recv()

    def own_shard(p, axis):
        return pltpu.make_async_copy(
            shard.at[span(p, core)], shard_at(p, axis, 0, core), lsem.at[p]
        )

    def begin(p, axis):
        @pl.when(core != block)
        def _():
            view = shard.at[span(p, core)]
            remote(view, view, gs.at[p], gr.at[p], sibling).wait_recv()

        view = shard.at[span(p, core)]
        land = shard_at(p, axis, 0, core)
        for k in (2, 1, 3):
            send(p, k, view, land, along(axis, k))
        send(p, 14, view, land, sibling)
        own_shard(p, axis).start()

    def lines(p, axis):
        own_shard(p, axis).wait()
        for k in (1, 3, 2):
            came(p, k, shard_at(p, axis, 4 - k, core))
        for half in (0, 1):
            for slot, step in ((4, 1), (6, 3)):
                view = line_at(p, 1 - axis, 0, half, core)
                send(p, slot + half, view, view, along(1 - axis, step))
        for k in (1, 3, 2):
            view = shard_at(p, axis, 4 - k, core)
            send(p, 14 + k, view, view, sibling)

    def forward(p, axis):
        for half, slot, step, to in ((0, 4, 3, 1), (1, 6, 1, 3), (1, 4, 3, 0), (0, 6, 1, 0)):
            land = line_at(p, 1 - axis, step, half, core)
            came(p, slot + half, land)
            if to:
                send(p, 8 + half, land, land, along(1 - axis, to))
            send(p, 14 + slot + half, land, land, sibling)

    def opposite(p, axis):
        for half in (0, 1):
            land = line_at(p, 1 - axis, 2, half, core)
            came(p, 8 + half, land)
            send(p, 22 + half, land, land, sibling)

    def passed_on(p, axis):
        came(p, 14, shard_at(p, 1 - axis, 0, sib))
        for k in (1, 3, 2):
            came(p, 14 + k, shard_at(p, 1 - axis, 4 - k, sib))
        for half, slot, step in ((0, 4, 3), (1, 6, 1), (1, 4, 3), (0, 6, 1)):
            came(p, 14 + slot + half, line_at(p, axis, step, half, sib))
        for half in (0, 1):
            came(p, 22 + half, line_at(p, axis, 2, half, sib))

    def sent(p, axis):
        for slot in (1, 2, 3, 14, 15, 16, 17):
            view = shard_at(p, axis, 0, core)
            remote(view, view, ssem.at[p, slot], rsem.at[p, slot], sibling).wait_send()
        for slot in (4, 5, 6, 7, 8, 9, 18, 19, 20, 21, 22, 23):
            view = line_at(p, axis, 0, 0, core)
            remote(view, view, ssem.at[p, slot], rsem.at[p, slot], sibling).wait_send()

    def both(*steps):
        @pl.when(first)
        def _():
            for step, p in steps:
                step(p, 0)

        @pl.when(jnp.logical_not(first))
        def _():
            for step, p in steps:
                step(p, 1)

    both((begin, 0))
    send_tokens()
    both(
        (begin, 1), (begin, 2), (lines, 0), (lines, 1), (forward, 0), (lines, 2),
        (opposite, 0), (passed_on, 0),
    )

    fetches = [
        pltpu.make_async_copy(
            full.at[:, :, pl.ds(QKV_ROWS[m], 48)], wqs.at[m], qsems.at[m]
        )
        for m in range(3)
    ]
    fetches.append(pltpu.make_async_copy(full.at[:, :, pl.ds(0, 16)], smalls, qsems.at[3]))
    for fetch in reversed(fetches):
        fetch.start()

    @pl.when(sends_tokens)
    def _():
        pltpu.make_async_copy(ins.at[0], stream.at[quarter], lsem.at[count]).wait()

    for j in (0, 1):

        @pl.when(z != 2 * core + j)
        def _():
            land = stream.at[pl.ds(256 * j, 256)]
            remote(land, land, xs.at[0], xr.at[j], sibling).wait_recv()

    fetches[3].wait()
    total = smalls[0, 0].astype(F32)
    for k in range(1, 16):
        total = total + smalls[k // 4, k % 4].astype(F32)
    par[...] = total
    zero = jnp.zeros((1, HALF), F32)
    par[12:13, :HALF] = total[3:4, :HALF]
    par[12:13, HALF:] = zero
    par[13:14, :HALF] = total[4:5, :HALF]
    par[13:14, HALF:] = total[3:4, HALF:]
    par[14:15, :HALF] = zero
    par[14:15, HALF:] = total[4:5, HALF:]

    def need(m):
        fetches[m].wait()

    for i, at in enumerate(TILES):
        front_tile(at, nothing if i else need, stream, wqs, par, packed, normed)
        if i == 0:
            both((forward, 1))

    def token_rows(c):
        return pl.ds(pl.multiple_of(c * T, T), T)

    out = remote(packed.at[sib], heads.at[token_rows(core)], asem.at[0], asem.at[1], sibling)
    back = remote(packed.at[0], heads.at[token_rows(sib)], asem.at[0], asem.at[1], sibling)
    keep = pltpu.make_async_copy(packed.at[core], heads.at[token_rows(core)], asem.at[2])
    out.start()
    keep.start()
    keep.wait()
    back.wait_recv()

    @pl.loop(0, 3)
    def _(pair):
        columns = part_columns(pair)
        narrow = pl.ds(pl.multiple_of(pair * 128, 128), 128)

        def put(at, value):
            omix[at, narrow] = value

        attend_pair(lambda name, rows: heads[rows, columns(name)], put, None)

        @pl.when(pair == 0)
        def _():
            both((opposite, 1), (forward, 2))

    m_out = remote(omix.at[token_rows(sib)], mixed.at[core], psem.at[0], psem.at[1], sibling)
    m_in = remote(omix.at[token_rows(core)], mixed.at[sib], psem.at[0], psem.at[1], sibling)
    m_own = pltpu.make_async_copy(omix.at[token_rows(core)], mixed.at[core], psem.at[2])
    m_out.start()
    m_own.start()
    both(
        (opposite, 2), (passed_on, 1), (passed_on, 2), (sent, 0), (sent, 1), (sent, 2),
    )
    m_own.wait()
    m_in.wait_recv()
    m_out.wait_send()
    out.wait_send()

    @pl.when(core == block)
    def _():
        for p in range(count):
            give(p).wait_send()

    @pl.when(sends_tokens)
    def _():
        for step in (1, 2, 3):
            remote(ins.at[0], stream.at[quarter], xs.at[step], xr.at[0], sibling).wait_send()


def head(wq, wo, wf, wp, small, ins, cots):
    dma = pltpu.SemaphoreType.DMA
    n = len(PIECES)
    return pl.pallas_call(
        head_kernel,
        name="head",
        out_shape=(
            jax.ShapeDtypeStruct((4, 4, ROWS, D), BF),
            jax.ShapeDtypeStruct((T, D), BF),
            jax.ShapeDtypeStruct((16, D), F32),
            jax.ShapeDtypeStruct((2, T, HALF), BF),
        ),
        in_specs=[VM] * 5 + [ANY] * 2,
        out_specs=(ANY, VM, VM, VM),
        scratch_shapes=[
            wide(ROWS),
            wide(4, 4, 16),
            wide(3, 4, 4, 48),
            pltpu.VMEM((2, T, 3 * HALF), BF),
            wide(T),
            pltpu.VMEM((L, 3 * HALF), BF),
            pltpu.VMEM((L, HALF), BF),
            dma((n + 1,)),
            dma((n,)),
            dma((n,)),
            dma((n, 24)),
            dma((n, 24)),
            dma((4,)),
            dma((2,)),
            dma((4,)),
            dma((3,)),
            dma((3,)),
        ],
        compiler_params=comm_params(0),
    )(wq, wo, wf, wp, small, ins, cots)


def cross_kernel(src, dst, stage, lsem, ssem, rsem):
    core, z, y, x = where_am_i()
    sibling = (1 - core, z, y * 4 + x)
    local_in = pltpu.make_async_copy(src.at[core], stage, lsem)
    local_in.start()
    greet([sibling])
    out = remote(src.at[1 - core], dst.at[core], ssem, rsem, sibling)
    out.start()
    local_in.wait()
    local_out = pltpu.make_async_copy(stage, dst.at[core], lsem)
    local_out.start()
    local_out.wait()
    out.wait_send()
    remote(src.at[1 - core], dst.at[1 - core], ssem, rsem, sibling).wait_recv()


def cross(pieces, ident):
    return pl.pallas_call(
        cross_kernel,
        name="cross_cores",
        out_shape=jax.ShapeDtypeStruct(pieces.shape, pieces.dtype),
        in_specs=[ANY],
        out_specs=ANY,
        scratch_shapes=[pltpu.VMEM(pieces.shape[1:], pieces.dtype)]
        + [pltpu.SemaphoreType.DMA] * 3,
        compiler_params=comm_params(ident),
    )(pieces)


def dot(a, b):
    return jnp.dot(a, b, preferred_element_type=F32)


def dot_nt(a, b):
    return lax.dot_general(a, b, (((1,), (1,)), ((), ())), preferred_element_type=F32)


def dot_tn(a, b):
    return lax.dot_general(a, b, (((0,), (0,)), ((), ())), preferred_element_type=F32)


def normalized(v):
    centre = v - jnp.mean(v, axis=-1, keepdims=True)
    inv = lax.rsqrt(jnp.mean(centre * centre, axis=-1, keepdims=True) + EPS)
    return centre * inv, inv


def norm_back(grad, gain, unit, inv):
    g = grad * gain
    return inv * (
        g
        - jnp.mean(g, axis=-1, keepdims=True)
        - unit * jnp.mean(g * unit, axis=-1, keepdims=True)
    )


def matrix(ref, m):
    return ref[m].reshape(D, D)


class Fetch:
    def __init__(self, w, sems, parts):
        self.copies = []
        for at, (buffer, m, kind) in enumerate(parts):
            if kind is None:
                src = w.at[pl.ds(4 * m, 4), pl.ds(400, 192)]
            else:
                src = w.at[:, pl.ds(kind, 48)]
            self.copies.append(pltpu.make_async_copy(src, buffer.at[m], sems.at[at]))
        for copy in self.copies:
            copy.start()

    def need(self, at):
        self.copies[at].wait()


class Store:
    def __init__(self, sems):
        self.sems = sems
        self.copies = []

    def put(self, src, dst):
        copy = pltpu.make_async_copy(src, dst, self.sems.at[len(self.copies)])
        copy.start()
        self.copies.append(copy)

    def finish(self):
        for copy in self.copies:
            copy.wait()


def wide(*lead):
    return pltpu.VMEM((*lead, D), BF)


def local_params():
    return pltpu.CompilerParams(vmem_limit_bytes=VLIM)


TILES = (slice(0, 256), slice(256, 512))


def front_tile(at, need, x, wq, par, packed, normed_out):
    unit, _ = normalized(x[at].astype(F32))
    normed = (unit * par[0:1] + par[2:3]).astype(BF)
    normed_out[at] = normed
    need(0)
    a = (dot(normed, matrix(wq, 0)) + par[12:13]).astype(BF)
    packed[0, at, :D] = a
    need(1)
    b = (dot(normed, matrix(wq, 1)) + par[13:14]).astype(BF)
    packed[0, at, D:] = b[:, :HALF]
    packed[1, at, :HALF] = b[:, HALF:]
    need(2)
    c = (dot(normed, matrix(wq, 2)) + par[14:15]).astype(BF)
    packed[1, at, HALF:] = c


def nothing(at):
    pass


def QKV_PARTS(wq):
    return [(wq, m, QKV_ROWS[m]) for m in range(3)]


QB = 256


def head_masks(ref_value):
    lane = lax.broadcasted_iota(jnp.int32, ref_value.shape, 1)
    zero = jnp.zeros_like(ref_value)
    return (
        jnp.where(lane < 64, ref_value, zero),
        jnp.where(lane >= 64, ref_value, zero),
    )


def causal(rows, cols, offset):
    row = lax.broadcasted_iota(jnp.int32, (rows, cols), 0) + offset
    return lax.broadcasted_iota(jnp.int32, (rows, cols), 1) <= row


def attend_pair(get, put, put_logs):
    for i in range(L // QB):
        at = slice(i * QB, (i + 1) * QB)
        stop = (i + 1) * QB
        keys = get("k", slice(0, stop))
        queries = head_masks(get("q", at))
        values = head_masks(get("v", slice(0, stop)))
        keep = causal(QB, stop, i * QB)
        total = None
        saved = []
        for h in range(2):
            s = jnp.where(keep, dot_nt(queries[h], keys), -1e30)
            peak = jnp.max(s, axis=-1, keepdims=True)
            p = jnp.exp2((s - peak) * C2)
            norm = jnp.sum(p, axis=-1, keepdims=True)
            o = dot(p.astype(BF), values[h]) * (1.0 / norm)
            total = o if total is None else total + o
            saved.append(peak * C2 + jnp.log2(norm))
        put(at, total.astype(BF))
        if put_logs:
            lane = lax.broadcasted_iota(jnp.int32, (QB, 128), 1)
            put_logs(at, jnp.where(lane < 64, saved[0], saved[1]))


def attend_kernel(q_ref, k_ref, v_ref, mixed, logs):
    refs = {"q": q_ref, "k": k_ref, "v": v_ref}

    def put(at, value):
        mixed[at] = value

    def put_logs(at, value):
        logs[0, at] = value

    attend_pair(lambda name, rows: refs[name][rows], put, put_logs)


def attend(heads):
    def col(k):
        return pl.BlockSpec((L, 128), lambda p: (0, p + 3 * k))

    return pl.pallas_call(
        attend_kernel,
        name="attend",
        grid=(3,),
        out_shape=(
            jax.ShapeDtypeStruct((L, HALF), BF),
            jax.ShapeDtypeStruct((3, L, 128), F32),
        ),
        in_specs=[col(0), col(1), col(2)],
        out_specs=(col(0), pl.BlockSpec((1, L, 128), lambda p: (p, 0, 0))),
        compiler_params=local_params(),
    )(heads, heads, heads)


def attend_back_pair(get, put, logs_at, dk, dv):
    dk[...] = jnp.zeros_like(dk)
    dv[...] = jnp.zeros_like(dv)
    for i in range(L // QB):
        at = slice(i * QB, (i + 1) * QB)
        stop = (i + 1) * QB
        keys = get("k", slice(0, stop))
        values = get("v", slice(0, stop))
        keys_of = head_masks(keys)
        queries = head_masks(get("q", at))
        top = get("do", at)
        tops = head_masks(top)
        keep = causal(QB, stop, i * QB)
        inner = head_masks(top.astype(F32) * get("o", at).astype(F32))
        dq = None
        for h in range(2):
            s = dot_nt(queries[h], keys)
            p = jnp.where(keep, jnp.exp2(s * C2 - logs_at(at, h)), 0.0)
            gw = dot_nt(tops[h], values)
            delta = jnp.sum(inner[h], axis=-1, keepdims=True)
            ds = (p * (gw - delta)).astype(BF)
            part = dot(ds, keys_of[h])
            dq = part if dq is None else dq + part
            dk[:stop] += dot_tn(ds, queries[h])
            dv[:stop] += dot_tn(p.astype(BF), tops[h])
        put("q", at, (dq * SCALE).astype(BF))
    put("k", slice(0, L), (dk[...] * SCALE).astype(BF))
    put("v", slice(0, L), dv[...].astype(BF))


def part_columns(pair):
    def columns(name):
        return pl.ds(pl.multiple_of("qkv".index(name) * HALF + pair * 128, 128), 128)

    return columns


def attend_back_kernel(q_ref, k_ref, v_ref, o_ref, do_ref, logs, out, dk, dv):
    refs = {"q": q_ref, "k": k_ref, "v": v_ref, "o": o_ref, "do": do_ref}
    columns = part_columns(pl.program_id(0))

    def get(name, rows):
        return refs[name][rows]

    def put(name, rows, value):
        out[rows, columns(name)] = value

    attend_back_pair(
        get, put, lambda at, h: logs[0, at, 64 * h : 64 * h + 1], dk, dv
    )


def attend_back(heads, mixed, grad_mixed, logs):
    def col(k):
        return pl.BlockSpec((L, 128), lambda p: (0, p + 3 * k))

    return pl.pallas_call(
        attend_back_kernel,
        name="attend_back",
        grid=(3,),
        out_shape=jax.ShapeDtypeStruct((L, 3 * HALF), BF),
        in_specs=[
            col(0),
            col(1),
            col(2),
            col(0),
            col(0),
            pl.BlockSpec((1, L, 128), lambda p: (p, 0, 0)),
        ],
        out_specs=pl.BlockSpec((L, 3 * HALF), lambda p: (0, 0)),
        scratch_shapes=[pltpu.VMEM((L, 128), F32)] * 2,
        compiler_params=local_params(),
    )(heads, heads, heads, mixed, grad_mixed, logs)


REAR_SCRATCH = [
    wide(1, 16, 48),
    wide(4, 16, 48),
    wide(4, 4, 192),
    pltpu.SemaphoreType.DMA((9,)),
]


def gelu(v):
    return 0.5 * v * (1.0 + jnp.tanh(0.79788456 * (v + 0.044715 * v * v * v)))


def gelu_slope(v):
    square = v * v
    t = jnp.tanh(0.79788456 * v * (1.0 + 0.044715 * square))
    return 0.5 * (1.0 + t) + 0.5 * v * (1.0 - t * t) * 0.79788456 * (
        1.0 + 3 * 0.044715 * square
    )


def forward_parts(wo, wf, wp):
    parts = [(wo, 0, OUT_ROW)]
    for m in range(4):
        parts += [(wf, m, FC_ROWS[m]), (wp, m, None)]
    return parts


def backward_parts(wo, wf, wp):
    parts = []
    for m in range(4):
        parts += [(wp, m, None), (wf, m, FC_ROWS[m])]
    return parts + [(wo, 0, OUT_ROW)]


def rear_tile(at, need, x, mixed, wo, wf, wp, par, result, kept, store):
    mix = jnp.concatenate([mixed[0, at], mixed[1, at]], axis=1)
    need(0)
    middle = x[at].astype(F32) + (dot(mix, matrix(wo, 0)) + par[5:6])
    unit, _ = normalized(middle)
    normed = (unit * par[1:2] + par[6:7]).astype(BF)
    if kept:
        kept[0][at] = middle
        kept[1][at] = normed
        store(0, at, None)
        store(1, at, None)
    total = middle + par[7:8]
    for m in range(4):
        need(1 + 2 * m)
        pre = dot(normed, matrix(wf, m)) + par[8 + m : 9 + m]
        active = gelu(pre).astype(BF)
        if kept:
            cols = slice(m * D, (m + 1) * D)
            kept[2][at, cols] = pre.astype(BF)
            kept[3][at, cols] = active
            store(2, at, cols)
            store(3, at, cols)
        need(2 + 2 * m)
        total = total + dot(active, matrix(wp, m))
    result[at] = total.astype(BF)


def column_sum(v):
    return jnp.sum(v, axis=0, keepdims=True)


def adder(sums, i):
    def add(row, v):
        if i:
            sums[row : row + 1] += column_sum(v)
        else:
            sums[row : row + 1] = column_sum(v)

    return add


def rear_back_tile(at, need, e, middle, pre, wo, wf, wp, par, gmixed, gmiddle, full):
    if full:
        add, mlow, gpre, store = full
    top = e[at]
    gnorm = None
    for m in range(4):
        cols = slice(m * D, (m + 1) * D)
        need(2 * m)
        gact = dot_nt(top, matrix(wp, m))
        low = (gact * gelu_slope(pre[at, cols].astype(F32))).astype(BF)
        if full:
            gpre[at, cols] = low
            store(0, at, cols)
            add(4 + m, low.astype(F32))
        need(2 * m + 1)
        part = dot_nt(low, matrix(wf, m))
        gnorm = part if gnorm is None else gnorm + part
    unit, inv = normalized(middle[at])
    top_wide = top.astype(F32)
    gmid = top_wide + norm_back(gnorm, par[1:2], unit, inv)
    gmiddle[at] = gmid
    low = gmid.astype(BF)
    if full:
        add(0, top_wide)
        add(1, gnorm * unit)
        add(2, gnorm)
        add(3, gmid)
        mlow[at] = low
        store(1, at, None)
    need(8)
    gm = dot_nt(low, matrix(wo, 0)).astype(BF)
    gmixed[0, at] = gm[:, :HALF]
    gmixed[1, at] = gm[:, HALF:]


def front_back_tile(at, need, gp, gmiddle, x, wq, par, grad, add):
    gnorm = None
    for m, piece in enumerate(packed_pieces(gp, at)):
        if add:
            add(2 + m, piece.astype(F32))
        need(m)
        part = dot_nt(piece, matrix(wq, m))
        gnorm = part if gnorm is None else gnorm + part
    unit, inv = normalized(x[at].astype(F32))
    if add:
        add(0, gnorm * unit)
        add(1, gnorm)
    grad[at] = (gmiddle[at] + norm_back(gnorm, par[0:1], unit, inv)).astype(BF)


def partner_of():
    core, z, y, x = where_am_i()
    return z % 2, (core, z + 1 - 2 * (z % 2), y * 4 + x)


def rear_front_kernel(
    x, mixed, w, par, x2, packed, normed, wo, wf, wp, sems, wq, qsems, res, ssem, rsem
):
    block, partner = partner_of()
    fetch = Fetch(w, sems, forward_parts(wo, wf, wp))
    fetch_q = Fetch(w, qsems, QKV_PARTS(wq))
    greet([partner])

    def hand(i):
        rows = pl.ds(256 * i, 256)
        return remote(res.at[rows], x2.at[rows], ssem.at[i], rsem.at[i], partner)

    @pl.when(block == 0)
    def _():
        for i, at in enumerate(TILES):
            rear_tile(
                at, nothing if i else fetch.need, x, mixed, wo, wf, wp, par, res, None, None
            )
            hand(i).start()
        x2[...] = x[...]

    @pl.when(block == 1)
    def _():
        for k in range(9):
            fetch.need(k)

    for k in range(3):
        fetch_q.need(k)
    for i, at in enumerate(TILES):
        pl.when(block == 1)(hand(i).wait_recv)
        front_tile(at, nothing, x2, wq, par, packed, normed)

    @pl.when(block == 0)
    def _():
        for i in range(2):
            hand(i).wait_send()


def rear_front(x, mixed, w, par):
    dma = pltpu.SemaphoreType.DMA
    return pl.pallas_call(
        rear_front_kernel,
        name="rear_hand_front",
        out_shape=(
            jax.ShapeDtypeStruct((T, D), BF),
            jax.ShapeDtypeStruct((2, T, 3 * HALF), BF),
            jax.ShapeDtypeStruct((T, D), BF),
        ),
        in_specs=[VM, VM, ANY, VM],
        out_specs=(VM, VM, VM),
        scratch_shapes=REAR_SCRATCH
        + [wide(3, 16, 48), dma((3,)), wide(T), dma((2,)), dma((2,))],
        compiler_params=comm_params(3),
    )(x, mixed, w, par)


def turn_kernel(
    x, mixed, e, w, par, result, gmixed, gmiddle, middle_out, normed_out, pre_out, active_out,
    wo, wf, wp, sems, middle, normed, pre, active, osems,
):
    fetch = Fetch(w, sems, forward_parts(wo, wf, wp))
    store = Store(osems)
    kept = (middle, normed, pre, active)
    outs = (middle_out, normed_out, pre_out, active_out)

    def put(n, at, cols):
        rows = pl.ds(at.start, at.stop - at.start)
        if cols is None:
            store.put(kept[n].at[rows], outs[n].at[rows])
        else:
            lanes = pl.ds(cols.start, D)
            store.put(kept[n].at[rows, lanes], outs[n].at[rows, lanes])

    for i, at in enumerate(TILES):
        rear_tile(
            at, nothing if i else fetch.need, x, mixed, wo, wf, wp, par, result, kept, put
        )
    for at in TILES:
        rear_back_tile(at, nothing, e, middle, pre, wo, wf, wp, par, gmixed, gmiddle, None)
    store.finish()


def turn(x, mixed, e, w, par):
    kept = [((T, D), F32), ((T, D), BF), ((T, 4 * D), BF), ((T, 4 * D), BF)]
    outs = [((T, D), BF), ((2, T, HALF), BF), ((T, D), F32)] + kept
    return pl.pallas_call(
        turn_kernel,
        name="turn",
        out_shape=tuple(jax.ShapeDtypeStruct(s, t) for s, t in outs),
        in_specs=[VM, VM, VM, ANY, VM],
        out_specs=(VM, VM, VM, ANY, ANY, ANY, ANY),
        scratch_shapes=REAR_SCRATCH
        + [pltpu.VMEM(s, t) for s, t in kept]
        + [pltpu.SemaphoreType.DMA((20,))],
        compiler_params=local_params(),
    )(x, mixed, e, w, par)


def back_back_kernel(
    gp, gmid_in, x, stream, middle, pre_in, w, par,
    e, gmixed, gmiddle, sums, mlow_out, gpre_out,
    wo, wf, wp, sems, wq, qsems, res, ssem, rsem, pre, mlow, gpre, psem, osems,
):
    block, partner = partner_of()
    fetch_q = Fetch(w, qsems, QKV_PARTS(wq))
    fetch = Fetch(w, sems, backward_parts(wo, wf, wp))
    load = pltpu.make_async_copy(pre_in, pre, psem)
    load.start()
    greet([partner])

    def hand(i):
        rows = pl.ds(256 * i, 256)
        return remote(res.at[rows], e.at[rows], ssem.at[i], rsem.at[i], partner)

    for k in range(3):
        fetch_q.need(k)

    @pl.when(block == 1)
    def _():
        for i, at in enumerate(TILES):
            front_back_tile(at, nothing, gp, gmid_in, x, wq, par, res, None)
            hand(i).start()
        e[...] = stream[...]

    for k in range(9):
        fetch.need(k)
    load.wait()
    store = Store(osems)

    def put(n, at, cols):
        rows = pl.ds(at.start, at.stop - at.start)
        if cols is None:
            store.put(mlow.at[rows], mlow_out.at[rows])
        else:
            lanes = pl.ds(cols.start, D)
            store.put(gpre.at[rows, lanes], gpre_out.at[rows, lanes])

    for i, at in enumerate(TILES):
        pl.when(block == 0)(hand(i).wait_recv)
        rear_back_tile(
            at, nothing, e, middle, pre, wo, wf, wp, par, gmixed, gmiddle,
            (adder(sums, i), mlow, gpre, put),
        )

    @pl.when(block == 1)
    def _():
        for i in range(2):
            hand(i).wait_send()

    store.finish()


def back_back(gp, gmid, x, stream, middle, pre, w, par):
    dma = pltpu.SemaphoreType.DMA
    return pl.pallas_call(
        back_back_kernel,
        name="front_back_hand_rear_back",
        out_shape=(
            jax.ShapeDtypeStruct((T, D), BF),
            jax.ShapeDtypeStruct((2, T, HALF), BF),
            jax.ShapeDtypeStruct((T, D), F32),
            jax.ShapeDtypeStruct((8, D), F32),
            jax.ShapeDtypeStruct((T, D), BF),
            jax.ShapeDtypeStruct((T, 4 * D), BF),
        ),
        in_specs=[VM, VM, VM, VM, VM, ANY, ANY, VM],
        out_specs=(VM, VM, VM, VM, ANY, ANY),
        scratch_shapes=REAR_SCRATCH
        + [wide(3, 16, 48), dma((3,)), wide(T), dma((2,)), dma((2,))]
        + [pltpu.VMEM((T, 4 * D), BF), wide(T), pltpu.VMEM((T, 4 * D), BF)]
        + [dma, dma((10,))],
        compiler_params=comm_params(4),
    )(gp, gmid, x, stream, middle, pre, w, par)


def packed_pieces(gp, at=slice(None)):
    return (
        gp[0, at, :D],
        jnp.concatenate([gp[0, at, D:], gp[1, at, :HALF]], axis=1),
        gp[1, at, HALF:],
    )


def rows_of(stage):
    return pl.ds(*stage)


class Reducer:
    def __init__(self, stages, buffers, sems):
        self.stages = stages
        self.own, self.r0, self.r1, self.r2, self.s1, self.s2, self.r3 = buffers
        self.s1s, self.s1r, self.s2s, self.s2r, self.s3s, self.s3r, self.ks = sems
        self.core, self.z, y, x = where_am_i()
        self.x, self.y = x, y
        self.dp = y * 4 + x
        self.block = self.z % 2
        self.seq = self.z // 2
        self.first = self.core == 0
        self.sibling = (1 - self.core, self.z, self.dp)
        self.line = jnp.where(self.first, y, x)
        self.place = jnp.where(self.first, x, y)

    def on_line(self, step):
        to = (self.line + step) % 4
        return (self.core, self.z, jnp.where(self.first, to * 4 + self.x, self.y * 4 + to))

    def on_place(self, step):
        to = (self.place + step) % 4
        return (self.core, self.z, jnp.where(self.first, self.y * 4 + to, to * 4 + self.x))

    def peers(self):
        found = [self.sibling]
        for step in (1, 2, 3):
            found += [self.on_line(step), self.on_place(step)]
            for k in (0, 1):
                found.append((k, (self.z + step) % 4, self.dp))
        return found

    def over_cores(self, p):
        own, r0, rows = self.own, self.r0, rows_of(self.stages[p])

        @pl.loop(0, 16)
        def _(i):
            a = own[i // 4, i % 4, rows].astype(F32)
            b = r0[i // 4, i % 4, rows].astype(F32)
            own[i // 4, i % 4, rows] = (a + b).astype(BF)

        for step in (2, 1, 3):
            remote(
                own.at[(self.line + step) % 4, :, rows],
                self.r1.at[step - 1, :, rows],
                self.s1s.at[p, step],
                self.s1r.at[p, step],
                self.on_line(step),
            ).start()

    def over_lines(self, p):
        own, r1, s1, rows = self.own, self.r1, self.s1, rows_of(self.stages[p])
        line = self.line
        for step in (1, 3, 2):
            remote(
                own.at[0, :, rows],
                r1.at[step - 1, :, rows],
                self.s1s.at[p, step],
                self.s1r.at[p, step],
                self.sibling,
            ).wait()

        @pl.loop(0, 4)
        def _(i):
            s1[i, rows] = (
                (own[line, i, rows].astype(F32) + r1[0, i, rows].astype(F32))
                + (r1[1, i, rows].astype(F32) + r1[2, i, rows].astype(F32))
            ).astype(BF)

        for step in (2, 1, 3):
            remote(
                s1.at[(self.place + step) % 4, rows],
                self.r2.at[step - 1, rows],
                self.s2s.at[p, step],
                self.s2r.at[p, step],
                self.on_place(step),
            ).start()

    def along_z(self, p, step):
        rows = rows_of(self.stages[p])
        return remote(
            self.s2.at[rows],
            self.r3.at[self.core, self.seq, rows],
            self.s3s.at[p, step],
            self.s3r.at[p, self.core, self.seq],
            (self.block, (self.z + step) % 4, self.dp),
        )

    def to_sibling(self, p):
        rows = rows_of(self.stages[p])
        return remote(
            self.s2.at[rows],
            self.r3.at[self.core, self.seq, rows],
            self.s3s.at[p, 0],
            self.s3r.at[p, self.core, self.seq],
            self.sibling,
        )

    def keep_sum(self, p):
        rows = rows_of(self.stages[p])
        return pltpu.make_async_copy(
            self.s2.at[rows], self.r3.at[self.core, self.seq, rows], self.ks.at[p]
        )

    def over_places(self, p):
        s1, r2, rows = self.s1, self.r2, rows_of(self.stages[p])
        for step in (1, 3, 2):
            remote(
                s1.at[0, rows],
                r2.at[step - 1, rows],
                self.s2s.at[p, step],
                self.s2r.at[p, step],
                self.sibling,
            ).wait()
        self.s2[rows] = (
            (s1[self.place, rows].astype(F32) + r2[0, rows].astype(F32))
            + (r2[1, rows].astype(F32) + r2[2, rows].astype(F32))
        ).astype(BF)
        for step in (2, 1, 3):
            self.along_z(p, step).start()
        pl.when(self.core == self.block)(self.keep_sum(p).start)
        pl.when(self.core != self.block)(self.to_sibling(p).start)

    def finish(self, p):
        for step in (1, 2, 3):
            self.along_z(p, step).wait_send()
        pl.when(self.core == self.block)(self.keep_sum(p).wait)
        pl.when(self.core != self.block)(self.to_sibling(p).wait_send)
        rows = rows_of(self.stages[p])
        for c in (0, 1):
            for s in (0, 1):
                here = (self.core == self.block) & (self.core == c) & (self.seq == s)
                land = self.r3.at[c, s, rows]

                @pl.when(jnp.logical_not(here))
                def _():
                    remote(
                        land, land, self.s3s.at[p, 0], self.s3r.at[p, c, s], self.sibling
                    ).wait_recv()

    def total(self, c, p):
        rows = rows_of(self.stages[p])
        return self.r3[c, 0, rows].astype(F32) + self.r3[c, 1, rows].astype(F32)


def reducer_buffers(rows):
    return [
        pltpu.VMEM((4, 4, rows, D), BF),
        pltpu.VMEM((4, 4, rows, D), BF),
        pltpu.VMEM((3, 4, rows, D), BF),
        pltpu.VMEM((3, rows, D), BF),
        pltpu.VMEM((4, rows, D), BF),
        pltpu.VMEM((rows, D), BF),
        pltpu.VMEM((2, 2, rows, D), BF),
    ]


def reducer_sems(count):
    dma = pltpu.SemaphoreType.DMA
    return [dma((count, 4))] * 5 + [dma((count, 2, 2)), dma((count,))]


REAR_STAGES = ((0, 48), (48, 48), (96, 48), (144, 48))
REAR_ROWS = 192


def tail_kernel(*refs):
    sources, refs = refs[:12], refs[12:]
    gmixed, result, w, par, rear_sums = refs[:5]
    gf, gd, gq, go, gsmall, out_a, out_b = refs[5:12]
    loaded, refs = refs[12:24], refs[24:]
    gheads, gp, wq, snd, grad, fsums, dk, dv = refs[:8]
    buffers, refs = refs[8:15], refs[15:]
    late_buffers, refs = buffers[:2] + refs[:5], refs[5:]
    sems, refs = refs[:7], refs[7:]
    late_sems, refs = refs[:7], refs[7:]
    lsem, qsems, xsem, s0s, s0r, l0s, l0r, os, orr, ol = refs
    e, active, normed2, gpre, heads, omix, logs, mixed, mlow, normed, gmid, x = loaded
    own, r0 = buffers[0], buffers[1]

    copies = [
        pltpu.make_async_copy(src, dst, lsem.at[k])
        for k, (src, dst) in enumerate(zip(sources, loaded))
    ]
    for copy in copies:
        copy.start()
    fetch = Fetch(w, qsems, QKV_PARTS(wq))
    reducer = Reducer(REAR_STAGES, buffers, sems)
    late = Reducer(FRONT_STAGES, late_buffers, late_sems)
    core, sibling, first = reducer.core, reducer.sibling, reducer.first
    z, dp, block, seq = reducer.z, reducer.dp, reducer.block, reducer.seq
    greet(reducer.peers())

    def outputs(j, n):
        src, dst = ((result, out_a), (grad, out_b))[n]
        here = (core == block) & (z == 2 * core + j)
        view = src.at[pl.ds(256 * j, 256)]
        keep = pltpu.make_async_copy(view, dst.at[seq], ol.at[n])
        give = remote(
            view, dst.at[seq], os.at[2 * j + n], orr.at[seq, n], (block, 2 * core + j, dp)
        )
        return here, keep, give

    def send_output(j, n):
        here, keep, send = outputs(j, n)
        pl.when(here)(keep.start)
        pl.when(jnp.logical_not(here))(send.start)

    for j in (0, 1):
        send_output(j, 0)

    top_out = remote(gmixed.at[1 - core], gheads.at[core], xsem.at[0], xsem.at[1], sibling)
    top_in = remote(gmixed.at[0], gheads.at[1 - core], xsem.at[0], xsem.at[1], sibling)
    top_own = pltpu.make_async_copy(gmixed.at[core], gheads.at[core], xsem.at[2])
    top_out.start()
    top_own.start()

    def hidden_out(m):
        value = dot_tn(active[:, m * D : (m + 1) * D], e[...])
        return value.astype(BF).reshape(4, 192, D)

    def hidden_in(m):
        value = dot_tn(normed2[...], gpre[:, m * D : (m + 1) * D])
        return value.astype(BF).reshape(4, 4, 48, D)

    def give_out(m):
        return remote(snd.at[m], r0.at[:, m], s0s.at[m], s0r.at[m], sibling)

    def give_in(m):
        rows = pl.ds(m * 48, 48)
        return remote(
            snd.at[:, :, rows], r0.at[:, :, rows], s0s.at[m], s0r.at[m], sibling
        )

    for k in range(4):
        copies[k].wait()

    @pl.when(first)
    def _():
        for m in range(4):
            snd[m] = hidden_out(m)
            give_out(m).start()
        for m in range(4):
            own[:, :, m * 48 : (m + 1) * 48] = hidden_in(m)
            give_in(m).wait_recv()
            reducer.over_cores(m)

    @pl.when(jnp.logical_not(first))
    def _():
        for m in range(4):
            snd[:, :, m * 48 : (m + 1) * 48] = hidden_in(m)
            give_in(m).start()
        for m in range(4):
            own[:, m] = hidden_out(m)
        for m in range(4):
            give_out(m).wait_recv()
        for m in range(4):
            reducer.over_cores(m)

    top_own.wait()
    top_in.wait_recv()
    for k in range(4, 12):
        copies[k].wait()

    @pl.loop(0, 3)
    def _(pair):
        columns = part_columns(pair)
        narrow = pl.ds(pl.multiple_of(pair * 128, 128), 128)

        def get(name, rows):
            if name == "o":
                return omix[rows, narrow]
            if name == "do":
                half, start = rows.start // T, rows.start % T
                return gheads[half, start : start + QB, narrow]
            return heads[rows, columns(name)]

        def put(name, rows, value):
            heads[rows, columns(name)] = value

        attend_back_pair(
            get, put, lambda at, h: logs[pair, at, 64 * h : 64 * h + 1], dk, dv
        )

        @pl.when(pair == 1)
        def _():
            reducer.over_lines(0)

    def half_rows(c):
        return heads.at[pl.ds(pl.multiple_of(c * T, T), T)]

    gp_out = remote(half_rows(1 - core), gp.at[core], xsem.at[3], xsem.at[4], sibling)
    gp_in = remote(half_rows(core), gp.at[1 - core], xsem.at[3], xsem.at[4], sibling)
    gp_own = pltpu.make_async_copy(half_rows(core), gp.at[core], xsem.at[5])
    gp_out.start()
    gp_own.start()
    reducer.over_lines(1)
    reducer.over_places(0)
    for k in range(3):
        fetch.need(k)
    gp_own.wait()
    gp_in.wait_recv()

    for i, at in enumerate(TILES):
        front_back_tile(at, nothing, gp, gmid, x, wq, par, grad, adder(fsums, i))
        send_output(i, 1)
        reducer.over_lines(2 + i)
        reducer.over_places(1 + i)

    @pl.when(first)
    def _():
        for m in range(4):
            give_out(m).wait_send()

    @pl.when(jnp.logical_not(first))
    def _():
        for m in range(4):
            give_in(m).wait_send()

    zero = jnp.zeros((1, D), F32)
    small = jnp.concatenate(
        [
            fsums[0:1],
            rear_sums[1:2],
            fsums[1:2],
            zero,
            zero,
            rear_sums[3:4],
            rear_sums[2:3],
            rear_sums[0:1],
            rear_sums[4:8],
            fsums[2:5],
            zero,
        ],
        0,
    ).astype(BF)

    def packed_grad(m):
        piece = packed_pieces(gp)[m]
        return dot_tn(normed[...], piece).astype(BF).reshape(4, 4, 48, D)

    def out_grad():
        mix = jnp.concatenate([mixed[0], mixed[1]], axis=1)
        return dot_tn(mix, mlow[...]).astype(BF).reshape(4, 4, 48, D)

    def give_late(p, k):
        rows = rows_of(FRONT_STAGES[p])
        return rows, snd.at[k, :, rows], l0s.at[p, k], l0r.at[p, k]

    def give_late_0(p, k):
        rows, src, ss, rs = give_late(p, k)
        return remote(src, r0.at[:, k, rows], ss, rs, sibling)

    def give_late_1(p, k):
        rows, src, ss, rs = give_late(p, k)
        return remote(src, r0.at[k, :, rows], ss, rs, sibling)

    def fill(dst, swapped, at, value):
        for k in range(4):
            if swapped:
                dst[:, k, at : at + value.shape[2]] = value[k]
            else:
                dst[k, :, at : at + value.shape[2]] = value[k]

    smalls = jnp.broadcast_to(small[None, None], (4, 4, 16, D))

    @pl.when(first)
    def _():
        fill(snd, False, 0, packed_grad(2))
        for k in range(4):
            give_late_0(0, k).start()
        fill(snd, False, 48, out_grad())
        fill(snd, False, 96, jnp.zeros((4, 4, 16, D), BF))
        for k in range(4):
            give_late_0(1, k).start()
        fill(own, False, 0, packed_grad(0))
        fill(own, False, 48, packed_grad(1))
        fill(own, False, 96, smalls)

    @pl.when(jnp.logical_not(first))
    def _():
        fill(snd, False, 0, packed_grad(0))
        for k in range(4):
            give_late_1(0, k).start()
        fill(snd, False, 48, packed_grad(1))
        fill(snd, False, 96, smalls)
        for k in range(4):
            give_late_1(1, k).start()
        fill(own, True, 0, packed_grad(2))
        fill(own, True, 48, out_grad())
        fill(own, True, 96, jnp.zeros((4, 4, 16, D), BF))

    for p in range(2):
        for k in range(4):
            give_late_1(p, k).wait()
        late.over_cores(p)
    reducer.over_places(3)
    for m in range(4):
        reducer.finish(m)
        gf[0, :, m * D : (m + 1) * D] = reducer.total(0, m)
        gd[0, m * 48 : (m + 1) * 48] = reducer.total(1, m)
        if m == 1:
            late.over_lines(0)
    late.over_lines(1)
    for p in range(2):
        late.over_places(p)
    for p in range(2):
        late.finish(p)

    def put(m, value):
        for side in (0, 1):
            h, k = (2 * m + side) // 3, (2 * m + side) % 3
            gq[0, :, k * D + h * HALF : k * D + (h + 1) * HALF] = value[
                :, side * HALF : (side + 1) * HALF
            ]

    put(0, late.total(0, 0))
    put(2, late.total(1, 0))
    both = late.total(0, 1)
    put(1, both[:48])
    go[0] = late.total(1, 1)[:48]
    small = both[48:]
    gsmall[...] = small
    gsmall[3:4, :HALF] = small[12:13, :HALF]
    gsmall[3:4, HALF:] = small[13:14, HALF:]
    gsmall[4:5, :HALF] = small[13:14, :HALF]
    gsmall[4:5, HALF:] = small[14:15, HALF:]

    top_out.wait_send()
    gp_out.wait_send()
    for j in (0, 1):
        for n in (0, 1):
            here, keep, send = outputs(j, n)
            pl.when(here)(keep.wait)
            pl.when(jnp.logical_not(here))(send.wait_send)

    for s in (0, 1):
        for n, dst in enumerate((out_a, out_b)):
            here = (core == seq) & (z == 2 * s + core)

            @pl.when(jnp.logical_not(here))
            def _():
                remote(dst.at[s], dst.at[s], os.at[0], orr.at[s, n], sibling).wait_recv()


def tail(loads, gmixed, result, w, par, rear_sums):
    dma = pltpu.SemaphoreType.DMA
    return pl.pallas_call(
        tail_kernel,
        name="tail",
        out_shape=(
            jax.ShapeDtypeStruct((1, 48, 4 * D), F32),
            jax.ShapeDtypeStruct((1, 192, D), F32),
            jax.ShapeDtypeStruct((1, 48, 3 * D), F32),
            jax.ShapeDtypeStruct((1, 48, D), F32),
            jax.ShapeDtypeStruct((16, D), F32),
            jax.ShapeDtypeStruct((2, 256, D), BF),
            jax.ShapeDtypeStruct((2, 256, D), BF),
        ),
        in_specs=[ANY] * 15 + [VM] * 2,
        out_specs=(VM, VM, VM, VM, VM, ANY, ANY),
        scratch_shapes=[pltpu.VMEM(v.shape, v.dtype) for v in loads]
        + [
            pltpu.VMEM((2, T, HALF), BF),
            pltpu.VMEM((2, T, 3 * HALF), BF),
            wide(3, 16, 48),
            wide(4, 4, REAR_ROWS),
            wide(T),
            pltpu.VMEM((8, D), F32),
            pltpu.VMEM((L, 128), F32),
            pltpu.VMEM((L, 128), F32),
        ]
        + reducer_buffers(REAR_ROWS)
        + reducer_buffers(FRONT_ROWS)[2:]
        + reducer_sems(4)
        + reducer_sems(2)
        + [dma((12,)), dma((3,)), dma((6,)), dma((4,)), dma((4,))]
        + [dma((2, 4)), dma((2, 4)), dma((4,)), dma((2, 2)), dma((2,))],
        compiler_params=comm_params(5),
    )(*loads, gmixed, result, w, par, rear_sums)


FRONT_STAGES = ((0, 48), (48, 64))
FRONT_ROWS = 112


def body(inputs, cotangent, w_qkv, w_out, w_fc, w_proj, gains, biases, fc_bias):
    dp = lax.axis_index("dp")
    strip = jnp.concatenate([gains[0], biases[0]], 0)
    small = lax.dynamic_update_slice(jnp.zeros((16, D), BF), strip, (0, dp * 48))
    small = lax.dynamic_update_slice(small, fc_bias, (8 + dp // 4, (dp % 4) * 192))
    full, stream, par, mixed = head(w_qkv, w_out, w_fc, w_proj, small, inputs, cotangent)
    full = full.reshape(16, ROWS, D)

    def attention(packed):
        heads = cross(packed, 1).reshape(L, 3 * HALF)
        mixed_heads, logs = attend(heads)
        return cross(mixed_heads.reshape(2, T, HALF), 2), (heads, mixed_heads, logs)

    def attention_back(kept, gmixed):
        heads, mixed_heads, logs = kept
        gheads = cross(gmixed, 2).reshape(L, HALF)
        gpacked = attend_back(heads, mixed_heads, gheads, logs)
        return cross(gpacked.reshape(2, T, 3 * HALF), 1)

    x, packed, normed = rear_front(stream, mixed, full, par)
    mixed, kept = attention(packed)
    result, gmixed, gmiddle, middle, normed2, pre, active = turn(x, mixed, stream, full, par)
    gp = attention_back(kept, gmixed)
    e, gmixed, gmiddle, rear_sums, mlow, gpre = back_back(
        gp, gmiddle, x, stream, middle, pre, full, par
    )
    heads, mixed_heads, logs = kept
    gf, gd, gq, go, total, section_out, in_grad = tail(
        [
            e, active, normed2, gpre, heads, mixed_heads, logs, mixed, mlow, normed, gmiddle, x,
        ],
        gmixed, result, full, par, rear_sums,
    )
    strip = lax.dynamic_slice(total, (0, dp * 48), (8, 48))
    up = lax.dynamic_slice(total, (8 + dp // 4, (dp % 4) * 192), (1, 192))
    return (
        section_out[None],
        in_grad[None],
        gq,
        go,
        gf,
        gd,
        strip[None, :2],
        strip[None, 2:],
        up,
    )


def solution(mesh):
    in_specs = (
        P("dp", "seq", None),
        P("dp", "seq", None),
        P("section", "dp", None),
        P("section", "dp", None),
        P("section", "dp", None),
        P("section", "dp", None),
        P("section", None, "dp"),
        P("section", None, "dp"),
        P("section", "dp"),
    )
    out_specs = (
        P("section", "dp", "seq", None),
        P("section", "dp", "seq", None),
        P("section", "dp", None),
        P("section", "dp", None),
        P("section", "dp", None),
        P("section", "dp", None),
        P("section", None, "dp"),
        P("section", None, "dp"),
        P("section", "dp"),
    )
    return jax.shard_map(body, mesh=mesh, in_specs=in_specs, out_specs=out_specs, check_vma=False)
```

```python
import functools
import math

import jax
import jax.numpy as jnp
from jax import lax
from jax.experimental import pallas as pl
from jax.experimental.pallas import tpu as pltpu
from jax.sharding import PartitionSpec as P

MESH = pl.DeviceIdType.MESH
BF = jnp.bfloat16
F32 = jnp.float32
D = 768
T = 512
L = 1024
HALF = 384
ROWS = 608
HROWS = ROWS // 2
EPS = 1e-05
FC_ROWS = (112, 160, 208, 256)
QKV_ROWS = (16, 64, 304)
OUT_ROW = 352
SCALE = 0.125
C2 = SCALE * math.log2(math.e)
VLIM = 60 * 1024 * 1024
ANY = pl.BlockSpec(memory_space=pl.ANY)
VM = pl.BlockSpec(memory_space=pltpu.VMEM)


def where_am_i():
    core = lax.axis_index("section")
    z = lax.axis_index("seq")
    dp = lax.axis_index("dp")
    return core, z, dp // 4, dp % 4


def greet(peers):
    barrier = pltpu.get_barrier_semaphore()
    for peer in peers:
        pl.semaphore_signal(barrier, inc=1, device_id=peer, device_id_type=MESH)
    pl.semaphore_wait(barrier, len(peers))


def remote(src, dst, send, recv, peer):
    return pltpu.make_async_remote_copy(
        src_ref=src, dst_ref=dst, send_sem=send, recv_sem=recv, device_id=peer, device_id_type=MESH
    )


def comm_params(ident):
    return pltpu.CompilerParams(
        collective_id=ident, has_side_effects=True, vmem_limit_bytes=VLIM
    )


PIECES = ((0, 112), (112, 96), (208, 96))


def head_kernel(
    wq, wo, wf, wp, small, ins, cots,
    full, stream, par, mixed,
    shard, smalls, wqs, packed, normed, heads, omix,
    lsem, gs, gr, ssem, rsem, xs, xr, qsems, asem, psem,
):
    core, z, y, x = where_am_i()
    block = z % 2
    sib = 1 - core
    dp = y * 4 + x
    sibling = (sib, z, dp)
    first = core == 0
    count = len(PIECES)

    def along(axis, step):
        if axis == 0:
            return (core, z, y * 4 + (x + step) % 4)
        return (core, z, ((y + step) % 4) * 4 + x)

    @pl.when(core == block)
    def _():
        for h in range(2):
            for k in range(3):
                at = h * 3 + k
                row = QKV_ROWS[at // 2]
                shard[row : row + 48, (at % 2) * HALF : (at % 2 + 1) * HALF] = (
                    wq[0, :, k * D + h * HALF : k * D + (h + 1) * HALF]
                )
        shard[OUT_ROW : OUT_ROW + 48] = wo[0]
        for m in range(4):
            shard[FC_ROWS[m] : FC_ROWS[m] + 48] = wf[0, :, m * D : (m + 1) * D]
        shard[0:16] = small[...]
        shard[400:592] = wp[0]
        shard[592:608] = jnp.zeros((16, D), BF)

    peers = [sibling]
    for step in (1, 2, 3):
        peers += [along(0, step), along(1, step), (core, (z + step) % 4, dp)]
    greet(peers)

    def span(p, whose):
        at, rows = PIECES[p]
        return pl.ds(pl.multiple_of(whose * HROWS + at, 16), rows)

    def give(p):
        view = shard.at[span(p, sib)]
        return remote(view, view, gs.at[p], gr.at[p], sibling)

    @pl.when(core == block)
    def _():
        for p in range(count):
            give(p).start()

    quarter = pl.ds(pl.multiple_of((z % 2) * 256, 256), 256)
    sends_tokens = (z // 2) == core

    def send_tokens():
        for step in (1, 2, 3):
            to = (z + step) % 4
            for source, parity in ((ins, 0), (cots, 1)):

                @pl.when(sends_tokens & (to % 2 == parity))
                def _():
                    remote(
                        source.at[to // 2],
                        stream.at[quarter],
                        xs.at[step],
                        xr.at[z % 2],
                        (core, to, dp),
                    ).start()

        for source, parity in ((ins, 0), (cots, 1)):

            @pl.when(sends_tokens & (z % 2 == parity))
            def _():
                pltpu.make_async_copy(
                    source.at[z // 2], stream.at[quarter], lsem.at[count]
                ).start()

    def shard_at(p, axis, step, whose):
        rows = span(p, whose)
        if axis == 0:
            return full.at[y, (x + step) % 4, rows]
        return full.at[(y + step) % 4, x, rows]

    def line_at(p, axis, step, half, whose):
        rows = span(p, whose)
        if axis == 0:
            return full.at[pl.ds(2 * half, 2), (x + step) % 4, rows]
        return full.at[(y + step) % 4, pl.ds(2 * half, 2), rows]

    def send(p, slot, src, dst, to):
        remote(src, dst, ssem.at[p, slot], rsem.at[p, slot], to).start()

    def came(p, slot, land):
        remote(land, land, ssem.at[p, slot], rsem.at[p, slot], sibling).wait_recv()

    def own_shard(p, axis):
        return pltpu.make_async_copy(
            shard.at[span(p, core)], shard_at(p, axis, 0, core), lsem.at[p]
        )

    def begin(p, axis):
        @pl.when(core != block)
        def _():
            view = shard.at[span(p, core)]
            remote(view, view, gs.at[p], gr.at[p], sibling).wait_recv()

        view = shard.at[span(p, core)]
        land = shard_at(p, axis, 0, core)
        for k in (2, 1, 3):
            send(p, k, view, land, along(axis, k))
        send(p, 14, view, land, sibling)
        own_shard(p, axis).start()

    def lines(p, axis):
        own_shard(p, axis).wait()
        for k in (1, 3, 2):
            came(p, k, shard_at(p, axis, 4 - k, core))
        for half in (0, 1):
            for slot, step in ((4, 1), (6, 3)):
                view = line_at(p, 1 - axis, 0, half, core)
                send(p, slot + half, view, view, along(1 - axis, step))
        for k in (1, 3, 2):
            view = shard_at(p, axis, 4 - k, core)
            send(p, 14 + k, view, view, sibling)

    def forward(p, axis):
        for half, slot, step, to in ((0, 4, 3, 1), (1, 6, 1, 3), (1, 4, 3, 0), (0, 6, 1, 0)):
            land = line_at(p, 1 - axis, step, half, core)
            came(p, slot + half, land)
            if to:
                send(p, 8 + half, land, land, along(1 - axis, to))
            send(p, 14 + slot + half, land, land, sibling)

    def opposite(p, axis):
        for half in (0, 1):
            land = line_at(p, 1 - axis, 2, half, core)
            came(p, 8 + half, land)
            send(p, 22 + half, land, land, sibling)

    def passed_on(p, axis):
        came(p, 14, shard_at(p, 1 - axis, 0, sib))
        for k in (1, 3, 2):
            came(p, 14 + k, shard_at(p, 1 - axis, 4 - k, sib))
        for half, slot, step in ((0, 4, 3), (1, 6, 1), (1, 4, 3), (0, 6, 1)):
            came(p, 14 + slot + half, line_at(p, axis, step, half, sib))
        for half in (0, 1):
            came(p, 22 + half, line_at(p, axis, 2, half, sib))

    def sent(p, axis):
        for slot in (1, 2, 3, 14, 15, 16, 17):
            view = shard_at(p, axis, 0, core)
            remote(view, view, ssem.at[p, slot], rsem.at[p, slot], sibling).wait_send()
        for slot in (4, 5, 6, 7, 8, 9, 18, 19, 20, 21, 22, 23):
            view = line_at(p, axis, 0, 0, core)
            remote(view, view, ssem.at[p, slot], rsem.at[p, slot], sibling).wait_send()

    def both(*steps):
        @pl.when(first)
        def _():
            for step, p in steps:
                step(p, 0)

        @pl.when(jnp.logical_not(first))
        def _():
            for step, p in steps:
                step(p, 1)

    both((begin, 0))
    send_tokens()
    both(
        (begin, 1), (begin, 2), (lines, 0), (forward, 0), (lines, 1), (opposite, 0),
        (passed_on, 0),
    )

    fetches = [
        pltpu.make_async_copy(
            full.at[:, :, pl.ds(QKV_ROWS[m], 48)], wqs.at[m], qsems.at[m]
        )
        for m in range(3)
    ]
    fetches.append(pltpu.make_async_copy(full.at[:, :, pl.ds(0, 16)], smalls, qsems.at[3]))
    for fetch in reversed(fetches):
        fetch.start()

    @pl.when(sends_tokens)
    def _():
        pltpu.make_async_copy(ins.at[0], stream.at[quarter], lsem.at[count]).wait()

    for j in (0, 1):

        @pl.when(z != 2 * core + j)
        def _():
            land = stream.at[pl.ds(256 * j, 256)]
            remote(land, land, xs.at[0], xr.at[j], sibling).wait_recv()

    fetches[3].wait()
    total = smalls[0, 0].astype(F32)
    for k in range(1, 16):
        total = total + smalls[k // 4, k % 4].astype(F32)
    par[...] = total
    zero = jnp.zeros((1, HALF), F32)
    par[12:13, :HALF] = total[3:4, :HALF]
    par[12:13, HALF:] = zero
    par[13:14, :HALF] = total[4:5, :HALF]
    par[13:14, HALF:] = total[3:4, HALF:]
    par[14:15, :HALF] = zero
    par[14:15, HALF:] = total[4:5, HALF:]

    def need(m):
        fetches[m].wait()

    for i, at in enumerate(TILES):
        front_tile(at, nothing if i else need, stream, wqs, par, packed, normed)
        if i == 0:
            both((lines, 2), (forward, 1))

    out = remote(packed.at[sib], heads.at[token_rows(core)], asem.at[0], asem.at[1], sibling)
    back = remote(packed.at[0], heads.at[token_rows(sib)], asem.at[0], asem.at[1], sibling)
    keep = pltpu.make_async_copy(packed.at[core], heads.at[token_rows(core)], asem.at[2])
    out.start()
    keep.start()
    keep.wait()
    back.wait_recv()

    @pl.loop(0, 3)
    def _(pair):
        columns = part_columns(pair)
        narrow = pl.ds(pl.multiple_of(pair * 128, 128), 128)

        def put(at, value):
            omix[at, narrow] = value

        attend_pair(lambda name, rows: heads[rows, columns(name)], put, None)

        @pl.when(pair == 0)
        def _():
            both((opposite, 1), (forward, 2))

    m_out = remote(omix.at[token_rows(sib)], mixed.at[core], psem.at[0], psem.at[1], sibling)
    m_in = remote(omix.at[token_rows(core)], mixed.at[sib], psem.at[0], psem.at[1], sibling)
    m_own = pltpu.make_async_copy(omix.at[token_rows(core)], mixed.at[core], psem.at[2])
    m_out.start()
    m_own.start()
    both(
        (opposite, 2), (passed_on, 1), (passed_on, 2), (sent, 0), (sent, 1), (sent, 2),
    )
    m_own.wait()
    m_in.wait_recv()
    m_out.wait_send()
    out.wait_send()

    @pl.when(core == block)
    def _():
        for p in range(count):
            give(p).wait_send()

    @pl.when(sends_tokens)
    def _():
        for step in (1, 2, 3):
            remote(ins.at[0], stream.at[quarter], xs.at[step], xr.at[0], sibling).wait_send()


def head(wq, wo, wf, wp, small, ins, cots):
    dma = pltpu.SemaphoreType.DMA
    n = len(PIECES)
    return pl.pallas_call(
        head_kernel,
        name="head",
        out_shape=(
            jax.ShapeDtypeStruct((4, 4, ROWS, D), BF),
            jax.ShapeDtypeStruct((T, D), BF),
            jax.ShapeDtypeStruct((16, D), F32),
            jax.ShapeDtypeStruct((2, T, HALF), BF),
        ),
        in_specs=[VM] * 5 + [ANY] * 2,
        out_specs=(ANY, VM, VM, VM),
        scratch_shapes=[
            wide(ROWS),
            wide(4, 4, 16),
            wide(3, 4, 4, 48),
            pltpu.VMEM((2, T, 3 * HALF), BF),
            wide(T),
            pltpu.VMEM((L, 3 * HALF), BF),
            pltpu.VMEM((L, HALF), BF),
            dma((n + 1,)),
            dma((n,)),
            dma((n,)),
            dma((n, 24)),
            dma((n, 24)),
            dma((4,)),
            dma((2,)),
            dma((4,)),
            dma((3,)),
            dma((3,)),
        ],
        compiler_params=comm_params(0),
    )(wq, wo, wf, wp, small, ins, cots)


def dot(a, b):
    return jnp.dot(a, b, preferred_element_type=F32)


def dot_nt(a, b):
    return lax.dot_general(a, b, (((1,), (1,)), ((), ())), preferred_element_type=F32)


def dot_tn(a, b):
    return lax.dot_general(a, b, (((0,), (0,)), ((), ())), preferred_element_type=F32)


def normalized(v):
    centre = v - jnp.mean(v, axis=-1, keepdims=True)
    inv = lax.rsqrt(jnp.mean(centre * centre, axis=-1, keepdims=True) + EPS)
    return centre * inv, inv


def norm_back(grad, gain, unit, inv):
    g = grad * gain
    return inv * (
        g
        - jnp.mean(g, axis=-1, keepdims=True)
        - unit * jnp.mean(g * unit, axis=-1, keepdims=True)
    )


def matrix(ref, m):
    return ref[m].reshape(D, D)


class Fetch:
    def __init__(self, w, sems, parts):
        self.copies = []
        for at, (buffer, m, kind) in enumerate(parts):
            if kind is None:
                src = w.at[pl.ds(4 * m, 4), pl.ds(400, 192)]
            else:
                src = w.at[:, pl.ds(kind, 48)]
            self.copies.append(pltpu.make_async_copy(src, buffer.at[m], sems.at[at]))
        for copy in self.copies:
            copy.start()

    def need(self, at):
        self.copies[at].wait()


class Store:
    def __init__(self, sems):
        self.sems = sems
        self.copies = []

    def put(self, src, dst):
        copy = pltpu.make_async_copy(src, dst, self.sems.at[len(self.copies)])
        copy.start()
        self.copies.append(copy)

    def finish(self):
        for copy in self.copies:
            copy.wait()


def wide(*lead):
    return pltpu.VMEM((*lead, D), BF)


def local_params():
    return pltpu.CompilerParams(vmem_limit_bytes=VLIM)


TILES = (slice(0, 256), slice(256, 512))
SENT = tuple(slice(128 * i, 128 * i + 128) for i in range(4))
TAKEN = ((slice(0, 256), (0, 1)), (slice(256, 384), (2,)), (slice(384, 512), (3,)))


def front_tile(at, need, x, wq, par, packed, normed_out):
    unit, _ = normalized(x[at].astype(F32))
    normed = (unit * par[0:1] + par[2:3]).astype(BF)
    normed_out[at] = normed
    need(0)
    a = (dot(normed, matrix(wq, 0)) + par[12:13]).astype(BF)
    packed[0, at, :D] = a
    need(1)
    b = (dot(normed, matrix(wq, 1)) + par[13:14]).astype(BF)
    packed[0, at, D:] = b[:, :HALF]
    packed[1, at, :HALF] = b[:, HALF:]
    need(2)
    c = (dot(normed, matrix(wq, 2)) + par[14:15]).astype(BF)
    packed[1, at, HALF:] = c


def nothing(at):
    pass


def QKV_PARTS(wq):
    return [(wq, m, QKV_ROWS[m]) for m in range(3)]


QB = 256


def head_masks(ref_value):
    lane = lax.broadcasted_iota(jnp.int32, ref_value.shape, 1)
    zero = jnp.zeros_like(ref_value)
    return (
        jnp.where(lane < 64, ref_value, zero),
        jnp.where(lane >= 64, ref_value, zero),
    )


def masked_tail(v, fill):
    row = lax.broadcasted_iota(jnp.int32, (QB, QB), 0)
    keep = lax.broadcasted_iota(jnp.int32, (QB, QB), 1) <= row
    start = v.shape[1] - QB
    last = jnp.where(keep, v[:, start:], fill)
    return jnp.concatenate([v[:, :start], last], axis=1) if start else last


def attend_pair(get, put, put_logs):
    for i in range(L // QB):
        at = slice(i * QB, (i + 1) * QB)
        stop = (i + 1) * QB
        keys = get("k", slice(0, stop))
        queries = head_masks(get("q", at))
        values = head_masks(get("v", slice(0, stop)))
        total = None
        saved = []
        for h in range(2):
            s = masked_tail(dot_nt(queries[h], keys), -1e30)
            peak = jnp.max(s, axis=-1, keepdims=True)
            p = jnp.exp2((s - peak) * C2)
            norm = jnp.sum(p, axis=-1, keepdims=True)
            o = dot(p.astype(BF), values[h]) * (1.0 / norm)
            total = o if total is None else total + o
            saved.append(peak * C2 + jnp.log2(norm))
        put(at, total.astype(BF))
        if put_logs:
            lane = lax.broadcasted_iota(jnp.int32, (QB, 128), 1)
            put_logs(at, jnp.where(lane < 64, saved[0], saved[1]))


def token_rows(c):
    return pl.ds(pl.multiple_of(c * T, T), T)


def attention_kernel(packed, mixed, heads, omix, logs, sems):
    core, z, y, x = where_am_i()
    sib = 1 - core
    sibling = (sib, z, y * 4 + x)
    keep = pltpu.make_async_copy(packed.at[core], heads.at[token_rows(core)], sems.at[2])
    keep.start()
    greet([sibling])
    out = remote(packed.at[sib], heads.at[token_rows(core)], sems.at[0], sems.at[1], sibling)
    back = remote(packed.at[0], heads.at[token_rows(sib)], sems.at[0], sems.at[1], sibling)
    out.start()
    keep.wait()
    back.wait_recv()

    @pl.loop(0, 3)
    def _(pair):
        columns = part_columns(pair)
        narrow = pl.ds(pl.multiple_of(pair * 128, 128), 128)

        def put(at, value):
            omix[at, narrow] = value

        def put_logs(at, value):
            logs[pair, at] = value

        attend_pair(lambda name, rows: heads[rows, columns(name)], put, put_logs)

    m_out = remote(omix.at[token_rows(sib)], mixed.at[core], sems.at[3], sems.at[4], sibling)
    m_in = remote(omix.at[token_rows(core)], mixed.at[sib], sems.at[3], sems.at[4], sibling)
    m_own = pltpu.make_async_copy(omix.at[token_rows(core)], mixed.at[core], sems.at[5])
    m_out.start()
    m_own.start()
    m_own.wait()
    m_in.wait_recv()
    out.wait_send()
    m_out.wait_send()


def attention(packed):
    return pl.pallas_call(
        attention_kernel,
        name="attention",
        out_shape=(
            jax.ShapeDtypeStruct((2, T, HALF), BF),
            jax.ShapeDtypeStruct((L, 3 * HALF), BF),
            jax.ShapeDtypeStruct((L, HALF), BF),
            jax.ShapeDtypeStruct((3, L, 128), F32),
        ),
        in_specs=[ANY],
        out_specs=(VM,) * 4,
        scratch_shapes=[pltpu.SemaphoreType.DMA((6,))],
        compiler_params=comm_params(1),
    )(packed)


def attend_back_pair(get, put, logs_at, dk, dv):
    dk[...] = jnp.zeros_like(dk)
    dv[...] = jnp.zeros_like(dv)
    for i in range(L // QB):
        at = slice(i * QB, (i + 1) * QB)
        stop = (i + 1) * QB
        keys = get("k", slice(0, stop))
        values = get("v", slice(0, stop))
        keys_of = head_masks(keys)
        queries = head_masks(get("q", at))
        top = get("do", at)
        tops = head_masks(top)
        inner = head_masks(top.astype(F32) * get("o", at).astype(F32))
        dq = None
        for h in range(2):
            s = dot_nt(queries[h], keys)
            p = masked_tail(jnp.exp2(s * C2 - logs_at(at, h)), 0.0)
            gw = dot_nt(tops[h], values)
            delta = jnp.sum(inner[h], axis=-1, keepdims=True)
            ds = (p * (gw - delta)).astype(BF)
            part = dot(ds, keys_of[h])
            dq = part if dq is None else dq + part
            dk[:stop] += dot_tn(ds, queries[h])
            dv[:stop] += dot_tn(p.astype(BF), tops[h])
        put("q", at, (dq * SCALE).astype(BF))
    put("k", slice(0, L), (dk[...] * SCALE).astype(BF))
    put("v", slice(0, L), dv[...].astype(BF))


def part_columns(pair):
    def columns(name):
        return pl.ds(pl.multiple_of("qkv".index(name) * HALF + pair * 128, 128), 128)

    return columns


def loop_pairs_back(heads, omix, gheads, logs, dk, dv, after=None):
    @pl.loop(0, 3)
    def _(pair):
        columns = part_columns(pair)
        narrow = pl.ds(pl.multiple_of(pair * 128, 128), 128)

        def get(name, rows):
            if name == "o":
                return omix[rows, narrow]
            if name == "do":
                half, start = rows.start // T, rows.start % T
                return gheads[half, start : start + QB, narrow]
            return heads[rows, columns(name)]

        def put(name, rows, value):
            heads[rows, columns(name)] = value

        attend_back_pair(
            get, put, lambda at, h: logs[pair, at, 64 * h : 64 * h + 1], dk, dv
        )
        if after:
            after(pair)


def attention_back_kernel(
    heads_in, omix_in, logs_in, gmixed, gp, heads, omix, logs, gheads, dk, dv, sems
):
    core, z, y, x = where_am_i()
    sib = 1 - core
    sibling = (sib, z, y * 4 + x)
    loads = [
        pltpu.make_async_copy(gmixed.at[core], gheads.at[core], sems.at[2]),
        pltpu.make_async_copy(heads_in, heads, sems.at[3]),
        pltpu.make_async_copy(omix_in, omix, sems.at[4]),
        pltpu.make_async_copy(logs_in, logs, sems.at[5]),
    ]
    for load in loads:
        load.start()
    greet([sibling])
    out = remote(gmixed.at[sib], gheads.at[core], sems.at[0], sems.at[1], sibling)
    back = remote(gmixed.at[0], gheads.at[sib], sems.at[0], sems.at[1], sibling)
    out.start()
    for load in loads:
        load.wait()
    back.wait_recv()
    loop_pairs_back(heads, omix, gheads, logs, dk, dv)
    g_out = remote(heads.at[token_rows(sib)], gp.at[core], sems.at[6], sems.at[7], sibling)
    g_in = remote(heads.at[token_rows(core)], gp.at[sib], sems.at[6], sems.at[7], sibling)
    g_own = pltpu.make_async_copy(heads.at[token_rows(core)], gp.at[core], sems.at[8])
    g_out.start()
    g_own.start()
    g_own.wait()
    g_in.wait_recv()
    out.wait_send()
    g_out.wait_send()


def attention_back(heads, omix, logs, gmixed):
    return pl.pallas_call(
        attention_back_kernel,
        name="attention_back",
        out_shape=jax.ShapeDtypeStruct((2, T, 3 * HALF), BF),
        in_specs=[ANY] * 4,
        out_specs=VM,
        scratch_shapes=[
            pltpu.VMEM((L, 3 * HALF), BF),
            pltpu.VMEM((L, HALF), BF),
            pltpu.VMEM((3, L, 128), F32),
            pltpu.VMEM((2, T, HALF), BF),
            pltpu.VMEM((L, 128), F32),
            pltpu.VMEM((L, 128), F32),
            pltpu.SemaphoreType.DMA((9,)),
        ],
        compiler_params=comm_params(2),
    )(heads, omix, logs, gmixed)


REAR_SCRATCH = [
    wide(1, 16, 48),
    wide(4, 16, 48),
    wide(4, 4, 192),
    pltpu.SemaphoreType.DMA((9,)),
]


def gelu(v):
    return 0.5 * v * (1.0 + jnp.tanh(0.79788456 * (v + 0.044715 * v * v * v)))


def gelu_slope(v):
    square = v * v
    t = jnp.tanh(0.79788456 * v * (1.0 + 0.044715 * square))
    return 0.5 * (1.0 + t) + 0.5 * v * (1.0 - t * t) * 0.79788456 * (
        1.0 + 3 * 0.044715 * square
    )


def forward_parts(wo, wf, wp):
    parts = [(wo, 0, OUT_ROW)]
    for m in range(4):
        parts += [(wf, m, FC_ROWS[m]), (wp, m, None)]
    return parts


def backward_parts(wo, wf, wp):
    parts = []
    for m in range(4):
        parts += [(wp, m, None), (wf, m, FC_ROWS[m])]
    return parts + [(wo, 0, OUT_ROW)]


def rear_tile(at, need, x, mixed, wo, wf, wp, par, result, kept, store):
    mix = jnp.concatenate([mixed[0, at], mixed[1, at]], axis=1)
    need(0)
    middle = x[at].astype(F32) + (dot(mix, matrix(wo, 0)) + par[5:6])
    unit, _ = normalized(middle)
    normed = (unit * par[1:2] + par[6:7]).astype(BF)
    if kept:
        kept[0][at] = middle
        kept[1][at] = normed
        store(0, at, None)
        store(1, at, None)
    total = middle + par[7:8]
    for m in range(4):
        need(1 + 2 * m)
        pre = dot(normed, matrix(wf, m)) + par[8 + m : 9 + m]
        active = gelu(pre).astype(BF)
        if kept:
            cols = slice(m * D, (m + 1) * D)
            kept[2][at, cols] = pre.astype(BF)
            kept[3][at, cols] = active
            store(2, at, cols)
            store(3, at, cols)
        need(2 + 2 * m)
        total = total + dot(active, matrix(wp, m))
    result[at] = total.astype(BF)


def column_sum(v):
    return jnp.sum(v, axis=0, keepdims=True)


def adder(sums, i):
    def add(row, v):
        if i:
            sums[row : row + 1] += column_sum(v)
        else:
            sums[row : row + 1] = column_sum(v)

    return add


def rear_back_tile(at, need, e, middle, pre, wo, wf, wp, par, gmixed, gmiddle, full):
    if full:
        add, mlow, gpre, store = full
    top = e[at]
    gnorm = None
    for m in range(4):
        cols = slice(m * D, (m + 1) * D)
        need(2 * m)
        gact = dot_nt(top, matrix(wp, m))
        low = (gact * gelu_slope(pre[at, cols].astype(F32))).astype(BF)
        if full:
            gpre[at, cols] = low
            store(0, at, cols)
            add(4 + m, low.astype(F32))
        need(2 * m + 1)
        part = dot_nt(low, matrix(wf, m))
        gnorm = part if gnorm is None else gnorm + part
    unit, inv = normalized(middle[at])
    top_wide = top.astype(F32)
    gmid = top_wide + norm_back(gnorm, par[1:2], unit, inv)
    gmiddle[at] = gmid
    low = gmid.astype(BF)
    if full:
        add(0, top_wide)
        add(1, gnorm * unit)
        add(2, gnorm)
        add(3, gmid)
        mlow[at] = low
        store(1, at, None)
    need(8)
    gm = dot_nt(low, matrix(wo, 0)).astype(BF)
    gmixed[0, at] = gm[:, :HALF]
    gmixed[1, at] = gm[:, HALF:]


def front_back_tile(at, need, gp, gmiddle, x, wq, par, grad, add):
    gnorm = None
    for m, piece in enumerate(packed_pieces(gp, at)):
        if add:
            add(2 + m, piece.astype(F32))
        need(m)
        part = dot_nt(piece, matrix(wq, m))
        gnorm = part if gnorm is None else gnorm + part
    unit, inv = normalized(x[at].astype(F32))
    if add:
        add(0, gnorm * unit)
        add(1, gnorm)
    grad[at] = (gmiddle[at] + norm_back(gnorm, par[0:1], unit, inv)).astype(BF)


def partner_of():
    core, z, y, x = where_am_i()
    return z % 2, (core, z + 1 - 2 * (z % 2), y * 4 + x)


def rear_front_kernel(
    x, mixed, w, par, x2, packed, normed, wo, wf, wp, sems, wq, qsems, res, ssem, rsem
):
    block, partner = partner_of()
    fetch = Fetch(w, sems, forward_parts(wo, wf, wp))
    fetch_q = Fetch(w, qsems, QKV_PARTS(wq))
    greet([partner])

    def hand(i):
        rows = pl.ds(128 * i, 128)
        return remote(res.at[rows], x2.at[rows], ssem.at[i], rsem.at[i], partner)

    @pl.when(block == 0)
    def _():
        for i, at in enumerate(SENT):
            rear_tile(
                at, nothing if i else fetch.need, x, mixed, wo, wf, wp, par, res, None, None
            )
            hand(i).start()
        x2[...] = x[...]

    @pl.when(block == 1)
    def _():
        for k in range(9):
            fetch.need(k)

    for k in range(3):
        fetch_q.need(k)
    for at, hands in TAKEN:
        for i in hands:
            pl.when(block == 1)(hand(i).wait_recv)
        front_tile(at, nothing, x2, wq, par, packed, normed)

    @pl.when(block == 0)
    def _():
        for i in range(4):
            hand(i).wait_send()


def rear_front(x, mixed, w, par):
    dma = pltpu.SemaphoreType.DMA
    return pl.pallas_call(
        rear_front_kernel,
        name="rear_hand_front",
        out_shape=(
            jax.ShapeDtypeStruct((T, D), BF),
            jax.ShapeDtypeStruct((2, T, 3 * HALF), BF),
            jax.ShapeDtypeStruct((T, D), BF),
        ),
        in_specs=[VM, VM, ANY, VM],
        out_specs=(VM, VM, VM),
        scratch_shapes=REAR_SCRATCH
        + [wide(3, 16, 48), dma((3,)), wide(T), dma((4,)), dma((4,))],
        compiler_params=comm_params(3),
    )(x, mixed, w, par)


def turn_kernel(
    x, mixed, e, w, par, result, gmixed, gmiddle, middle_out, normed_out, pre_out, active_out,
    wo, wf, wp, sems, middle, normed, pre, active, osems,
):
    fetch = Fetch(w, sems, forward_parts(wo, wf, wp))
    store = Store(osems)
    kept = (middle, normed, pre, active)
    outs = (middle_out, normed_out, pre_out, active_out)

    def put(n, at, cols):
        rows = pl.ds(at.start, at.stop - at.start)
        if cols is None:
            store.put(kept[n].at[rows], outs[n].at[rows])
        else:
            lanes = pl.ds(cols.start, D)
            store.put(kept[n].at[rows, lanes], outs[n].at[rows, lanes])

    for i, at in enumerate(TILES):
        rear_tile(
            at, nothing if i else fetch.need, x, mixed, wo, wf, wp, par, result, kept, put
        )
    for at in TILES:
        rear_back_tile(at, nothing, e, middle, pre, wo, wf, wp, par, gmixed, gmiddle, None)
    store.finish()


def turn(x, mixed, e, w, par):
    kept = [((T, D), F32), ((T, D), BF), ((T, 4 * D), BF), ((T, 4 * D), BF)]
    outs = [((T, D), BF), ((2, T, HALF), BF), ((T, D), F32)] + kept
    return pl.pallas_call(
        turn_kernel,
        name="turn",
        out_shape=tuple(jax.ShapeDtypeStruct(s, t) for s, t in outs),
        in_specs=[VM, VM, VM, ANY, VM],
        out_specs=(VM, VM, VM, ANY, ANY, ANY, ANY),
        scratch_shapes=REAR_SCRATCH
        + [pltpu.VMEM(s, t) for s, t in kept]
        + [pltpu.SemaphoreType.DMA((20,))],
        compiler_params=local_params(),
    )(x, mixed, e, w, par)


def back_back_kernel(
    gp, gmid_in, x, stream, middle, pre_in, w, par,
    e, gmixed, gmiddle, sums, mlow_out, gpre_out,
    wo, wf, wp, sems, wq, qsems, res, ssem, rsem, pre, mlow, gpre, psem, osems,
):
    block, partner = partner_of()
    fetch_q = Fetch(w, qsems, QKV_PARTS(wq))
    fetch = Fetch(w, sems, backward_parts(wo, wf, wp))
    load = pltpu.make_async_copy(pre_in, pre, psem)
    load.start()
    greet([partner])

    def hand(i):
        rows = pl.ds(128 * i, 128)
        return remote(res.at[rows], e.at[rows], ssem.at[i], rsem.at[i], partner)

    for k in range(3):
        fetch_q.need(k)

    @pl.when(block == 1)
    def _():
        for i, at in enumerate(SENT):
            front_back_tile(at, nothing, gp, gmid_in, x, wq, par, res, None)
            hand(i).start()
        e[...] = stream[...]

    for k in range(9):
        fetch.need(k)
    load.wait()
    store = Store(osems)

    def put(n, at, cols):
        rows = pl.ds(at.start, at.stop - at.start)
        if cols is None:
            store.put(mlow.at[rows], mlow_out.at[rows])
        else:
            lanes = pl.ds(cols.start, D)
            store.put(gpre.at[rows, lanes], gpre_out.at[rows, lanes])

    for i, (at, hands) in enumerate(TAKEN):
        for k in hands:
            pl.when(block == 0)(hand(k).wait_recv)
        rear_back_tile(
            at, nothing, e, middle, pre, wo, wf, wp, par, gmixed, gmiddle,
            (adder(sums, i), mlow, gpre, put),
        )

    @pl.when(block == 1)
    def _():
        for i in range(4):
            hand(i).wait_send()

    store.finish()


def back_back(gp, gmid, x, stream, middle, pre, w, par):
    dma = pltpu.SemaphoreType.DMA
    return pl.pallas_call(
        back_back_kernel,
        name="front_back_hand_rear_back",
        out_shape=(
            jax.ShapeDtypeStruct((T, D), BF),
            jax.ShapeDtypeStruct((2, T, HALF), BF),
            jax.ShapeDtypeStruct((T, D), F32),
            jax.ShapeDtypeStruct((8, D), F32),
            jax.ShapeDtypeStruct((T, D), BF),
            jax.ShapeDtypeStruct((T, 4 * D), BF),
        ),
        in_specs=[VM, VM, VM, VM, VM, ANY, ANY, VM],
        out_specs=(VM, VM, VM, VM, ANY, ANY),
        scratch_shapes=REAR_SCRATCH
        + [wide(3, 16, 48), dma((3,)), wide(T), dma((4,)), dma((4,))]
        + [pltpu.VMEM((T, 4 * D), BF), wide(T), pltpu.VMEM((T, 4 * D), BF)]
        + [dma, dma((15,))],
        compiler_params=comm_params(4),
    )(gp, gmid, x, stream, middle, pre, w, par)


def packed_pieces(gp, at=slice(None)):
    return (
        gp[0, at, :D],
        jnp.concatenate([gp[0, at, D:], gp[1, at, :HALF]], axis=1),
        gp[1, at, HALF:],
    )


def rows_of(stage):
    return pl.ds(*stage)


class Reducer:
    def __init__(self, stages, buffers, sems):
        self.stages = stages
        self.own, self.r0, self.r1, self.r2, self.s1, self.s2, self.r3 = buffers
        self.s1s, self.s1r, self.s2s, self.s2r, self.s3s, self.s3r, self.ks = sems
        self.core, self.z, y, x = where_am_i()
        self.x, self.y = x, y
        self.dp = y * 4 + x
        self.block = self.z % 2
        self.seq = self.z // 2
        self.first = self.core == 0
        self.sibling = (1 - self.core, self.z, self.dp)
        self.line = jnp.where(self.first, y, x)
        self.place = jnp.where(self.first, x, y)

    def on_line(self, step):
        to = (self.line + step) % 4
        return (self.core, self.z, jnp.where(self.first, to * 4 + self.x, self.y * 4 + to))

    def on_place(self, step):
        to = (self.place + step) % 4
        return (self.core, self.z, jnp.where(self.first, self.y * 4 + to, to * 4 + self.x))

    def peers(self):
        found = [self.sibling]
        for step in (1, 2, 3):
            found += [self.on_line(step), self.on_place(step)]
            for k in (0, 1):
                found.append((k, (self.z + step) % 4, self.dp))
        return found

    def over_cores(self, p):
        own, r0, rows = self.own, self.r0, rows_of(self.stages[p])

        @pl.loop(0, 16)
        def _(i):
            a = own[i // 4, i % 4, rows].astype(F32)
            b = r0[i // 4, i % 4, rows].astype(F32)
            own[i // 4, i % 4, rows] = (a + b).astype(BF)

        for step in (2, 1, 3):
            remote(
                own.at[(self.line + step) % 4, :, rows],
                self.r1.at[step - 1, :, rows],
                self.s1s.at[p, step],
                self.s1r.at[p, step],
                self.on_line(step),
            ).start()

    def over_lines(self, p):
        own, r1, s1, rows = self.own, self.r1, self.s1, rows_of(self.stages[p])
        line = self.line
        for step in (1, 3, 2):
            remote(
                own.at[0, :, rows],
                r1.at[step - 1, :, rows],
                self.s1s.at[p, step],
                self.s1r.at[p, step],
                self.sibling,
            ).wait()

        @pl.loop(0, 4)
        def _(i):
            s1[i, rows] = (
                (own[line, i, rows].astype(F32) + r1[0, i, rows].astype(F32))
                + (r1[1, i, rows].astype(F32) + r1[2, i, rows].astype(F32))
            ).astype(BF)

        for step in (2, 1, 3):
            remote(
                s1.at[(self.place + step) % 4, rows],
                self.r2.at[step - 1, rows],
                self.s2s.at[p, step],
                self.s2r.at[p, step],
                self.on_place(step),
            ).start()

    def along_z(self, p, step):
        rows = rows_of(self.stages[p])
        return remote(
            self.s2.at[rows],
            self.r3.at[self.core, self.seq, rows],
            self.s3s.at[p, step],
            self.s3r.at[p, self.core, self.seq],
            (self.block, (self.z + step) % 4, self.dp),
        )

    def to_sibling(self, p):
        rows = rows_of(self.stages[p])
        return remote(
            self.s2.at[rows],
            self.r3.at[self.core, self.seq, rows],
            self.s3s.at[p, 0],
            self.s3r.at[p, self.core, self.seq],
            self.sibling,
        )

    def keep_sum(self, p):
        rows = rows_of(self.stages[p])
        return pltpu.make_async_copy(
            self.s2.at[rows], self.r3.at[self.core, self.seq, rows], self.ks.at[p]
        )

    def over_places(self, p):
        s1, r2, rows = self.s1, self.r2, rows_of(self.stages[p])
        for step in (1, 3, 2):
            remote(
                s1.at[0, rows],
                r2.at[step - 1, rows],
                self.s2s.at[p, step],
                self.s2r.at[p, step],
                self.sibling,
            ).wait()
        self.s2[rows] = (
            (s1[self.place, rows].astype(F32) + r2[0, rows].astype(F32))
            + (r2[1, rows].astype(F32) + r2[2, rows].astype(F32))
        ).astype(BF)
        for step in (2, 1, 3):
            self.along_z(p, step).start()
        pl.when(self.core == self.block)(self.keep_sum(p).start)
        pl.when(self.core != self.block)(self.to_sibling(p).start)

    def finish(self, p):
        for step in (1, 2, 3):
            self.along_z(p, step).wait_send()
        pl.when(self.core == self.block)(self.keep_sum(p).wait)
        pl.when(self.core != self.block)(self.to_sibling(p).wait_send)
        rows = rows_of(self.stages[p])
        for c in (0, 1):
            for s in (0, 1):
                here = (self.core == self.block) & (self.core == c) & (self.seq == s)
                land = self.r3.at[c, s, rows]

                @pl.when(jnp.logical_not(here))
                def _():
                    remote(
                        land, land, self.s3s.at[p, 0], self.s3r.at[p, c, s], self.sibling
                    ).wait_recv()

    def total(self, c, p):
        rows = rows_of(self.stages[p])
        return self.r3[c, 0, rows].astype(F32) + self.r3[c, 1, rows].astype(F32)


def reducer_buffers(rows):
    return [
        pltpu.VMEM((4, 4, rows, D), BF),
        pltpu.VMEM((4, 4, rows, D), BF),
        pltpu.VMEM((3, 4, rows, D), BF),
        pltpu.VMEM((3, rows, D), BF),
        pltpu.VMEM((4, rows, D), BF),
        pltpu.VMEM((rows, D), BF),
        pltpu.VMEM((2, 2, rows, D), BF),
    ]


def reducer_sems(count):
    dma = pltpu.SemaphoreType.DMA
    return [dma((count, 4))] * 5 + [dma((count, 2, 2)), dma((count,))]


REAR_STAGES = ((0, 48), (48, 48), (96, 48), (144, 48), (192, 32))
REAR_ROWS = 224


def tail_kernel(*refs):
    sources, refs = refs[:12], refs[12:]
    gmixed, result, w, par, rear_sums = refs[:5]
    gf, gd, gq, go, gsmall, out_a, out_b = refs[5:12]
    loaded, refs = refs[12:24], refs[24:]
    gheads, gp, wq, snd, grad, fsums, dk, dv = refs[:8]
    buffers, refs = refs[8:15], refs[15:]
    late_buffers, refs = (refs[0], buffers[1]) + refs[1:6], refs[6:]
    late_own = late_buffers[0]
    sems, refs = refs[:7], refs[7:]
    late_sems, refs = refs[:7], refs[7:]
    lsem, qsems, xsem, s0s, s0r, l0s, l0r, os, orr, ol = refs
    e, active, normed2, gpre, heads, omix, logs, mixed, mlow, normed, gmid, x = loaded
    own, r0 = buffers[0], buffers[1]

    copies = [
        pltpu.make_async_copy(src, dst, lsem.at[k])
        for k, (src, dst) in enumerate(zip(sources, loaded))
    ]
    for copy in copies:
        copy.start()
    fetch = Fetch(w, qsems, QKV_PARTS(wq))
    reducer = Reducer(REAR_STAGES, buffers, sems)
    late = Reducer(FRONT_STAGES, late_buffers, late_sems)
    core, sibling, first = reducer.core, reducer.sibling, reducer.first
    z, dp, block, seq = reducer.z, reducer.dp, reducer.block, reducer.seq
    greet(reducer.peers())

    def outputs(j, n):
        src, dst = ((result, out_a), (grad, out_b))[n]
        here = (core == block) & (z == 2 * core + j)
        view = src.at[pl.ds(256 * j, 256)]
        keep = pltpu.make_async_copy(view, dst.at[seq], ol.at[n])
        give = remote(
            view, dst.at[seq], os.at[2 * j + n], orr.at[seq, n], (block, 2 * core + j, dp)
        )
        return here, keep, give

    def send_output(j, n):
        here, keep, send = outputs(j, n)
        pl.when(here)(keep.start)
        pl.when(jnp.logical_not(here))(send.start)

    for j in (0, 1):
        send_output(j, 0)

    top_out = remote(gmixed.at[1 - core], gheads.at[core], xsem.at[0], xsem.at[1], sibling)
    top_in = remote(gmixed.at[0], gheads.at[1 - core], xsem.at[0], xsem.at[1], sibling)
    top_own = pltpu.make_async_copy(gmixed.at[core], gheads.at[core], xsem.at[2])
    top_out.start()
    top_own.start()

    def hidden_out(m):
        value = dot_tn(active[:, m * D : (m + 1) * D], e[...])
        return value.astype(BF).reshape(4, 192, D)

    def hidden_in(m):
        value = dot_tn(normed2[...], gpre[:, m * D : (m + 1) * D])
        return value.astype(BF).reshape(4, 4, 48, D)

    def out_grad():
        mix = jnp.concatenate([mixed[0], mixed[1]], axis=1)
        return dot_tn(mix, mlow[...]).astype(BF).reshape(4, 4, 48, D)

    last = pl.ds(192, 32)

    def give_out(m):
        return remote(
            snd.at[m, :, pl.ds(0, 192)], r0.at[:, m, pl.ds(0, 192)], s0s.at[m], s0r.at[m], sibling
        )

    def give_last_out():
        for k in range(4):
            remote(
                snd.at[k, :, last], r0.at[:, k, last], s0s.at[4 + k], s0r.at[4 + k], sibling
            ).start()

    def give_last_in():
        for k in range(4):
            remote(
                snd.at[k, :, last], r0.at[k, :, last], s0s.at[4 + k], s0r.at[4 + k], sibling
            ).start()

    def last_wait(side):
        for k in range(4):
            copy = remote(
                snd.at[k, :, last], r0.at[k, :, last], s0s.at[4 + k], s0r.at[4 + k], sibling
            )
            copy.wait_send() if side == "sent" else copy.wait_recv()

    zeros = jnp.zeros((4, 4, 16, D), BF)

    def give_in(m):
        rows = pl.ds(m * 48, 48)
        return remote(
            snd.at[:, :, rows], r0.at[:, :, rows], s0s.at[m], s0r.at[m], sibling
        )

    for k in (0, 1, 2, 3, 7, 8):
        copies[k].wait()

    @pl.when(first)
    def _():
        value = out_grad()
        snd[:, :, 192:224] = value[:, :, 16:48]
        give_last_out()
        own[:, :, 192:208] = value[:, :, :16]
        own[:, :, 208:224] = zeros
        for m in range(4):
            snd[m, :, :192] = hidden_out(m)
            give_out(m).start()
        for m in range(4):
            own[:, :, m * 48 : (m + 1) * 48] = hidden_in(m)
            give_in(m).wait_recv()
            reducer.over_cores(m)
        last_wait("came")
        reducer.over_cores(4)

    @pl.when(jnp.logical_not(first))
    def _():
        value = out_grad()
        snd[:, :, 192:208] = value[:, :, :16]
        snd[:, :, 208:224] = zeros
        give_last_in()
        for k in range(4):
            own[:, k, 192:224] = value[k, :, 16:48]
        for m in range(4):
            snd[:, :, m * 48 : (m + 1) * 48] = hidden_in(m)
            give_in(m).start()
        for m in range(4):
            own[:, m, :192] = hidden_out(m)
        for m in range(4):
            give_out(m).wait_recv()
        last_wait("came")
        for m in range(5):
            reducer.over_cores(m)

    top_own.wait()
    top_in.wait_recv()
    for k in (4, 5, 6, 9, 10, 11):
        copies[k].wait()

    def progress(pair):
        @pl.when(pair == 1)
        def _():
            reducer.over_lines(0)

    loop_pairs_back(heads, omix, gheads, logs, dk, dv, progress)

    def half_rows(c):
        return heads.at[pl.ds(pl.multiple_of(c * T, T), T)]

    gp_out = remote(half_rows(1 - core), gp.at[core], xsem.at[3], xsem.at[4], sibling)
    gp_in = remote(half_rows(core), gp.at[1 - core], xsem.at[3], xsem.at[4], sibling)
    gp_own = pltpu.make_async_copy(half_rows(core), gp.at[core], xsem.at[5])
    gp_out.start()
    gp_own.start()
    reducer.over_lines(1)
    reducer.over_places(0)
    for k in range(3):
        fetch.need(k)
    gp_own.wait()
    gp_in.wait_recv()

    @pl.when(first)
    def _():
        for m in range(4):
            give_out(m).wait_send()

    @pl.when(jnp.logical_not(first))
    def _():
        for m in range(4):
            give_in(m).wait_send()

    last_wait("sent")

    def packed_grad(m):
        piece = packed_pieces(gp)[m]
        return dot_tn(normed[...], piece).astype(BF).reshape(4, 4, 48, D)

    def give_late(p, k):
        rows = rows_of(FRONT_STAGES[p])
        return rows, snd.at[k, :, rows], l0s.at[p, k], l0r.at[p, k]

    def give_late_0(p, k):
        rows, src, ss, rs = give_late(p, k)
        return remote(src, r0.at[:, k, rows], ss, rs, sibling)

    def give_late_1(p, k):
        rows, src, ss, rs = give_late(p, k)
        return remote(src, r0.at[k, :, rows], ss, rs, sibling)

    def fill(dst, swapped, at, value):
        for k in range(4):
            if swapped:
                dst[:, k, at : at + value.shape[2]] = value[k]
            else:
                dst[k, :, at : at + value.shape[2]] = value[k]

    @pl.when(first)
    def _():
        fill(snd, False, 0, packed_grad(2))
        for k in range(4):
            give_late_0(0, k).start()
        value = packed_grad(1)
        fill(snd, False, 48, value[:, :, 16:48])
        for k in range(4):
            give_late_0(1, k).start()
            give_late_0(2, k).start()
        fill(late_own, False, 0, packed_grad(0))
        fill(late_own, False, 48, value[:, :, :16])

    @pl.when(jnp.logical_not(first))
    def _():
        fill(snd, False, 0, packed_grad(0))
        for k in range(4):
            give_late_1(0, k).start()
        value = packed_grad(1)
        fill(snd, False, 48, value[:, :, :16])
        for k in range(4):
            give_late_1(1, k).start()
        fill(late_own, True, 0, packed_grad(2))
        fill(late_own, True, 48, value[:, :, 16:48])

    def late_cores(p):
        for k in range(4):
            give_late_1(p, k).wait()
        late.over_cores(p)

    late_cores(0)
    late_cores(1)
    for i, at in enumerate(TILES):
        front_back_tile(at, nothing, gp, gmid, x, wq, par, grad, adder(fsums, i))
        send_output(i, 1)
        reducer.over_lines(2 + i)
        reducer.over_places(1 + i)

    zero = jnp.zeros((1, D), F32)
    small = jnp.concatenate(
        [
            fsums[0:1],
            rear_sums[1:2],
            fsums[1:2],
            zero,
            zero,
            rear_sums[3:4],
            rear_sums[2:3],
            rear_sums[0:1],
            rear_sums[4:8],
            fsums[2:5],
            zero,
        ],
        0,
    ).astype(BF)

    smalls = jnp.broadcast_to(small[None, None], (4, 4, 16, D))

    @pl.when(first)
    def _():
        fill(late_own, False, 64, smalls)

    @pl.when(jnp.logical_not(first))
    def _():
        fill(snd, False, 64, smalls)
        for k in range(4):
            give_late_1(2, k).start()

    late_cores(2)
    reducer.over_lines(4)
    reducer.over_places(3)
    late.over_lines(0)
    late.over_lines(1)
    reducer.over_places(4)
    late.over_places(0)
    late.over_places(1)
    late.over_lines(2)
    late.over_places(2)
    for m in range(4):
        reducer.finish(m)
        gf[0, :, m * D : (m + 1) * D] = reducer.total(0, m)
        gd[0, m * 48 : (m + 1) * 48] = reducer.total(1, m)
    reducer.finish(4)
    go[0, :16] = reducer.total(0, 4)[:16]
    go[0, 16:] = reducer.total(1, 4)
    for p in range(3):
        late.finish(p)

    def put(m, value):
        for side in (0, 1):
            h, k = (2 * m + side) // 3, (2 * m + side) % 3
            gq[0, :, k * D + h * HALF : k * D + (h + 1) * HALF] = value[
                :, side * HALF : (side + 1) * HALF
            ]

    put(0, late.total(0, 0))
    put(2, late.total(1, 0))
    put(1, jnp.concatenate([late.total(0, 1), late.total(1, 1), late.total(1, 2)], axis=0))
    small = late.total(0, 2)
    gsmall[...] = small
    gsmall[3:4, :HALF] = small[12:13, :HALF]
    gsmall[3:4, HALF:] = small[13:14, HALF:]
    gsmall[4:5, :HALF] = small[13:14, :HALF]
    gsmall[4:5, HALF:] = small[14:15, HALF:]

    top_out.wait_send()
    gp_out.wait_send()
    for j in (0, 1):
        for n in (0, 1):
            here, keep, send = outputs(j, n)
            pl.when(here)(keep.wait)
            pl.when(jnp.logical_not(here))(send.wait_send)

    for s in (0, 1):
        for n, dst in enumerate((out_a, out_b)):
            here = (core == seq) & (z == 2 * s + core)

            @pl.when(jnp.logical_not(here))
            def _():
                remote(dst.at[s], dst.at[s], os.at[0], orr.at[s, n], sibling).wait_recv()


def tail(loads, gmixed, result, w, par, rear_sums):
    dma = pltpu.SemaphoreType.DMA
    return pl.pallas_call(
        tail_kernel,
        name="tail",
        out_shape=(
            jax.ShapeDtypeStruct((1, 48, 4 * D), F32),
            jax.ShapeDtypeStruct((1, 192, D), F32),
            jax.ShapeDtypeStruct((1, 48, 3 * D), F32),
            jax.ShapeDtypeStruct((1, 48, D), F32),
            jax.ShapeDtypeStruct((16, D), F32),
            jax.ShapeDtypeStruct((2, 256, D), BF),
            jax.ShapeDtypeStruct((2, 256, D), BF),
        ),
        in_specs=[ANY] * 15 + [VM] * 2,
        out_specs=(VM, VM, VM, VM, VM, ANY, ANY),
        scratch_shapes=[pltpu.VMEM(v.shape, v.dtype) for v in loads]
        + [
            pltpu.VMEM((2, T, HALF), BF),
            pltpu.VMEM((2, T, 3 * HALF), BF),
            wide(3, 16, 48),
            wide(4, 4, REAR_ROWS),
            wide(T),
            pltpu.VMEM((8, D), F32),
            pltpu.VMEM((L, 128), F32),
            pltpu.VMEM((L, 128), F32),
        ]
        + reducer_buffers(REAR_ROWS)
        + reducer_buffers(FRONT_ROWS)[1:]
        + reducer_sems(5)
        + reducer_sems(3)
        + [dma((12,)), dma((3,)), dma((6,)), dma((8,)), dma((8,))]
        + [dma((3, 4)), dma((3, 4)), dma((4,)), dma((2, 2)), dma((2,))],
        compiler_params=comm_params(5),
    )(*loads, gmixed, result, w, par, rear_sums)


FRONT_STAGES = ((0, 48), (48, 16), (64, 16))
FRONT_ROWS = 80


def place_kernel(*refs):
    small = refs[6]
    outs = refs[7:]
    for src, dst in zip(refs[:6], outs[:6]):
        dst[...] = src[...]
    dp = lax.axis_index("dp")

    def picked(rows, start, count):
        row = lax.broadcasted_iota(jnp.int32, (D, count), 0)
        lane = lax.broadcasted_iota(jnp.int32, (D, count), 1)
        chosen = jnp.where(row == lane + start, 1.0, 0.0)
        return jnp.dot(
            rows, chosen, preferred_element_type=F32, precision=lax.Precision.HIGHEST
        )

    strip = picked(small[0:8], dp * 48, 48)
    outs[6][0] = strip[:2]
    outs[7][0] = strip[2:]
    up = picked(small[8:16], (dp % 4) * 192, 192)
    mine = lax.broadcasted_iota(jnp.int32, up.shape, 0) == dp // 4
    outs[8][...] = jnp.sum(jnp.where(mine, up, 0.0), axis=0, keepdims=True)


def place(*operands):
    shapes = [(v.shape, v.dtype) for v in operands[:6]]
    shapes += [((1, 2, 48), F32), ((1, 6, 48), F32), ((1, 192), F32)]
    return pl.pallas_call(
        place_kernel,
        name="place",
        out_shape=tuple(jax.ShapeDtypeStruct(s, t) for s, t in shapes),
        in_specs=[VM] * 7,
        out_specs=(VM,) * 9,
        compiler_params=local_params(),
    )(*operands)


def body(inputs, cotangent, w_qkv, w_out, w_fc, w_proj, gains, biases, fc_bias):
    dp = lax.axis_index("dp")
    strip = jnp.concatenate([gains[0], biases[0]], 0)
    small = lax.dynamic_update_slice(jnp.zeros((16, D), BF), strip, (0, dp * 48))
    small = lax.dynamic_update_slice(small, fc_bias, (8 + dp // 4, (dp % 4) * 192))
    full, stream, par, mixed = head(w_qkv, w_out, w_fc, w_proj, small, inputs, cotangent)
    full = full.reshape(16, ROWS, D)

    x, packed, normed = rear_front(stream, mixed, full, par)
    mixed, *kept = attention(packed)
    result, gmixed, gmiddle, middle, normed2, pre, active = turn(x, mixed, stream, full, par)
    gp = attention_back(*kept, gmixed)
    e, gmixed, gmiddle, rear_sums, mlow, gpre = back_back(
        gp, gmiddle, x, stream, middle, pre, full, par
    )
    gf, gd, gq, go, small, section_out, in_grad = tail(
        [e, active, normed2, gpre, *kept, mixed, mlow, normed, gmiddle, x],
        gmixed, result, full, par, rear_sums,
    )
    return place(section_out[None], in_grad[None], gq, go, gf, gd, small)


def solution(mesh):
    in_specs = (
        P("dp", "seq", None),
        P("dp", "seq", None),
        P("section", "dp", None),
        P("section", "dp", None),
        P("section", "dp", None),
        P("section", "dp", None),
        P("section", None, "dp"),
        P("section", None, "dp"),
        P("section", "dp"),
    )
    out_specs = (
        P("section", "dp", "seq", None),
        P("section", "dp", "seq", None),
        P("section", "dp", None),
        P("section", "dp", None),
        P("section", "dp", None),
        P("section", "dp", None),
        P("section", None, "dp"),
        P("section", None, "dp"),
        P("section", "dp"),
    )
    return jax.shard_map(body, mesh=mesh, in_specs=in_specs, out_specs=out_specs, check_vma=False)
```
